512 devices in a mesh: ctx: 128 (over z, y, core), tp: 4 (over x).
Axes of the slice: x: 4, y: 8, z: 8, core: 2. Of those that a mesh axis runs over, the one named last changes fastest.
Arguments:
- query_base: bfloat16 [16384, 3584], P('ctx', 'tp'), may hold values from -6 to 6
- key_base: bfloat16 [16384, 3584], P('ctx', 'tp'), may hold values from -6 to 6
- value_base: bfloat16 [16384, 3584], P('ctx', 'tp'), may hold values from -6 to 6
- adapter_activation: bfloat16 [16384, 128], P('ctx'), may hold values from -6 to 6
- adapter_up_weight: bfloat16 [2, 128, 3584], P(None, None, 'tp'), may hold values from -0.5 to 0.5
- output_grad: bfloat16 [16384, 3584], P('ctx', 'tp'), may hold values from -6 to 6
- stretch_doc: int32 [256], replicated, may hold values from 3 to 255, as said below
- doc_first: int32 [256], replicated, may hold values from 0 to 255, as said below
- slot_stretch: int32 [256], replicated, may hold values from 0 to 255, as said below
Outputs:
- grad_query: bfloat16 [16384, 3584], P('ctx', 'tp')
- grad_key: bfloat16 [16384, 3584], P('ctx', 'tp')
- grad_value: bfloat16 [16384, 3584], P('ctx', 'tp')
- grad_input: bfloat16 [16384, 128], P('ctx')
- grad_adapter: float32 [2, 128, 3584], P(None, None, 'tp')
The draws below stay inside these ranges and needn't reach their ends.
Inputs may be any that keep to these rules, and one draw needn't show every extreme that they name: stretch_doc never falls along the slab; a document covers 1 to 4 consecutive stretches, the first document exactly 4, the last stretch a document of its own; a document's id is the slab index of its last stretch. doc_first[c] is the smallest stretch index with the document id of stretch c. `slot_stretch`: each stretch is held in exactly one slot; slot s lies on ctx index s // 2; the ctx indices of each aligned group of 2 hold exactly that group's 4 consecutive stretches.
All inputs are finite; a program needn't handle non-finite values.
Results may differ from the reference program's by a relative error of at most 0.012.
The reference program's roundings to bfloat16 on the way (of `query`, `value`, `probs_low` and `grad_scores`) count: a program that leaves them out, or rounds other values in their place, can miss the bound.
Values may be sent and summed in bfloat16 or wider, within the bound.
A program may use at most 64 MiB of HBM per device.

```python
import jax
import jax.numpy as jnp
from jax import lax

LOCAL_HEADS = 16
HEAD_WIDTH = 224
ADAPTER_RANK = 128
STRETCH_LEN = 64
STRETCHES_DEV = 2
GROUP_SIZE = 2
DOC_SPAN = 4
STRETCHES = 256
SLAB_TOKENS = 16384
N_CTX = 128


def documents(key):
    lengths = jax.random.randint(key, (STRETCHES,), 1, DOC_SPAN + 1).astype(jnp.int32)
    lengths = lengths.at[0].set(DOC_SPAN)
    ends = jnp.cumsum(lengths)
    places = jnp.arange(STRETCHES, dtype=jnp.int32)
    owner_doc = jnp.sum((ends[None, :] <= places[:, None]).astype(jnp.int32), axis=1)
    starts = ends - lengths
    first = jnp.sum(jnp.where(places[None, :] == owner_doc[:, None], starts[None, :], 0), axis=1)
    doc_end = jnp.sum(jnp.where(places[None, :] == owner_doc[:, None], ends[None, :], 0), axis=1)
    last_place = STRETCHES - 1
    doc_id = jnp.minimum(doc_end, last_place) - 1
    doc_id = jnp.where(places == last_place, last_place, doc_id)
    first = jnp.where(places == last_place, last_place, first)
    return (doc_id.astype(jnp.int32), first.astype(jnp.int32))


def draw_stretch_doc(key, part):
    return documents(key)[0]


def draw_doc_first(key, part):
    return documents(key)[1]


def draw_slot_stretch(key, part):
    owner_doc, first = documents(key)
    group_stretches = STRETCHES_DEV * GROUP_SIZE
    places = jnp.arange(STRETCHES, dtype=jnp.int32)
    workload = places - first + 1
    priority = (workload * group_stretches + places % group_stretches).reshape(STRETCHES // group_stretches, group_stretches)
    offsets = (jnp.arange(STRETCHES // group_stretches, dtype=jnp.int32) * group_stretches)[:, None]
    ranked = jnp.argsort(priority, axis=1).astype(jnp.int32) + offsets
    lighter = ranked[:, :GROUP_SIZE]
    heavier = ranked[:, ::-1][:, :GROUP_SIZE]
    return jnp.stack([lighter, heavier], axis=2).reshape(STRETCHES).astype(jnp.int32)


def draw_query_base(key, part):
    key = jax.random.fold_in(key, 11)
    values = jnp.clip(jax.random.normal(key, (SLAB_TOKENS, LOCAL_HEADS * HEAD_WIDTH), jnp.float32), -6.0, 6.0)
    return values.astype(jnp.bfloat16)


def draw_key_base(key, part):
    key = jax.random.fold_in(key, 12)
    values = jnp.clip(jax.random.normal(key, (SLAB_TOKENS, LOCAL_HEADS * HEAD_WIDTH), jnp.float32), -6.0, 6.0)
    return values.astype(jnp.bfloat16)


def block_scale(stream_key, extent, pieces, least, largest):
    def one(dim, parts):
        steps = jax.random.uniform(jax.random.fold_in(jax.random.fold_in(stream_key, 6), dim), (parts,), jnp.float32, least / len(pieces), largest / len(pieces))
        return jnp.repeat(jnp.exp(steps), extent[dim] // parts).reshape((-1,) + (1,) * (len(extent) - dim - 1))

    level = one(*pieces[0])
    for cut in pieces[1:]:
        level = level * one(*cut)
    return level


def gaussian(stream_key, shape, deviation, bound, pieces=(), kind=jnp.bfloat16):
    result = deviation * jax.random.normal(stream_key, shape, jnp.float32)
    if pieces:
        result = result * block_scale(stream_key, shape, pieces, -0.22, 0.18)
    return jnp.clip(result, -bound, bound).astype(kind)


def setup_inputs(seed: int = 0) -> dict:
    streams_of = jax.random.split(jax.random.key(seed), 10)
    query_base = draw_query_base(jax.random.fold_in(streams_of[9], 71), 0)
    key_base = draw_key_base(jax.random.fold_in(streams_of[9], 71), 0)
    value_base = gaussian(streams_of[2], (SLAB_TOKENS, LOCAL_HEADS * HEAD_WIDTH), 1.0, 6.0, ((0, 128), (1, 4)))
    adapter_activation = gaussian(streams_of[3], (SLAB_TOKENS, ADAPTER_RANK), 1.0, 6.0, ((0, 128),))
    adapter_up_weight = gaussian(streams_of[4], (2, ADAPTER_RANK, LOCAL_HEADS * HEAD_WIDTH), ADAPTER_RANK ** -0.5, 0.5, ((2, 4),))
    output_grad = gaussian(streams_of[5], (SLAB_TOKENS, LOCAL_HEADS * HEAD_WIDTH), 1.0, 6.0, ((0, 128), (1, 4)))
    stretch_doc = draw_stretch_doc(jax.random.fold_in(streams_of[9], 71), 0)
    doc_first = draw_doc_first(jax.random.fold_in(streams_of[9], 71), 0)
    slot_stretch = draw_slot_stretch(jax.random.fold_in(streams_of[9], 71), 0)
    return {"query_base": query_base, "key_base": key_base, "value_base": value_base, "adapter_activation": adapter_activation, "adapter_up_weight": adapter_up_weight, "output_grad": output_grad, "stretch_doc": stretch_doc, "doc_first": doc_first, "slot_stretch": slot_stretch}


masked_fill = -1e30


def rounded(values):
    return lax.optimization_barrier(values.astype(jnp.bfloat16)).astype(jnp.float32)


def reference(query_base, key_base, value_base, adapter_activation, adapter_up_weight, output_grad, stretch_doc, doc_first, slot_stretch):
    columns = LOCAL_HEADS * HEAD_WIDTH
    block_rows = STRETCHES_DEV * STRETCH_LEN
    window = 2 * DOC_SPAN
    score_scale = HEAD_WIDTH ** -0.5
    query = (query_base.astype(jnp.float32) + jnp.dot(adapter_activation, adapter_up_weight[0], preferred_element_type=jnp.float32)).astype(jnp.bfloat16)
    value = (value_base.astype(jnp.float32) + jnp.dot(adapter_activation, adapter_up_weight[1], preferred_element_type=jnp.float32)).astype(jnp.bfloat16)
    slab_keys = jnp.zeros((STRETCHES, STRETCH_LEN, columns), jnp.bfloat16).at[slot_stretch].set(key_base.reshape(STRETCHES, STRETCH_LEN, columns))
    slab_values = jnp.zeros((STRETCHES, STRETCH_LEN, columns), jnp.bfloat16).at[slot_stretch].set(value.reshape(STRETCHES, STRETCH_LEN, columns))
    front = jnp.zeros((DOC_SPAN, STRETCH_LEN, columns), jnp.bfloat16)
    padded_keys = jnp.concatenate([front, slab_keys], axis=0)
    padded_values = jnp.concatenate([front, slab_values], axis=0)
    padded_doc = jnp.concatenate([jnp.full((DOC_SPAN,), -1, jnp.int32), stretch_doc.astype(jnp.int32)])
    inside = jnp.arange(STRETCH_LEN, dtype=jnp.int32)
    lower = inside[:, None] >= inside[None, :]

    def per_device(carry, device_at):
        key_grads, value_grads = carry
        own = lax.dynamic_slice_in_dim(slot_stretch, device_at * STRETCHES_DEV, STRETCHES_DEV).astype(jnp.int32)
        start = (device_at // GROUP_SIZE) * DOC_SPAN
        window_stretches = start - DOC_SPAN + jnp.arange(window, dtype=jnp.int32)
        window_doc = lax.dynamic_slice_in_dim(padded_doc, start, window)
        own_doc = stretch_doc[own]
        own_first = doc_first[own]
        earlier = (window_stretches[None, :] < own[:, None]) & (window_stretches[None, :] >= own_first[:, None]) & (window_doc[None, :] == own_doc[:, None])
        same = window_stretches[None, :] == own[:, None]
        visible = (earlier[:, None, :, None] | (same[:, None, :, None] & lower[None, :, None, :])).reshape(block_rows, window * STRETCH_LEN)
        key_block = lax.dynamic_slice_in_dim(padded_keys, start, window).reshape(window * STRETCH_LEN, LOCAL_HEADS, HEAD_WIDTH).astype(jnp.float32)
        value_block = lax.dynamic_slice_in_dim(padded_values, start, window).reshape(window * STRETCH_LEN, LOCAL_HEADS, HEAD_WIDTH).astype(jnp.float32)
        query_block = lax.dynamic_slice_in_dim(query, device_at * block_rows, block_rows).reshape(block_rows, LOCAL_HEADS, HEAD_WIDTH).astype(jnp.float32)
        grad_block = lax.dynamic_slice_in_dim(output_grad, device_at * block_rows, block_rows).reshape(block_rows, LOCAL_HEADS, HEAD_WIDTH).astype(jnp.float32)
        scores = jnp.einsum("qhe,khe->hqk", query_block, key_block) * score_scale
        scores = jnp.where(visible[None], scores, masked_fill)
        peak = jnp.max(scores, axis=2, keepdims=True)
        expo = jnp.where(visible[None], jnp.exp(scores - peak), 0.0)
        probs = expo / jnp.sum(expo, axis=2, keepdims=True)
        probs_low = rounded(probs)
        attended = jnp.einsum("hqk,khe->qhe", probs_low, value_block)
        row_dot = jnp.sum(grad_block * attended, axis=2).T
        grad_probs = jnp.einsum("qhe,khe->hqk", grad_block, value_block)
        grad_scores = rounded(probs * (grad_probs - row_dot[..., None]))
        query_gradient = score_scale * jnp.einsum("hqk,khe->qhe", grad_scores, key_block)
        key_terms = score_scale * jnp.einsum("hqk,qhe->khe", grad_scores, query_block)
        value_terms = jnp.einsum("hqk,qhe->khe", probs_low, grad_block)
        mine = jnp.any(window_stretches[:, None] == own[None, :], axis=1)
        mine_rows = jnp.repeat(mine, STRETCH_LEN)[:, None, None]
        key_terms = jnp.where(mine_rows, key_terms, rounded(key_terms)).reshape(window, STRETCH_LEN, columns)
        value_terms = jnp.where(mine_rows, value_terms, rounded(value_terms)).reshape(window, STRETCH_LEN, columns)
        key_grads = lax.dynamic_update_slice_in_dim(key_grads, lax.dynamic_slice_in_dim(key_grads, start, window) + key_terms, start, 0)
        value_grads = lax.dynamic_update_slice_in_dim(value_grads, lax.dynamic_slice_in_dim(value_grads, start, window) + value_terms, start, 0)
        return (key_grads, value_grads), query_gradient.reshape(block_rows, columns)

    grads_init = jnp.zeros((STRETCHES + DOC_SPAN, STRETCH_LEN, columns), jnp.float32)
    (key_grads, value_grads), query_gradient_rows = lax.scan(per_device, (grads_init, grads_init), jnp.arange(N_CTX, dtype=jnp.int32))
    grad_query = query_gradient_rows.reshape(SLAB_TOKENS, columns).astype(jnp.bfloat16)
    grad_key = key_grads[DOC_SPAN:][slot_stretch].reshape(SLAB_TOKENS, columns).astype(jnp.bfloat16)
    grad_value = value_grads[DOC_SPAN:][slot_stretch].reshape(SLAB_TOKENS, columns).astype(jnp.bfloat16)
    grad_input = (jnp.dot(grad_query, adapter_up_weight[0].T, preferred_element_type=jnp.float32) + jnp.dot(grad_value, adapter_up_weight[1].T, preferred_element_type=jnp.float32)).astype(jnp.bfloat16)
    grad_adapter = jnp.stack([jnp.dot(adapter_activation.T, grad_query, preferred_element_type=jnp.float32), jnp.dot(adapter_activation.T, grad_value, preferred_element_type=jnp.float32)])
    return grad_query, grad_key, grad_value, grad_input, grad_adapter
```

```python
import functools
import math

import jax
import jax.numpy as jnp
from jax import lax
from jax.experimental import pallas as pl
from jax.experimental.pallas import tpu as pltpu
from jax.sharding import PartitionSpec as P

HEAD = 224
PAD = 256
HEADS = 4
PAIR = 2 * PAD
ROWS = 128
STRETCH = 64
GROUP_ROWS = 2 * ROWS
WINDOW = 2 * GROUP_ROWS
SENT = 3 * STRETCH
RANK = 128
COLUMNS = HEADS * HEAD
SCALE = HEAD ** -0.5
FILL = -1e30

KEY, VALUE, QUERY, GRAD = range(4)
S_KEY, S_VALUE, S_QUERY, S_GRAD, S_ACT = range(5)
S_OUT = 5
S_INPUT = 8
S_ADAPTER = 9
S_NEXT = 11
S_BACK = 13
S_ALONG = 15
MESH = pl.DeviceIdType.MESH
F32 = jnp.float32
BF16 = jnp.bfloat16


def dot(a, b, contract):
    return lax.dot_general(a, b, ((contract[:1], contract[1:]), ((), ())), preferred_element_type=F32)


def padded(values):
    rows = values.shape[0]
    blank = jnp.zeros((rows, PAD - HEAD), values.dtype)
    parts = []
    for head in range(HEADS):
        parts += [values[:, head * HEAD:(head + 1) * HEAD], blank]
    return jnp.concatenate(parts, axis=1)


def unpadded(pairs):
    return jnp.concatenate(
        [pair[:, head * PAD:head * PAD + HEAD] for pair in pairs for head in range(2)], axis=1
    )


def kernel(
    side, n_tp,
    slot_ref, first_ref, q_hbm, k_hbm, v_hbm, a_hbm, w_hbm, g_hbm,
    out_ref, gi_ref, ga_ref,
    raw, act, weight, weight_pad, packed, sibling, act_sib, act_sorted,
    window_kv, sorted_qg, probs, probs_low, back_send, back_recv, own_kv,
    grads, sib_send, outs, gi_send, gi_sib, gi_along,
    part, scattered, crossed, gathered,
    load_sem, send_sem, recv_sem,
):
    me = lax.axis_index("ctx")
    tp = lax.axis_index("tp")
    core = lax.rem(me, 2)
    chip = lax.div(me, 2)
    y, z = lax.rem(chip, side), lax.div(chip, side)
    chips = side * side
    other = me + 1 - 2 * core
    after = lax.rem(chip + 1, chips) * 2 + core
    before = lax.rem(chip + chips - 1, chips) * 2 + core
    rows = RANK // side

    def along(axis, step):
        if axis == 0:
            return (z * side + lax.rem(y + step, side)) * 2 + core
        return (lax.rem(z + step, side) * side + y) * 2 + core

    def remote(src, dst, sem, ctx, x=None):
        return pltpu.make_async_remote_copy(
            src_ref=src, dst_ref=dst, send_sem=send_sem.at[sem], recv_sem=recv_sem.at[sem],
            device_id=(ctx, tp if x is None else x), device_id_type=MESH,
        )

    loads = [
        pltpu.make_async_copy(src, dst, load_sem.at[i])
        for i, (src, dst) in enumerate([
            (k_hbm, raw.at[KEY]), (a_hbm, act), (w_hbm, weight), (v_hbm, raw.at[VALUE]),
            (q_hbm, raw.at[QUERY]), (g_hbm, raw.at[GRAD]),
        ])
    ]
    for load in loads:
        load.start()

    barrier = pltpu.get_barrier_semaphore()

    def greet(ctx, x):
        pl.semaphore_signal(barrier, inc=1, device_id=(ctx, x), device_id_type=MESH)

    for device in (other, after, before):
        greet(device, tp)

    def greet_side(step, carry):
        greet(along(0, step), tp)
        greet(along(1, step), tp)
        return carry

    lax.fori_loop(1, side, greet_side, 0)

    def greet_tp(step, carry):
        greet(me, lax.rem(tp + step, n_tp))
        return carry

    lax.fori_loop(1, n_tp, greet_tp, 0)

    places = [
        slot_ref[2 * me] - 4 * chip, slot_ref[2 * me + 1] - 4 * chip,
        slot_ref[2 * other] - 4 * chip, slot_ref[2 * other + 1] - 4 * chip,
    ]

    def in_order(own, sib):
        slots = [own[:STRETCH], own[STRETCH:], sib[:STRETCH], sib[STRETCH:]]
        result = []
        for i in range(4):
            picked = slots[3]
            for j in (2, 1, 0):
                picked = jnp.where(places[j] == i, slots[j], picked)
            result.append(picked)
        return result

    def to_slots(values):
        result = []
        for j in range(4):
            picked = values[3 * STRETCH:]
            for i in (2, 1, 0):
                picked = jnp.where(places[j] == i, values[i * STRETCH:(i + 1) * STRETCH], picked)
            result.append(picked)
        return result

    def pack(kind, values):
        packed[kind, 0] = values[:, :PAIR]
        packed[kind, 1] = values[:, PAIR:]

    def to_sibling(kind, sem):
        return remote(packed.at[kind, 1 - core], sibling.at[kind], sem, other)

    loads[0].wait()
    pack(KEY, padded(raw[KEY]))
    pl.semaphore_wait(barrier, 3 + 2 * (side - 1) + n_tp - 1)
    sib_key = to_sibling(KEY, S_KEY)
    sib_key.start()
    loads[1].wait()
    sib_act = remote(act, act_sib, S_ACT, other)
    sib_act.start()
    loads[2].wait()
    for i in range(2):
        wide = padded(weight[i])
        weight_pad[i, 0] = wide[:, :PAIR]
        weight_pad[i, 1] = wide[:, PAIR:]

    def adapt(kind, i):
        wide = padded(raw[kind])
        for pair in range(2):
            update = dot(act[...], weight_pad[i, pair], (1, 0))
            base = wide[:, pair * PAIR:(pair + 1) * PAIR].astype(F32)
            packed[kind, pair] = (base + update).astype(BF16)

    loads[3].wait()
    adapt(VALUE, 1)
    sib_value = to_sibling(VALUE, S_VALUE)
    sib_value.start()

    def spread(kind):
        window_kv[kind, :STRETCH] = jnp.zeros((STRETCH, PAIR), BF16)
        for i, values in enumerate(in_order(packed[kind, core], sibling[kind])):
            window_kv[kind, GROUP_ROWS + i * STRETCH:GROUP_ROWS + (i + 1) * STRETCH] = values

    def to_next(kind):
        return remote(
            window_kv.at[kind, pl.ds(GROUP_ROWS + STRETCH, SENT)],
            window_kv.at[kind, pl.ds(STRETCH, SENT)], S_NEXT + kind, after,
        )

    sib_key.wait_recv()
    spread(KEY)
    next_key = to_next(KEY)
    next_key.start()
    sib_value.wait_recv()
    spread(VALUE)
    next_value = to_next(VALUE)
    next_value.start()

    loads[4].wait()
    adapt(QUERY, 0)
    sib_query = to_sibling(QUERY, S_QUERY)
    sib_query.start()
    loads[5].wait()
    pack(GRAD, padded(raw[GRAD]))
    sib_grad = to_sibling(GRAD, S_GRAD)
    sib_grad.start()

    sib_act.wait_recv()
    for i, values in enumerate(in_order(act[...], act_sib[...])):
        act_sorted[i * STRETCH:(i + 1) * STRETCH] = values
    for kind, copy in ((QUERY, sib_query), (GRAD, sib_grad)):
        copy.wait_recv()
        for i, values in enumerate(in_order(packed[kind, core], sibling[kind])):
            sorted_qg[kind - QUERY, i * STRETCH:(i + 1) * STRETCH] = values

    key_place = lax.broadcasted_iota(jnp.int32, (WINDOW, GROUP_ROWS), 0)
    query_place = lax.broadcasted_iota(jnp.int32, (1, GROUP_ROWS), 1)
    lowest = jnp.zeros((1, GROUP_ROWS), jnp.int32)
    for i in range(4):
        start = STRETCH * (first_ref[4 * chip + i] - 4 * chip + 4)
        lowest = jnp.where(query_place >= i * STRETCH, start, lowest)
    visible = (key_place >= lowest) & (key_place <= query_place + GROUP_ROWS)

    next_key.wait_recv()
    for head in range(2):
        lanes = slice(head * PAD, (head + 1) * PAD)
        scores = dot(window_kv[KEY, :, lanes], sorted_qg[0, :, lanes], (1, 1)) * SCALE
        scores = jnp.where(visible, scores, FILL)
        peak = jnp.max(scores, axis=0, keepdims=True)
        weights = jnp.exp(scores - peak)
        share = weights / jnp.sum(weights, axis=0, keepdims=True)
        probs[head] = share
        low = share.astype(BF16)
        probs_low[head] = low
        terms = dot(low, sorted_qg[1, :, lanes], (1, 0))
        back_send[VALUE, :, lanes] = terms[STRETCH:GROUP_ROWS].astype(BF16)
        own_kv[VALUE, :, lanes] = terms[GROUP_ROWS:]
    back_value = remote(back_send.at[VALUE], back_recv.at[VALUE], S_BACK + VALUE, before)
    back_value.start()

    next_value.wait_recv()
    for head in range(2):
        lanes = slice(head * PAD, (head + 1) * PAD)
        grad_probs = dot(window_kv[VALUE, :, lanes], sorted_qg[1, :, lanes], (1, 1))
        row_dot = jnp.sum(probs_low[head].astype(F32) * grad_probs, axis=0, keepdims=True)
        grad_scores = (probs[head] * (grad_probs - row_dot)).astype(BF16)
        terms = dot(grad_scores, sorted_qg[0, :, lanes], (1, 0)) * SCALE
        back_send[KEY, :, lanes] = terms[STRETCH:GROUP_ROWS].astype(BF16)
        own_kv[KEY, :, lanes] = terms[GROUP_ROWS:]
        summed = dot(grad_scores, window_kv[KEY, :, lanes], (0, 0)) * SCALE
        grads[0, :, lanes] = summed.astype(BF16)
    back_key = remote(back_send.at[KEY], back_recv.at[KEY], S_BACK + KEY, before)
    back_key.start()

    def along_sem(t, stage, step):
        return S_ALONG + (t * 3 + stage) * side + step

    position = [(y, z), (z, y)]

    def scatter(t, step):
        target = lax.rem(position[t][0] + step, side)
        return remote(part.at[t, target], scattered.at[t, step], along_sem(t, 0, step), along(t, step))

    def cross(t, step):
        mine = position[t][1]
        return remote(crossed.at[t, mine], crossed.at[t, mine], along_sem(t, 1, step), along(1 - t, step))

    def gather(t, step):
        mine = position[t][0]
        return remote(
            gathered.at[t, core, mine], gathered.at[t, core, mine], along_sem(t, 2, step), along(t, step)
        )

    def each(make, t, method):
        def run(step, carry):
            getattr(make(t, step), method)()
            return carry

        lax.fori_loop(1, side, run, 0)

    def adapter_terms(t, values):
        terms = dot(act_sorted[...], values, (0, 0)).astype(BF16)
        for j in range(side):
            part[t, j] = terms[j * rows:(j + 1) * rows]
        each(scatter, t, "start")

    def input_terms(t, values):
        return dot(values, weight_pad[t, core], (1, 1))

    def hand_out(t, slots):
        outs[t, core, :STRETCH] = slots[0]
        outs[t, core, STRETCH:] = slots[1]
        sib_send[t, :STRETCH] = slots[2]
        sib_send[t, STRETCH:] = slots[3]
        copy = remote(sib_send.at[t], outs.at[t, core], S_OUT + t, other)
        copy.start()
        return copy

    adapter_terms(0, grads[0])
    input_part = input_terms(0, grads[0])
    out_query = hand_out(0, to_slots(grads[0]))

    def add_back(kind):
        mine = own_kv[kind]
        return jnp.concatenate(
            [mine[:STRETCH], mine[STRETCH:] + back_recv[kind].astype(F32)], axis=0
        ).astype(BF16)

    back_value.wait_recv()
    grads[1] = add_back(VALUE)
    adapter_terms(1, grads[1])
    input_slots = to_slots(input_part + input_terms(1, grads[1]))
    gi_send[:STRETCH] = input_slots[2]
    gi_send[STRETCH:] = input_slots[3]
    sib_input = remote(gi_send, gi_sib, S_INPUT, other)
    sib_input.start()
    out_value = hand_out(2, to_slots(grads[1]))

    for t in range(2):
        each(scatter, t, "wait_recv")
        total = part[t, position[t][0]].astype(F32)
        for step in range(1, side):
            total = total + scattered[t, step].astype(F32)
        crossed[t, position[t][1]] = total.astype(BF16)
        each(cross, t, "start")

    sib_input.wait_recv()
    gi_along[tp, :STRETCH] = input_slots[0] + gi_sib[:STRETCH]
    gi_along[tp, STRETCH:] = input_slots[1] + gi_sib[STRETCH:]

    def tp_copy(step):
        return remote(
            gi_along.at[tp], gi_along.at[tp], S_ALONG + 6 * side + step, me, lax.rem(tp + step, n_tp)
        )

    def each_tp(method):
        def run(step, carry):
            getattr(tp_copy(step), method)()
            return carry

        lax.fori_loop(1, n_tp, run, 0)

    each_tp("start")

    for t in range(2):
        each(cross, t, "wait_recv")
        total = crossed[t, 0].astype(F32)
        for step in range(1, side):
            total = total + crossed[t, step].astype(F32)
        gathered[t, core, position[t][0]] = total.astype(BF16)
        each(gather, t, "start")

    back_key.wait_recv()
    out_key = hand_out(1, to_slots(add_back(KEY)))

    each_tp("wait_recv")
    total = gi_along[0]
    for x in range(1, n_tp):
        total = total + gi_along[x]
    gi_ref[...] = total.astype(BF16)

    sib_adapter = []
    for t in range(2):
        each(gather, t, "wait_recv")
        copy = remote(gathered.at[t, core], gathered.at[t, core], S_ADAPTER + t, other)
        copy.start()
        sib_adapter.append(copy)

    for copy in (out_query, out_value, out_key):
        copy.wait_recv()
    out_ref[...] = outs[...]
    for copy in sib_adapter:
        copy.wait_recv()
    ga_ref[...] = gathered[...]

    for copy in (
        sib_key, sib_act, sib_value, next_key, next_value, sib_query, sib_grad, back_value, back_key,
        out_query, out_value, out_key, sib_input, *sib_adapter,
    ):
        copy.wait_send()
    for t in range(2):
        each(scatter, t, "wait_send")
        each(cross, t, "wait_send")
        each(gather, t, "wait_send")
    each_tp("wait_send")


def finish(out_ref, ga_ref, q_ref, k_ref, v_ref, adapter_ref):
    for i, ref in enumerate((q_ref, k_ref, v_ref)):
        ref[...] = unpadded([out_ref[i, 0], out_ref[i, 1]])
    for i in range(2):
        adapter_ref[i] = unpadded([ga_ref[i, 0].astype(F32), ga_ref[i, 1].astype(F32)])


def body(
    query_base, key_base, value_base, adapter_activation, adapter_up_weight, output_grad,
    stretch_doc, doc_first, slot_stretch,
):
    n_tp = lax.axis_size("tp")
    side = math.isqrt(lax.axis_size("ctx") // 2)
    rows = RANK // side
    copies = S_ALONG + 6 * side + n_tp
    anywhere = pl.BlockSpec(memory_space=pl.ANY)
    vmem = pl.BlockSpec(memory_space=pltpu.VMEM)
    smem = pl.BlockSpec(memory_space=pltpu.SMEM)

    def block(*shape, dtype=BF16):
        return pltpu.VMEM(shape, dtype)

    outs, grad_input, adapter = pl.pallas_call(
        functools.partial(kernel, side, n_tp),
        out_shape=(
            jax.ShapeDtypeStruct((3, 2, ROWS, PAIR), BF16),
            jax.ShapeDtypeStruct((ROWS, RANK), BF16),
            jax.ShapeDtypeStruct((2, 2, side, rows, PAIR), BF16),
        ),
        in_specs=[smem, smem] + [anywhere] * 6,
        out_specs=(vmem, vmem, vmem),
        scratch_shapes=[
            block(4, ROWS, COLUMNS),
            block(ROWS, RANK),
            block(2, RANK, COLUMNS),
            block(2, 2, RANK, PAIR),
            block(4, 2, ROWS, PAIR),
            block(4, ROWS, PAIR),
            block(ROWS, RANK),
            block(GROUP_ROWS, RANK),
            block(2, WINDOW, PAIR),
            block(2, GROUP_ROWS, PAIR),
            block(2, WINDOW, GROUP_ROWS, dtype=F32),
            block(2, WINDOW, GROUP_ROWS),
            block(2, SENT, PAIR),
            block(2, SENT, PAIR),
            block(2, GROUP_ROWS, PAIR, dtype=F32),
            block(2, GROUP_ROWS, PAIR),
            block(3, ROWS, PAIR),
            block(3, 2, ROWS, PAIR),
            block(ROWS, RANK, dtype=F32),
            block(ROWS, RANK, dtype=F32),
            block(n_tp, ROWS, RANK, dtype=F32),
            block(2, side, rows, PAIR),
            block(2, side, rows, PAIR),
            block(2, side, rows, PAIR),
            block(2, 2, side, rows, PAIR),
            pltpu.SemaphoreType.DMA((6,)),
            pltpu.SemaphoreType.DMA((copies,)),
            pltpu.SemaphoreType.DMA((copies,)),
        ],
        compiler_params=pltpu.CompilerParams(
            collective_id=0, has_side_effects=True, vmem_limit_bytes=48 * 2**20
        ),
    )(
        slot_stretch, doc_first, query_base, key_base, value_base, adapter_activation,
        adapter_up_weight, output_grad,
    )
    grad_query, grad_key, grad_value, grad_adapter = pl.pallas_call(
        finish,
        out_shape=(
            jax.ShapeDtypeStruct((ROWS, COLUMNS), BF16),
            jax.ShapeDtypeStruct((ROWS, COLUMNS), BF16),
            jax.ShapeDtypeStruct((ROWS, COLUMNS), BF16),
            jax.ShapeDtypeStruct((2, RANK, COLUMNS), F32),
        ),
        in_specs=[vmem, vmem],
        out_specs=(vmem,) * 4,
        compiler_params=pltpu.CompilerParams(vmem_limit_bytes=48 * 2**20),
    )(outs, adapter.reshape(2, 2, RANK, PAIR))
    return grad_query, grad_key, grad_value, grad_input, grad_adapter


def solution(mesh):
    return jax.shard_map(
        body,
        mesh=mesh,
        in_specs=(
            P("ctx", "tp"),
            P("ctx", "tp"),
            P("ctx", "tp"),
            P("ctx", None),
            P(None, None, "tp"),
            P("ctx", "tp"),
            P(),
            P(),
            P(),
        ),
        out_specs=(
            P("ctx", "tp"),
            P("ctx", "tp"),
            P("ctx", "tp"),
            P("ctx", None),
            P(None, None, "tp"),
        ),
        check_vma=False,
    )
```

```python
import functools
import math

import jax
import jax.numpy as jnp
from jax import lax
from jax.experimental import pallas as pl
from jax.experimental.pallas import tpu as pltpu
from jax.sharding import PartitionSpec as P

HEAD = 224
PAD = 256
HEADS = 4
PAIR = 2 * PAD
ROWS = 128
STRETCH = 64
GROUP_ROWS = 2 * ROWS
WINDOW = 2 * GROUP_ROWS
SENT = 3 * STRETCH
RANK = 128
COLUMNS = HEADS * HEAD
SCALE = HEAD ** -0.5
FILL = -1e30

KEY, VALUE, QUERY, GRAD = range(4)
S_KEY, S_VALUE, S_QUERY, S_GRAD, S_ACT = range(5)
S_OUT = 5
S_INPUT = 8
S_ADAPTER = 9
S_NEXT = 11
S_BACK = 15
S_PAST = 19
S_ALONG = 21
MESH = pl.DeviceIdType.MESH
F32 = jnp.float32
BF16 = jnp.bfloat16


def dot(a, b, contract):
    return lax.dot_general(a, b, ((contract[:1], contract[1:]), ((), ())), preferred_element_type=F32)


def padded(values):
    rows = values.shape[0]
    blank = jnp.zeros((rows, PAD - HEAD), values.dtype)
    parts = []
    for head in range(HEADS):
        parts += [values[:, head * HEAD:(head + 1) * HEAD], blank]
    return jnp.concatenate(parts, axis=1)


def unpadded(pairs):
    return jnp.concatenate(
        [pair[:, head * PAD:head * PAD + HEAD] for pair in pairs for head in range(2)], axis=1
    )


def kernel(
    side, n_tp,
    slot_ref, first_ref, q_hbm, k_hbm, v_hbm, a_hbm, w_hbm, g_hbm,
    out_ref, gi_ref, ga_ref,
    raw, act, weight, weight_pad, packed, sibling, act_sib, act_past, act_window,
    window_kv, sorted_qg, probs, probs_low, back_send, back_recv, own_kv,
    grads, sib_send, outs, gi_send, gi_sib, gi_along,
    part, scattered, crossed, gathered,
    load_sem, send_sem, recv_sem,
):
    me = lax.axis_index("ctx")
    tp = lax.axis_index("tp")
    core = lax.rem(me, 2)
    chip = lax.div(me, 2)
    y, z = lax.rem(chip, side), lax.div(chip, side)
    chips = side * side
    other = me + 1 - 2 * core
    after = lax.rem(chip + 1, chips) * 2 + core
    before = lax.rem(chip + chips - 1, chips) * 2 + core
    rows = RANK // side

    def along(axis, step):
        if axis == 0:
            return (z * side + lax.rem(y + step, side)) * 2 + core
        return (lax.rem(z + step, side) * side + y) * 2 + core

    def remote(src, dst, sem, ctx, x=None):
        return pltpu.make_async_remote_copy(
            src_ref=src, dst_ref=dst, send_sem=send_sem.at[sem], recv_sem=recv_sem.at[sem],
            device_id=(ctx, tp if x is None else x), device_id_type=MESH,
        )

    loads = [
        pltpu.make_async_copy(src, dst, load_sem.at[i])
        for i, (src, dst) in enumerate([
            (k_hbm, raw.at[KEY]), (a_hbm, act), (w_hbm, weight), (v_hbm, raw.at[VALUE]),
            (q_hbm, raw.at[QUERY]), (g_hbm, raw.at[GRAD]),
        ])
    ]
    for load in loads:
        load.start()

    barrier = pltpu.get_barrier_semaphore()

    def greet(ctx, x):
        pl.semaphore_signal(barrier, inc=1, device_id=(ctx, x), device_id_type=MESH)

    after_other = after + 1 - 2 * core
    before_other = before + 1 - 2 * core
    for device in (other, after, after_other, before, before_other):
        greet(device, tp)

    def greet_side(step, carry):
        greet(along(0, step), tp)
        greet(along(1, step), tp)
        return carry

    lax.fori_loop(1, side, greet_side, 0)

    def greet_tp(step, carry):
        greet(me, lax.rem(tp + step, n_tp))
        return carry

    lax.fori_loop(1, n_tp, greet_tp, 0)

    places = [
        slot_ref[2 * me] - 4 * chip, slot_ref[2 * me + 1] - 4 * chip,
        slot_ref[2 * other] - 4 * chip, slot_ref[2 * other + 1] - 4 * chip,
    ]
    past = lax.rem(chip + chips - 1, chips)
    past_places = [slot_ref[4 * past + j] - 4 * past for j in range(4)]

    def in_order(own, sib, places=places):
        slots = [own[:STRETCH], own[STRETCH:], sib[:STRETCH], sib[STRETCH:]]
        result = []
        for i in range(4):
            picked = slots[3]
            for j in (2, 1, 0):
                picked = jnp.where(places[j] == i, slots[j], picked)
            result.append(picked)
        return result

    def to_slots(values):
        result = []
        for j in range(4):
            picked = values[3 * STRETCH:]
            for i in (2, 1, 0):
                picked = jnp.where(places[j] == i, values[i * STRETCH:(i + 1) * STRETCH], picked)
            result.append(picked)
        return result

    def pack(kind, values):
        packed[kind, 0] = values[:, :PAIR]
        packed[kind, 1] = values[:, PAIR:]

    def to_sibling(kind, sem):
        return remote(packed.at[kind, 1 - core], sibling.at[kind], sem, other)

    loads[0].wait()
    pack(KEY, padded(raw[KEY]))
    loads[1].wait()
    pl.semaphore_wait(barrier, 5 + 2 * (side - 1) + n_tp - 1)
    sib_key = to_sibling(KEY, S_KEY)
    sib_key.start()
    sib_act = remote(act, act_sib, S_ACT, other)
    sib_act.start()
    past_acts = [
        remote(act, act_past.at[core], S_PAST, after),
        remote(act, act_past.at[core], S_PAST + 1, after_other),
    ]
    for copy in past_acts:
        copy.start()
    loads[2].wait()
    for i in range(2):
        wide = padded(weight[i])
        weight_pad[i, 0] = wide[:, :PAIR]
        weight_pad[i, 1] = wide[:, PAIR:]

    def adapt(kind, i):
        wide = padded(raw[kind])
        for pair in range(2):
            update = dot(act[...], weight_pad[i, pair], (1, 0))
            base = wide[:, pair * PAIR:(pair + 1) * PAIR].astype(F32)
            packed[kind, pair] = (base + update).astype(BF16)

    loads[3].wait()
    adapt(VALUE, 1)
    sib_value = to_sibling(VALUE, S_VALUE)
    sib_value.start()

    def spread(kind):
        window_kv[kind, :STRETCH] = jnp.zeros((STRETCH, PAIR), BF16)
        for i, values in enumerate(in_order(packed[kind, core], sibling[kind])):
            window_kv[kind, GROUP_ROWS + i * STRETCH:GROUP_ROWS + (i + 1) * STRETCH] = values

    def to_next(kind, head):
        lanes = pl.ds(head * PAD, PAD)
        return remote(
            window_kv.at[kind, pl.ds(GROUP_ROWS + STRETCH, SENT), lanes],
            window_kv.at[kind, pl.ds(STRETCH, SENT), lanes], S_NEXT + 2 * head + kind, after,
        )

    next_kv = {}
    sib_key.wait_recv()
    spread(KEY)
    next_kv[KEY, 0] = to_next(KEY, 0)
    next_kv[KEY, 0].start()
    sib_value.wait_recv()
    spread(VALUE)
    for kind, head in ((VALUE, 0), (KEY, 1), (VALUE, 1)):
        next_kv[kind, head] = to_next(kind, head)
        next_kv[kind, head].start()

    loads[4].wait()
    adapt(QUERY, 0)
    sib_query = to_sibling(QUERY, S_QUERY)
    sib_query.start()
    loads[5].wait()
    pack(GRAD, padded(raw[GRAD]))
    sib_grad = to_sibling(GRAD, S_GRAD)
    sib_grad.start()

    sib_act.wait_recv()
    for i, values in enumerate(in_order(act[...], act_sib[...])):
        act_window[GROUP_ROWS + i * STRETCH:GROUP_ROWS + (i + 1) * STRETCH] = values
    for copy in past_acts:
        copy.wait_recv()
    act_window[:STRETCH] = jnp.zeros((STRETCH, RANK), BF16)
    for i, values in enumerate(in_order(act_past[0], act_past[1], past_places)):
        if i:
            act_window[i * STRETCH:(i + 1) * STRETCH] = values
    for kind, copy in ((QUERY, sib_query), (GRAD, sib_grad)):
        copy.wait_recv()
        for i, values in enumerate(in_order(packed[kind, core], sibling[kind])):
            sorted_qg[kind - QUERY, i * STRETCH:(i + 1) * STRETCH] = values

    key_place = lax.broadcasted_iota(jnp.int32, (WINDOW, GROUP_ROWS), 0)
    query_place = lax.broadcasted_iota(jnp.int32, (1, GROUP_ROWS), 1)
    lowest = jnp.zeros((1, GROUP_ROWS), jnp.int32)
    for i in range(4):
        start = STRETCH * (first_ref[4 * chip + i] - 4 * chip + 4)
        lowest = jnp.where(query_place >= i * STRETCH, start, lowest)
    visible = (key_place >= lowest) & (key_place <= query_place + GROUP_ROWS)

    def along_sem(unit, stage, step):
        return S_ALONG + (unit * 3 + stage) * side + step

    position = [(y, z), (z, y)]

    def scatter(unit, step):
        target = lax.rem(position[unit][0] + step, side)
        return remote(
            part.at[unit, target], scattered.at[unit, step], along_sem(unit, 0, step), along(unit, step)
        )

    def cross(unit, step):
        block = crossed.at[unit, position[unit][1]]
        return remote(block, block, along_sem(unit, 1, step), along(1 - unit, step))

    def gather(unit, step):
        block = gathered.at[unit, core, position[unit][0]]
        return remote(block, block, along_sem(unit, 2, step), along(unit, step))

    def each(make, unit, method):
        def run(step, carry):
            getattr(make(unit, step), method)()
            return carry

        lax.fori_loop(1, side, run, 0)

    def back(kind, head):
        lanes = pl.ds(head * PAD, PAD)
        return remote(
            back_send.at[kind, :, lanes], back_recv.at[kind, :, lanes],
            S_BACK + 2 * head + kind, before,
        )

    backs = {}
    for head in range(2):
        lanes = slice(head * PAD, (head + 1) * PAD)
        next_kv[KEY, head].wait_recv()
        scores = dot(window_kv[KEY, :, lanes], sorted_qg[0, :, lanes], (1, 1)) * SCALE
        scores = jnp.where(visible, scores, FILL)
        peak = jnp.max(scores, axis=0, keepdims=True)
        weights = jnp.exp(scores - peak)
        share = weights / jnp.sum(weights, axis=0, keepdims=True)
        probs[head] = share
        low = share.astype(BF16)
        probs_low[head] = low
        terms = dot(low, sorted_qg[1, :, lanes], (1, 0))
        own_kv[VALUE, :, lanes] = terms[GROUP_ROWS:]
        terms = terms.astype(BF16)
        back_send[VALUE, :, lanes] = terms[STRETCH:GROUP_ROWS]
        backs[VALUE, head] = back(VALUE, head)
        backs[VALUE, head].start()
        adapter = dot(act_window[...], terms, (0, 0)).astype(BF16)
        for j in range(side):
            part[head, j, 1] = adapter[j * rows:(j + 1) * rows]

        next_kv[VALUE, head].wait_recv()
        grad_probs = dot(window_kv[VALUE, :, lanes], sorted_qg[1, :, lanes], (1, 1))
        row_dot = jnp.sum(probs_low[head].astype(F32) * grad_probs, axis=0, keepdims=True)
        grad_scores = (probs[head] * (grad_probs - row_dot)).astype(BF16)
        summed = (dot(grad_scores, window_kv[KEY, :, lanes], (0, 0)) * SCALE).astype(BF16)
        grads[0, :, lanes] = summed
        adapter = dot(act_window[GROUP_ROWS:], summed, (0, 0)).astype(BF16)
        for j in range(side):
            part[head, j, 0] = adapter[j * rows:(j + 1) * rows]
        each(scatter, head, "start")
        terms = dot(grad_scores, sorted_qg[0, :, lanes], (1, 0)) * SCALE
        back_send[KEY, :, lanes] = terms[STRETCH:GROUP_ROWS].astype(BF16)
        own_kv[KEY, :, lanes] = terms[GROUP_ROWS:]
        backs[KEY, head] = back(KEY, head)
        backs[KEY, head].start()

    def input_terms(i, values):
        return dot(values, weight_pad[i, core], (1, 1))

    def hand_out(i, slots):
        outs[i, core, :STRETCH] = slots[0]
        outs[i, core, STRETCH:] = slots[1]
        sib_send[i, :STRETCH] = slots[2]
        sib_send[i, STRETCH:] = slots[3]
        copy = remote(sib_send.at[i], outs.at[i, core], S_OUT + i, other)
        copy.start()
        return copy

    def add_back(kind):
        mine = own_kv[kind]
        return jnp.concatenate(
            [mine[:STRETCH], mine[STRETCH:] + back_recv[kind].astype(F32)], axis=0
        ).astype(BF16)

    def go_across(unit):
        each(scatter, unit, "wait_recv")
        total = part[unit, position[unit][0]].astype(F32)
        for step in range(1, side):
            total = total + scattered[unit, step].astype(F32)
        crossed[unit, position[unit][1]] = total.astype(BF16)
        each(cross, unit, "start")

    def go_around(unit):
        each(cross, unit, "wait_recv")
        total = crossed[unit, 0].astype(F32)
        for step in range(1, side):
            total = total + crossed[unit, step].astype(F32)
        gathered[unit, core, position[unit][0]] = total.astype(BF16)
        each(gather, unit, "start")

    input_part = input_terms(0, grads[0])
    out_query = hand_out(0, to_slots(grads[0]))
    go_across(0)

    for head in range(2):
        backs[VALUE, head].wait_recv()
    grads[1] = add_back(VALUE)
    input_slots = to_slots(input_part + input_terms(1, grads[1]))
    gi_send[:STRETCH] = input_slots[2]
    gi_send[STRETCH:] = input_slots[3]
    sib_input = remote(gi_send, gi_sib, S_INPUT, other)
    sib_input.start()
    gi_along[tp, :STRETCH] = input_slots[0]
    gi_along[tp, STRETCH:] = input_slots[1]
    out_value = hand_out(2, to_slots(grads[1]))

    go_across(1)

    sib_input.wait_recv()
    gi_along[tp] = gi_along[tp] + gi_sib[...]

    def tp_copy(step):
        return remote(
            gi_along.at[tp], gi_along.at[tp], S_ALONG + 6 * side + step, me, lax.rem(tp + step, n_tp)
        )

    def each_tp(method):
        def run(step, carry):
            getattr(tp_copy(step), method)()
            return carry

        lax.fori_loop(1, n_tp, run, 0)

    each_tp("start")
    for head in range(2):
        backs[KEY, head].wait_recv()
    out_key = hand_out(1, to_slots(add_back(KEY)))

    go_around(0)
    each_tp("wait_recv")
    total = gi_along[0]
    for x in range(1, n_tp):
        total = total + gi_along[x]
    gi_ref[...] = total.astype(BF16)
    go_around(1)

    for copy in (out_query, out_value, out_key):
        copy.wait_recv()
    out_ref[...] = outs[...]

    sib_adapter = []
    for unit in range(2):
        each(gather, unit, "wait_recv")
        block = gathered.at[unit, core]
        copy = remote(block, block, S_ADAPTER + unit, other)
        copy.start()
        sib_adapter.append(copy)

    for copy in (
        sib_key, sib_act, sib_value, sib_query, sib_grad, *past_acts, *next_kv.values(),
        *backs.values(), out_query, out_value, out_key, sib_input,
    ):
        copy.wait_send()
    for unit in range(2):
        each(scatter, unit, "wait_send")
        each(cross, unit, "wait_send")
        each(gather, unit, "wait_send")
    each_tp("wait_send")
    for unit in range(2):
        sib_adapter[unit].wait_recv()
        ga_ref[unit] = gathered[unit]
        sib_adapter[unit].wait_send()


def finish(out_ref, gi_ref, ga_ref, q_ref, k_ref, v_ref, input_ref, adapter_ref):
    input_ref[...] = gi_ref[...]
    for i, ref in enumerate((q_ref, k_ref, v_ref)):
        ref[...] = unpadded([out_ref[i, 0], out_ref[i, 1]])
    for i in range(2):
        heads = [
            ga_ref[unit, pair, :, i].reshape(RANK, PAD)[:, :HEAD].astype(F32)
            for pair in range(2) for unit in range(2)
        ]
        adapter_ref[i] = jnp.concatenate(heads, axis=1)


def body(
    query_base, key_base, value_base, adapter_activation, adapter_up_weight, output_grad,
    stretch_doc, doc_first, slot_stretch,
):
    n_tp = lax.axis_size("tp")
    side = math.isqrt(lax.axis_size("ctx") // 2)
    rows = RANK // side
    copies = S_ALONG + 6 * side + n_tp
    anywhere = pl.BlockSpec(memory_space=pltpu.HBM)
    vmem = pl.BlockSpec(memory_space=pltpu.VMEM)
    smem = pl.BlockSpec(memory_space=pltpu.SMEM)

    def block(*shape, dtype=BF16):
        return pltpu.VMEM(shape, dtype)

    outs, grad_input, adapter = pl.pallas_call(
        functools.partial(kernel, side, n_tp),
        out_shape=(
            jax.ShapeDtypeStruct((3, 2, ROWS, PAIR), BF16),
            jax.ShapeDtypeStruct((ROWS, RANK), BF16),
            jax.ShapeDtypeStruct((2, 2, side, 2, rows, PAD), BF16),
        ),
        in_specs=[smem, smem] + [anywhere] * 6,
        out_specs=(vmem, vmem, vmem),
        scratch_shapes=[
            block(4, ROWS, COLUMNS),
            block(ROWS, RANK),
            block(2, RANK, COLUMNS),
            block(2, 2, RANK, PAIR),
            block(4, 2, ROWS, PAIR),
            block(4, ROWS, PAIR),
            block(ROWS, RANK),
            block(2, ROWS, RANK),
            block(WINDOW, RANK),
            block(2, WINDOW, PAIR),
            block(2, GROUP_ROWS, PAIR),
            block(2, WINDOW, GROUP_ROWS, dtype=F32),
            block(2, WINDOW, GROUP_ROWS),
            block(2, SENT, PAIR),
            block(2, SENT, PAIR),
            block(2, GROUP_ROWS, PAIR, dtype=F32),
            block(2, GROUP_ROWS, PAIR),
            block(3, ROWS, PAIR),
            block(3, 2, ROWS, PAIR),
            block(ROWS, RANK, dtype=F32),
            block(ROWS, RANK, dtype=F32),
            block(n_tp, ROWS, RANK, dtype=F32),
            block(2, side, 2, rows, PAD),
            block(2, side, 2, rows, PAD),
            block(2, side, 2, rows, PAD),
            block(2, 2, side, 2, rows, PAD),
            pltpu.SemaphoreType.DMA((6,)),
            pltpu.SemaphoreType.DMA((copies,)),
            pltpu.SemaphoreType.DMA((copies,)),
        ],
        compiler_params=pltpu.CompilerParams(
            collective_id=0, has_side_effects=True, vmem_limit_bytes=56 * 2**20
        ),
    )(
        slot_stretch, doc_first, query_base, key_base, value_base, adapter_activation,
        adapter_up_weight, output_grad,
    )
    return pl.pallas_call(
        finish,
        out_shape=(
            jax.ShapeDtypeStruct((ROWS, COLUMNS), BF16),
            jax.ShapeDtypeStruct((ROWS, COLUMNS), BF16),
            jax.ShapeDtypeStruct((ROWS, COLUMNS), BF16),
            jax.ShapeDtypeStruct((ROWS, RANK), BF16),
            jax.ShapeDtypeStruct((2, RANK, COLUMNS), F32),
        ),
        in_specs=[vmem] * 3,
        out_specs=(vmem,) * 5,
        compiler_params=pltpu.CompilerParams(vmem_limit_bytes=56 * 2**20),
    )(outs, grad_input, adapter)


def solution(mesh):
    return jax.shard_map(
        body,
        mesh=mesh,
        in_specs=(
            P("ctx", "tp"),
            P("ctx", "tp"),
            P("ctx", "tp"),
            P("ctx", None),
            P(None, None, "tp"),
            P("ctx", "tp"),
            P(),
            P(),
            P(),
        ),
        out_specs=(
            P("ctx", "tp"),
            P("ctx", "tp"),
            P("ctx", "tp"),
            P("ctx", None),
            P(None, None, "tp"),
        ),
        check_vma=False,
    )
```

```python
import functools
import math

import jax
import jax.numpy as jnp
from jax import lax
from jax.experimental import pallas as pl
from jax.experimental.pallas import tpu as pltpu
from jax.sharding import PartitionSpec as P

HEAD = 224
PAD = 256
HEADS = 4
PAIR = 2 * PAD
ROWS = 128
STRETCH = 64
GROUP_ROWS = 2 * ROWS
WINDOW = 2 * GROUP_ROWS
SENT = 3 * STRETCH
RANK = 128
COLUMNS = HEADS * HEAD
SCALE = HEAD ** -0.5
FILL = -1e30

KEY, VALUE, QUERY, GRAD = range(4)
S_KEY, S_VALUE, S_QUERY, S_GRAD, S_ACT = range(5)
S_OUT = 5
S_INPUT = 8
S_ADAPTER = 9
S_NEXT = 11
S_BACK = 15
S_PAST = 19
S_FIRST = 21
S_ALONG = 22
MESH = pl.DeviceIdType.MESH
F32 = jnp.float32
BF16 = jnp.bfloat16


def dot(a, b, contract):
    return lax.dot_general(a, b, ((contract[:1], contract[1:]), ((), ())), preferred_element_type=F32)


def padded(values):
    rows = values.shape[0]
    blank = jnp.zeros((rows, PAD - HEAD), values.dtype)
    parts = []
    for head in range(HEADS):
        parts += [values[:, head * HEAD:(head + 1) * HEAD], blank]
    return jnp.concatenate(parts, axis=1)


def unpadded(pairs):
    return jnp.concatenate(
        [pair[:, head * PAD:head * PAD + HEAD] for pair in pairs for head in range(2)], axis=1
    )


def kernel(
    side, n_tp,
    slot_ref, first_ref, q_hbm, k_hbm, v_hbm, a_hbm, w_hbm, g_hbm,
    out_hbm, gi_hbm, ga_hbm,
    raw, act, weight, weight_pad, packed, sibling, act_sib, act_past, act_window, key_past,
    window_kv, sorted_qg, probs, probs_low, back_send, back_recv, own_kv,
    grads, sib_send, outs, gi_send, gi_sib, gi_along,
    part, scattered, crossed, gathered, gi_out,
    load_sem, store_sem, send_sem, recv_sem,
):
    me = lax.axis_index("ctx")
    tp = lax.axis_index("tp")
    core = lax.rem(me, 2)
    chip = lax.div(me, 2)
    y, z = lax.rem(chip, side), lax.div(chip, side)
    chips = side * side
    other = me + 1 - 2 * core
    after = lax.rem(chip + 1, chips) * 2 + core
    before = lax.rem(chip + chips - 1, chips) * 2 + core
    rows = RANK // side

    def along(axis, step):
        if axis == 0:
            return (z * side + lax.rem(y + step, side)) * 2 + core
        return (lax.rem(z + step, side) * side + y) * 2 + core

    def remote(src, dst, sem, ctx, x=None):
        return pltpu.make_async_remote_copy(
            src_ref=src, dst_ref=dst, send_sem=send_sem.at[sem], recv_sem=recv_sem.at[sem],
            device_id=(ctx, tp if x is None else x), device_id_type=MESH,
        )

    loads = [
        pltpu.make_async_copy(src, dst, load_sem.at[i])
        for i, (src, dst) in enumerate([
            (k_hbm, raw.at[KEY]), (a_hbm, act), (w_hbm, weight), (v_hbm, raw.at[VALUE]),
            (q_hbm, raw.at[QUERY]), (g_hbm, raw.at[GRAD]),
        ])
    ]
    loads[0].start()

    barrier = pltpu.get_barrier_semaphore()

    def greet(ctx, x):
        pl.semaphore_signal(barrier, inc=1, device_id=(ctx, x), device_id_type=MESH)

    steps = [side // 2 + (i // 2) * (1 - 2 * (i % 2)) for i in range(1, side)]
    for step in steps:
        greet(along(0, step), tp)
        greet(along(1, step), tp)
    for step in range(1, n_tp):
        greet(me, lax.rem(tp + step, n_tp))
    after_other = after + 1 - 2 * core
    before_other = before + 1 - 2 * core
    for device in (after, after_other, before, before_other, other):
        greet(device, tp)
    for load in loads[1:]:
        load.start()

    places = [
        slot_ref[2 * me] - 4 * chip, slot_ref[2 * me + 1] - 4 * chip,
        slot_ref[2 * other] - 4 * chip, slot_ref[2 * other + 1] - 4 * chip,
    ]
    past = lax.rem(chip + chips - 1, chips)
    past_places = [slot_ref[4 * past + j] - 4 * past for j in range(4)]

    def in_order(own, sib, places=places):
        slots = [own[:STRETCH], own[STRETCH:], sib[:STRETCH], sib[STRETCH:]]
        result = []
        for i in range(4):
            picked = slots[3]
            for j in (2, 1, 0):
                picked = jnp.where(places[j] == i, slots[j], picked)
            result.append(picked)
        return result

    def to_slots(values):
        result = []
        for j in range(4):
            picked = values[3 * STRETCH:]
            for i in (2, 1, 0):
                picked = jnp.where(places[j] == i, values[i * STRETCH:(i + 1) * STRETCH], picked)
            result.append(picked)
        return result

    def pack(kind, values):
        packed[kind, 0] = values[:, :PAIR]
        packed[kind, 1] = values[:, PAIR:]

    def to_sibling(kind, sem):
        return remote(packed.at[kind, 1 - core], sibling.at[kind], sem, other)

    loads[0].wait()
    pack(KEY, padded(raw[KEY]))
    loads[1].wait()
    pl.semaphore_wait(barrier, 5 + 2 * (side - 1) + n_tp - 1)
    sib_key = to_sibling(KEY, S_KEY)
    sib_key.start()
    sib_act = remote(act, act_sib, S_ACT, other)
    sib_act.start()
    first = pl.ds(0, PAD)
    next_first = [
        remote(packed.at[KEY, core, :, first], key_past.at[core], S_NEXT, after),
        remote(packed.at[KEY, 1 - core, :, first], key_past.at[core], S_FIRST, after_other),
    ]
    for copy in next_first:
        copy.start()
    next_act = remote(act, act_past.at[core], S_PAST, after)
    next_act.start()
    loads[2].wait()
    for i in range(2):
        wide = padded(weight[i])
        weight_pad[i, 0] = wide[:, :PAIR]
        weight_pad[i, 1] = wide[:, PAIR:]

    def adapt(kind, i):
        wide = padded(raw[kind])
        for pair in range(2):
            update = dot(act[...], weight_pad[i, pair], (1, 0))
            base = wide[:, pair * PAIR:(pair + 1) * PAIR].astype(F32)
            packed[kind, pair] = (base + update).astype(BF16)

    loads[3].wait()
    adapt(VALUE, 1)
    sib_value = to_sibling(VALUE, S_VALUE)
    sib_value.start()

    def spread(kind):
        window_kv[kind, :STRETCH] = jnp.zeros((STRETCH, PAIR), BF16)
        for i, values in enumerate(in_order(packed[kind, core], sibling[kind])):
            window_kv[kind, GROUP_ROWS + i * STRETCH:GROUP_ROWS + (i + 1) * STRETCH] = values

    def to_next(kind, head):
        lanes = pl.ds(head * PAD, PAD)
        return remote(
            window_kv.at[kind, pl.ds(GROUP_ROWS + STRETCH, SENT), lanes],
            window_kv.at[kind, pl.ds(STRETCH, SENT), lanes], S_NEXT + 2 * head + kind, after,
        )

    next_kv = {}
    sib_key.wait_recv()
    spread(KEY)
    sib_value.wait_recv()
    spread(VALUE)
    for kind, head in ((VALUE, 0), (KEY, 1), (VALUE, 1)):
        next_kv[kind, head] = to_next(kind, head)
        next_kv[kind, head].start()

    loads[4].wait()
    adapt(QUERY, 0)
    sib_query = to_sibling(QUERY, S_QUERY)
    sib_query.start()
    loads[5].wait()
    pack(GRAD, padded(raw[GRAD]))
    sib_grad = to_sibling(GRAD, S_GRAD)
    sib_grad.start()

    sib_act.wait_recv()
    for i, values in enumerate(in_order(act[...], act_sib[...])):
        act_window[GROUP_ROWS + i * STRETCH:GROUP_ROWS + (i + 1) * STRETCH] = values
    for kind, copy in ((QUERY, sib_query), (GRAD, sib_grad)):
        copy.wait_recv()
        for i, values in enumerate(in_order(packed[kind, core], sibling[kind])):
            sorted_qg[kind - QUERY, i * STRETCH:(i + 1) * STRETCH] = values
    next_act.wait_recv()
    pass_act = remote(act_past.at[core], act_past.at[core], S_PAST + 1, other)
    pass_act.start()

    key_place = lax.broadcasted_iota(jnp.int32, (WINDOW, GROUP_ROWS), 0)
    query_place = lax.broadcasted_iota(jnp.int32, (1, GROUP_ROWS), 1)
    lowest = jnp.zeros((1, GROUP_ROWS), jnp.int32)
    for i in range(4):
        start = STRETCH * (first_ref[4 * chip + i] - 4 * chip + 4)
        lowest = jnp.where(query_place >= i * STRETCH, start, lowest)
    visible = (key_place >= lowest) & (key_place <= query_place + GROUP_ROWS)

    def along_sem(unit, stage, step):
        return S_ALONG + (unit * 3 + stage) * side + step

    position = [(y, z), (z, y)]

    def scatter(unit, step):
        target = lax.rem(position[unit][0] + step, side)
        return remote(
            part.at[unit, target], scattered.at[unit, step], along_sem(unit, 0, step), along(unit, step)
        )

    def cross(unit, step):
        block = crossed.at[unit, position[unit][1]]
        return remote(block, block, along_sem(unit, 1, step), along(1 - unit, step))

    def gather(unit, step):
        block = gathered.at[unit, core, position[unit][0]]
        return remote(block, block, along_sem(unit, 2, step), along(unit, step))

    def each(make, unit, method):
        if method == "start":
            for step in steps:
                make(unit, step).start()
            return

        def run(step, carry):
            getattr(make(unit, step), method)()
            return carry

        lax.fori_loop(1, side, run, 0)

    def back(kind, head):
        lanes = pl.ds(head * PAD, PAD)
        return remote(
            back_send.at[kind, :, lanes], back_recv.at[kind, :, lanes],
            S_BACK + 2 * head + kind, before,
        )

    backs = {}
    for head in range(2):
        lanes = slice(head * PAD, (head + 1) * PAD)
        if head:
            next_kv[KEY, head].wait_recv()
        else:
            for copy in next_first:
                copy.wait_recv()
            for i, values in enumerate(in_order(key_past[0], key_past[1], past_places)):
                if i:
                    window_kv[KEY, i * STRETCH:(i + 1) * STRETCH, lanes] = values
        scores = dot(window_kv[KEY, :, lanes], sorted_qg[0, :, lanes], (1, 1)) * SCALE
        scores = jnp.where(visible, scores, FILL)
        peak = jnp.max(scores, axis=0, keepdims=True)
        weights = jnp.exp(scores - peak)
        share = weights / jnp.sum(weights, axis=0, keepdims=True)
        probs[head] = share
        low = share.astype(BF16)
        probs_low[head] = low
        terms = dot(low, sorted_qg[1, :, lanes], (1, 0))
        own_kv[VALUE, :, lanes] = terms[GROUP_ROWS:]
        terms = terms.astype(BF16)
        back_send[VALUE, :, lanes] = terms[STRETCH:GROUP_ROWS]
        backs[VALUE, head] = back(VALUE, head)
        backs[VALUE, head].start()
        if not head:
            pass_act.wait_recv()
            act_window[:STRETCH] = jnp.zeros((STRETCH, RANK), BF16)
            for i, values in enumerate(in_order(act_past[0], act_past[1], past_places)):
                if i:
                    act_window[i * STRETCH:(i + 1) * STRETCH] = values
        adapter = dot(act_window[...], terms, (0, 0)).astype(BF16)
        for j in range(side):
            part[head, j, 1] = adapter[j * rows:(j + 1) * rows]

        next_kv[VALUE, head].wait_recv()
        grad_probs = dot(window_kv[VALUE, :, lanes], sorted_qg[1, :, lanes], (1, 1))
        row_dot = jnp.sum(probs_low[head].astype(F32) * grad_probs, axis=0, keepdims=True)
        grad_scores = (probs[head] * (grad_probs - row_dot)).astype(BF16)
        summed = (dot(grad_scores, window_kv[KEY, :, lanes], (0, 0)) * SCALE).astype(BF16)
        grads[0, :, lanes] = summed
        adapter = dot(act_window[GROUP_ROWS:], summed, (0, 0)).astype(BF16)
        for j in range(side):
            part[head, j, 0] = adapter[j * rows:(j + 1) * rows]
        each(scatter, head, "start")
        terms = dot(grad_scores, sorted_qg[0, :, lanes], (1, 0)) * SCALE
        back_send[KEY, :, lanes] = terms[STRETCH:GROUP_ROWS].astype(BF16)
        own_kv[KEY, :, lanes] = terms[GROUP_ROWS:]
        backs[KEY, head] = back(KEY, head)
        backs[KEY, head].start()

    def input_terms(i, values):
        return dot(values, weight_pad[i, core], (1, 1))

    def hand_out(i, slots):
        outs[i, core, :STRETCH] = slots[0]
        outs[i, core, STRETCH:] = slots[1]
        sib_send[i, :STRETCH] = slots[2]
        sib_send[i, STRETCH:] = slots[3]
        copy = remote(sib_send.at[i], outs.at[i, core], S_OUT + i, other)
        copy.start()
        return copy

    def add_back(kind):
        mine = own_kv[kind]
        return jnp.concatenate(
            [mine[:STRETCH], mine[STRETCH:] + back_recv[kind].astype(F32)], axis=0
        ).astype(BF16)

    def go_across(unit):
        each(scatter, unit, "wait_recv")
        total = part[unit, position[unit][0]].astype(F32)
        for step in range(1, side):
            total = total + scattered[unit, step].astype(F32)
        crossed[unit, position[unit][1]] = total.astype(BF16)
        each(cross, unit, "start")

    def go_around(unit):
        each(cross, unit, "wait_recv")
        total = crossed[unit, 0].astype(F32)
        for step in range(1, side):
            total = total + crossed[unit, step].astype(F32)
        gathered[unit, core, position[unit][0]] = total.astype(BF16)
        each(gather, unit, "start")

    input_part = input_terms(0, grads[0])
    out_query = hand_out(0, to_slots(grads[0]))
    go_across(0)

    for head in range(2):
        backs[VALUE, head].wait_recv()
    grads[1] = add_back(VALUE)
    input_slots = to_slots(input_part + input_terms(1, grads[1]))
    gi_send[:STRETCH] = input_slots[2]
    gi_send[STRETCH:] = input_slots[3]
    sib_input = remote(gi_send, gi_sib, S_INPUT, other)
    sib_input.start()
    gi_along[tp, :STRETCH] = input_slots[0]
    gi_along[tp, STRETCH:] = input_slots[1]
    out_value = hand_out(2, to_slots(grads[1]))

    go_across(1)

    sib_input.wait_recv()
    gi_along[tp] = gi_along[tp] + gi_sib[...]

    def tp_copy(step):
        return remote(
            gi_along.at[tp], gi_along.at[tp], S_ALONG + 6 * side + step, me, lax.rem(tp + step, n_tp)
        )

    def each_tp(method):
        def run(step, carry):
            getattr(tp_copy(step), method)()
            return carry

        lax.fori_loop(1, n_tp, run, 0)

    each_tp("start")
    for head in range(2):
        backs[KEY, head].wait_recv()
    out_key = hand_out(1, to_slots(add_back(KEY)))

    go_around(0)
    each_tp("wait_recv")
    total = gi_along[0]
    for x in range(1, n_tp):
        total = total + gi_along[x]
    gi_out[...] = total.astype(BF16)
    stores = [pltpu.make_async_copy(gi_out, gi_hbm, store_sem.at[0])]
    stores[0].start()
    go_around(1)

    for copy in (out_query, out_value, out_key):
        copy.wait_recv()
    stores.append(pltpu.make_async_copy(outs, out_hbm, store_sem.at[1]))
    stores[1].start()

    sib_adapter = []
    for unit in range(2):
        each(gather, unit, "wait_recv")
        block = gathered.at[unit, core]
        copy = remote(block, block, S_ADAPTER + unit, other)
        copy.start()
        sib_adapter.append(copy)

    for copy in (
        sib_key, sib_act, sib_value, sib_query, sib_grad, *next_first, next_act, pass_act, *next_kv.values(),
        *backs.values(), out_query, out_value, out_key, sib_input,
    ):
        copy.wait_send()
    for unit in range(2):
        each(scatter, unit, "wait_send")
        each(cross, unit, "wait_send")
        each(gather, unit, "wait_send")
    each_tp("wait_send")
    for unit in range(2):
        sib_adapter[unit].wait_recv()
        stores.append(pltpu.make_async_copy(gathered.at[unit], ga_hbm.at[unit], store_sem.at[2 + unit]))
        stores[2 + unit].start()
        sib_adapter[unit].wait_send()
    for store in stores:
        store.wait()


def finish(
    out_hbm, gi_hbm, ga_hbm, q_hbm, k_hbm, v_hbm, input_hbm, adapter_hbm,
    outs, gathered, wide, adapter, load_sem, store_sem,
):
    loads = [pltpu.make_async_copy(out_hbm.at[i], outs.at[i], load_sem.at[i]) for i in range(3)]
    loads += [pltpu.make_async_copy(ga_hbm.at[i], gathered.at[i], load_sem.at[3 + i]) for i in range(2)]
    for load in loads:
        load.start()
    stores = [
        pltpu.make_async_copy(wide.at[i], hbm, store_sem.at[i])
        for i, hbm in enumerate((q_hbm, k_hbm, v_hbm))
    ]
    stores += [pltpu.make_async_copy(adapter.at[i], adapter_hbm.at[i], store_sem.at[3 + i]) for i in range(2)]
    stores += [pltpu.make_async_copy(gi_hbm, input_hbm, store_sem.at[5])]
    stores[5].start()
    for i in range(3):
        loads[i].wait()
        wide[i] = unpadded([outs[i, 0], outs[i, 1]])
        stores[i].start()
    loads[3].wait()
    loads[4].wait()
    for i in range(2):
        heads = [
            gathered[unit, pair, :, i].reshape(RANK, PAD)[:, :HEAD].astype(F32)
            for pair in range(2) for unit in range(2)
        ]
        adapter[i] = jnp.concatenate(heads, axis=1)
        stores[3 + i].start()
    for store in stores:
        store.wait()


def body(
    query_base, key_base, value_base, adapter_activation, adapter_up_weight, output_grad,
    stretch_doc, doc_first, slot_stretch,
):
    n_tp = lax.axis_size("tp")
    side = math.isqrt(lax.axis_size("ctx") // 2)
    rows = RANK // side
    copies = S_ALONG + 6 * side + n_tp
    anywhere = pl.BlockSpec(memory_space=pltpu.HBM)
    smem = pl.BlockSpec(memory_space=pltpu.SMEM)

    def block(*shape, dtype=BF16):
        return pltpu.VMEM(shape, dtype)

    outs, grad_input, adapter = pl.pallas_call(
        functools.partial(kernel, side, n_tp),
        out_shape=(
            jax.ShapeDtypeStruct((3, 2, ROWS, PAIR), BF16),
            jax.ShapeDtypeStruct((ROWS, RANK), BF16),
            jax.ShapeDtypeStruct((2, 2, side, 2, rows, PAD), BF16),
        ),
        in_specs=[smem, smem] + [anywhere] * 6,
        out_specs=(anywhere,) * 3,
        scratch_shapes=[
            block(4, ROWS, COLUMNS),
            block(ROWS, RANK),
            block(2, RANK, COLUMNS),
            block(2, 2, RANK, PAIR),
            block(4, 2, ROWS, PAIR),
            block(4, ROWS, PAIR),
            block(ROWS, RANK),
            block(2, ROWS, RANK),
            block(WINDOW, RANK),
            block(2, ROWS, PAD),
            block(2, WINDOW, PAIR),
            block(2, GROUP_ROWS, PAIR),
            block(2, WINDOW, GROUP_ROWS, dtype=F32),
            block(2, WINDOW, GROUP_ROWS),
            block(2, SENT, PAIR),
            block(2, SENT, PAIR),
            block(2, GROUP_ROWS, PAIR, dtype=F32),
            block(2, GROUP_ROWS, PAIR),
            block(3, ROWS, PAIR),
            block(3, 2, ROWS, PAIR),
            block(ROWS, RANK, dtype=F32),
            block(ROWS, RANK, dtype=F32),
            block(n_tp, ROWS, RANK, dtype=F32),
            block(2, side, 2, rows, PAD),
            block(2, side, 2, rows, PAD),
            block(2, side, 2, rows, PAD),
            block(2, 2, side, 2, rows, PAD),
            block(ROWS, RANK),
            pltpu.SemaphoreType.DMA((6,)),
            pltpu.SemaphoreType.DMA((4,)),
            pltpu.SemaphoreType.DMA((copies,)),
            pltpu.SemaphoreType.DMA((copies,)),
        ],
        compiler_params=pltpu.CompilerParams(
            collective_id=0, has_side_effects=True, vmem_limit_bytes=56 * 2**20
        ),
    )(
        slot_stretch, doc_first, query_base, key_base, value_base, adapter_activation,
        adapter_up_weight, output_grad,
    )
    return pl.pallas_call(
        finish,
        out_shape=(
            jax.ShapeDtypeStruct((ROWS, COLUMNS), BF16),
            jax.ShapeDtypeStruct((ROWS, COLUMNS), BF16),
            jax.ShapeDtypeStruct((ROWS, COLUMNS), BF16),
            jax.ShapeDtypeStruct((ROWS, RANK), BF16),
            jax.ShapeDtypeStruct((2, RANK, COLUMNS), F32),
        ),
        in_specs=[anywhere] * 3,
        out_specs=(anywhere,) * 5,
        scratch_shapes=[
            block(3, 2, ROWS, PAIR),
            block(2, 2, side, 2, rows, PAD),
            block(3, ROWS, COLUMNS),
            block(2, RANK, COLUMNS, dtype=F32),
            pltpu.SemaphoreType.DMA((5,)),
            pltpu.SemaphoreType.DMA((6,)),
        ],
        compiler_params=pltpu.CompilerParams(vmem_limit_bytes=56 * 2**20),
    )(outs, grad_input, adapter)


def solution(mesh):
    return jax.shard_map(
        body,
        mesh=mesh,
        in_specs=(
            P("ctx", "tp"),
            P("ctx", "tp"),
            P("ctx", "tp"),
            P("ctx", None),
            P(None, None, "tp"),
            P("ctx", "tp"),
            P(),
            P(),
            P(),
        ),
        out_specs=(
            P("ctx", "tp"),
            P("ctx", "tp"),
            P("ctx", "tp"),
            P("ctx", None),
            P(None, None, "tp"),
        ),
        check_vma=False,
    )
```

```python
import functools
import math

import jax
import jax.numpy as jnp
from jax import lax
from jax.experimental import pallas as pl
from jax.experimental.pallas import tpu as pltpu
from jax.sharding import PartitionSpec as P

HEAD = 224
PAD = 256
HEADS = 4
PAIR = 2 * PAD
ROWS = 128
STRETCH = 64
GROUP_ROWS = 2 * ROWS
WINDOW = 2 * GROUP_ROWS
SENT = 3 * STRETCH
RANK = 128
COLUMNS = HEADS * HEAD
SCALE = HEAD ** -0.5
FILL = -1e30

KEY, VALUE, QUERY, GRAD = range(4)
S_KEY, S_VALUE, S_QUERY, S_GRAD, S_ACT = range(5)
S_OUT = 5
S_INPUT = 8
S_NEXT = 9
S_BACK = 13
S_PAST = 17
S_FIRST = 19
S_ALONG = 20
UNIT_AXIS = (0, 0, 1)
MESH = pl.DeviceIdType.MESH
F32 = jnp.float32
BF16 = jnp.bfloat16


def dot(a, b, contract):
    return lax.dot_general(a, b, ((contract[:1], contract[1:]), ((), ())), preferred_element_type=F32)


def padded(values):
    rows = values.shape[0]
    blank = jnp.zeros((rows, PAD - HEAD), values.dtype)
    parts = []
    for head in range(HEADS):
        parts += [values[:, head * HEAD:(head + 1) * HEAD], blank]
    return jnp.concatenate(parts, axis=1)


def unpadded(pairs):
    return jnp.concatenate(
        [pair[:, head * PAD:head * PAD + HEAD] for pair in pairs for head in range(2)], axis=1
    )


def kernel(
    side, n_tp,
    slot_ref, first_ref, q_hbm, k_hbm, v_hbm, a_hbm, w_hbm, g_hbm,
    out_hbm, gi_hbm, ga0_hbm, ga1_hbm, ga2_hbm,
    raw, act, weight, weight_pad, packed, sibling, act_sib, act_past, act_window, key_past,
    window_kv, sorted_qg, probs, probs_low, back_send, back_recv, own_kv,
    grads, sib_send, outs, gi_send, gi_sib, gi_along,
    part0, part1, part2, scattered0, scattered1, scattered2,
    crossed0, crossed1, crossed2, gathered0, gathered1, gathered2, gi_out,
    load_sem, store_sem, send_sem, recv_sem, entered_sem,
):
    part = (part0, part1, part2)
    scattered = (scattered0, scattered1, scattered2)
    crossed = (crossed0, crossed1, crossed2)
    gathered = (gathered0, gathered1, gathered2)
    me = lax.axis_index("ctx")
    tp = lax.axis_index("tp")
    core = lax.rem(me, 2)
    chip = lax.div(me, 2)
    y, z = lax.rem(chip, side), lax.div(chip, side)
    chips = side * side
    other = me + 1 - 2 * core
    after = lax.rem(chip + 1, chips) * 2 + core
    before = lax.rem(chip + chips - 1, chips) * 2 + core
    rows = RANK // side

    def along(axis, step):
        if axis == 0:
            return (z * side + lax.rem(y + step, side)) * 2 + core
        return (lax.rem(z + step, side) * side + y) * 2 + core

    def remote(src, dst, sem, ctx, x=None):
        return pltpu.make_async_remote_copy(
            src_ref=src, dst_ref=dst, send_sem=send_sem.at[sem], recv_sem=recv_sem.at[sem],
            device_id=(ctx, tp if x is None else x), device_id_type=MESH,
        )

    loads = [
        pltpu.make_async_copy(src, dst, load_sem.at[i])
        for i, (src, dst) in enumerate([
            (k_hbm, raw.at[KEY]), (a_hbm, act), (w_hbm, weight), (v_hbm, raw.at[VALUE]),
            (q_hbm, raw.at[QUERY]), (g_hbm, raw.at[GRAD]),
        ])
    ]
    loads[0].start()

    barrier = pltpu.get_barrier_semaphore()

    def greet(ctx, x):
        pl.semaphore_signal(barrier, inc=1, device_id=(ctx, x), device_id_type=MESH)

    steps = [side // 2 + (i // 2) * (1 - 2 * (i % 2)) for i in range(1, side)]
    near = [step for step in steps if min(step, side - step) <= 2]
    for step in near:
        greet(along(0, step), tp)
        greet(along(1, step), tp)
    for step in range(1, n_tp):
        greet(me, lax.rem(tp + step, n_tp))
    after_other = after + 1 - 2 * core
    before_other = before + 1 - 2 * core
    for device in (after, after_other, before, before_other, other):
        greet(device, tp)
    for load in loads[1:]:
        load.start()

    places = [
        slot_ref[2 * me] - 4 * chip, slot_ref[2 * me + 1] - 4 * chip,
        slot_ref[2 * other] - 4 * chip, slot_ref[2 * other + 1] - 4 * chip,
    ]
    past = lax.rem(chip + chips - 1, chips)
    past_places = [slot_ref[4 * past + j] - 4 * past for j in range(4)]

    def in_order(own, sib, places=places):
        slots = [own[:STRETCH], own[STRETCH:], sib[:STRETCH], sib[STRETCH:]]
        result = []
        for i in range(4):
            picked = slots[3]
            for j in (2, 1, 0):
                picked = jnp.where(places[j] == i, slots[j], picked)
            result.append(picked)
        return result

    def to_slots(values):
        result = []
        for j in range(4):
            picked = values[3 * STRETCH:]
            for i in (2, 1, 0):
                picked = jnp.where(places[j] == i, values[i * STRETCH:(i + 1) * STRETCH], picked)
            result.append(picked)
        return result

    def pack(kind, values):
        packed[kind, 0] = values[:, :PAIR]
        packed[kind, 1] = values[:, PAIR:]

    def to_sibling(kind, sem):
        return remote(packed.at[kind, 1 - core], sibling.at[kind], sem, other)

    loads[0].wait()
    pack(KEY, padded(raw[KEY]))
    loads[1].wait()
    pl.semaphore_wait(barrier, 5 + 2 * len(near) + n_tp - 1)
    sib_key = to_sibling(KEY, S_KEY)
    sib_key.start()
    sib_act = remote(act, act_sib, S_ACT, other)
    sib_act.start()
    first = pl.ds(0, PAD)
    next_first = [
        remote(packed.at[KEY, core, :, first], key_past.at[core], S_NEXT, after),
        remote(packed.at[KEY, 1 - core, :, first], key_past.at[core], S_FIRST, after_other),
    ]
    for copy in next_first:
        copy.start()
    next_act = remote(act, act_past.at[core], S_PAST, after)
    next_act.start()
    relays = [(axis, step) for axis in (0, 1) for step in (2, side - 2)] if len(near) < len(steps) else []
    for axis, step in relays:
        pl.semaphore_signal(entered_sem, inc=1, device_id=(along(axis, step), tp), device_id_type=MESH)
    loads[2].wait()
    for i in range(2):
        wide = padded(weight[i])
        weight_pad[i, 0] = wide[:, :PAIR]
        weight_pad[i, 1] = wide[:, PAIR:]

    def adapt(kind, i):
        wide = padded(raw[kind])
        for pair in range(2):
            update = dot(act[...], weight_pad[i, pair], (1, 0))
            base = wide[:, pair * PAIR:(pair + 1) * PAIR].astype(F32)
            packed[kind, pair] = (base + update).astype(BF16)

    loads[3].wait()
    adapt(VALUE, 1)
    sib_value = to_sibling(VALUE, S_VALUE)
    sib_value.start()

    def spread(kind):
        window_kv[kind, :STRETCH] = jnp.zeros((STRETCH, PAIR), BF16)
        for i, values in enumerate(in_order(packed[kind, core], sibling[kind])):
            window_kv[kind, GROUP_ROWS + i * STRETCH:GROUP_ROWS + (i + 1) * STRETCH] = values

    def to_next(kind, head):
        lanes = pl.ds(head * PAD, PAD)
        return remote(
            window_kv.at[kind, pl.ds(GROUP_ROWS + STRETCH, SENT), lanes],
            window_kv.at[kind, pl.ds(STRETCH, SENT), lanes], S_NEXT + 2 * head + kind, after,
        )

    next_kv = {}
    sib_key.wait_recv()
    spread(KEY)
    sib_value.wait_recv()
    spread(VALUE)
    for kind, head in ((VALUE, 0), (KEY, 1), (VALUE, 1)):
        next_kv[kind, head] = to_next(kind, head)
        next_kv[kind, head].start()

    loads[4].wait()
    adapt(QUERY, 0)
    sib_query = to_sibling(QUERY, S_QUERY)
    sib_query.start()
    loads[5].wait()
    pack(GRAD, padded(raw[GRAD]))
    sib_grad = to_sibling(GRAD, S_GRAD)
    sib_grad.start()

    sib_act.wait_recv()
    for i, values in enumerate(in_order(act[...], act_sib[...])):
        act_window[GROUP_ROWS + i * STRETCH:GROUP_ROWS + (i + 1) * STRETCH] = values
    for kind, copy in ((QUERY, sib_query), (GRAD, sib_grad)):
        copy.wait_recv()
        for i, values in enumerate(in_order(packed[kind, core], sibling[kind])):
            sorted_qg[kind - QUERY, i * STRETCH:(i + 1) * STRETCH] = values
    next_act.wait_recv()
    pass_act = remote(act_past.at[core], act_past.at[core], S_PAST + 1, other)
    pass_act.start()

    key_place = lax.broadcasted_iota(jnp.int32, (WINDOW, GROUP_ROWS), 0)
    query_place = lax.broadcasted_iota(jnp.int32, (1, GROUP_ROWS), 1)
    lowest = jnp.zeros((1, GROUP_ROWS), jnp.int32)
    for i in range(4):
        start = STRETCH * (first_ref[4 * chip + i] - 4 * chip + 4)
        lowest = jnp.where(query_place >= i * STRETCH, start, lowest)
    visible = (key_place >= lowest) & (key_place <= query_place + GROUP_ROWS)

    def along_sem(unit, stage, step):
        return S_ALONG + (unit * 4 + stage) * side + step

    def position(unit, crossing):
        return (y, z)[UNIT_AXIS[unit] ^ crossing]

    def scatter(unit, step):
        target = lax.rem(position(unit, 0) + step, side)
        return remote(
            part[unit].at[target], scattered[unit].at[step], along_sem(unit, 0, step),
            along(UNIT_AXIS[unit], step),
        )

    def cross(unit, step):
        block = crossed[unit].at[position(unit, 1)]
        return remote(block, block, along_sem(unit, 1, step), along(1 - UNIT_AXIS[unit], step))

    def gather(unit, step):
        block = gathered[unit].at[core, position(unit, 0)]
        return remote(block, block, along_sem(unit, 2, step), along(UNIT_AXIS[unit], step))

    def gather_other(unit, step):
        block = gathered[unit].at[core, position(unit, 0)]
        target = along(UNIT_AXIS[unit], step) + 1 - 2 * core
        return remote(block, block, along_sem(unit, 3, step), target)

    def each(make, unit, method, first=1):
        def run(step, carry):
            getattr(make(unit, step), method)()
            return carry

        lax.fori_loop(first, side, run, 0)

    def adapter_terms(block, activations, values):
        terms = dot(activations, values, (0, 0)).astype(BF16)
        for j in range(side):
            block(j)[...] = terms[j * rows:(j + 1) * rows]

    def send_unit(unit):
        for step in steps:
            scatter(unit, step).start()

    def back(kind, head):
        lanes = pl.ds(head * PAD, PAD)
        return remote(
            back_send.at[kind, :, lanes], back_recv.at[kind, :, lanes],
            S_BACK + 2 * head + kind, before,
        )

    backs = {}
    for head in range(2):
        lanes = slice(head * PAD, (head + 1) * PAD)
        if head:
            next_kv[KEY, head].wait_recv()
        else:
            for copy in next_first:
                copy.wait_recv()
            for i, values in enumerate(in_order(key_past[0], key_past[1], past_places)):
                if i:
                    window_kv[KEY, i * STRETCH:(i + 1) * STRETCH, lanes] = values
        scores = dot(window_kv[KEY, :, lanes], sorted_qg[0, :, lanes], (1, 1)) * SCALE
        scores = jnp.where(visible, scores, FILL)
        peak = jnp.max(scores, axis=0, keepdims=True)
        weights = jnp.exp(scores - peak)
        share = weights / jnp.sum(weights, axis=0, keepdims=True)
        probs[head] = share
        low = share.astype(BF16)
        probs_low[head] = low
        terms = dot(low, sorted_qg[1, :, lanes], (1, 0))
        own_kv[VALUE, :, lanes] = terms[GROUP_ROWS:]
        terms = terms.astype(BF16)
        back_send[VALUE, :, lanes] = terms[STRETCH:GROUP_ROWS]
        backs[VALUE, head] = back(VALUE, head)
        backs[VALUE, head].start()
        if not head:
            pass_act.wait_recv()
            act_window[:STRETCH] = jnp.zeros((STRETCH, RANK), BF16)
            for i, values in enumerate(in_order(act_past[0], act_past[1], past_places)):
                if i:
                    act_window[i * STRETCH:(i + 1) * STRETCH] = values
        if head:
            adapter_terms(lambda j: part[1].at[j], act_window[...], terms)
            send_unit(1)
        else:
            adapter_terms(lambda j: part[0].at[j, 1], act_window[...], terms)

        next_kv[VALUE, head].wait_recv()
        grad_probs = dot(window_kv[VALUE, :, lanes], sorted_qg[1, :, lanes], (1, 1))
        row_dot = jnp.sum(probs_low[head].astype(F32) * grad_probs, axis=0, keepdims=True)
        grad_scores = (probs[head] * (grad_probs - row_dot)).astype(BF16)
        summed = (dot(grad_scores, window_kv[KEY, :, lanes], (0, 0)) * SCALE).astype(BF16)
        grads[0, :, lanes] = summed
        if head:
            adapter_terms(lambda j: part[2].at[j], act_window[GROUP_ROWS:], summed)
            send_unit(2)
        else:
            adapter_terms(lambda j: part[0].at[j, 0], act_window[GROUP_ROWS:], summed)
            if relays:
                pl.semaphore_wait(entered_sem, len(relays))
            send_unit(0)
        terms = dot(grad_scores, sorted_qg[0, :, lanes], (1, 0)) * SCALE
        back_send[KEY, :, lanes] = terms[STRETCH:GROUP_ROWS].astype(BF16)
        own_kv[KEY, :, lanes] = terms[GROUP_ROWS:]
        backs[KEY, head] = back(KEY, head)
        backs[KEY, head].start()

    def input_terms(i, values):
        return dot(values, weight_pad[i, core], (1, 1))

    def hand_out(i, slots):
        outs[i, core, :STRETCH] = slots[0]
        outs[i, core, STRETCH:] = slots[1]
        sib_send[i, :STRETCH] = slots[2]
        sib_send[i, STRETCH:] = slots[3]
        copy = remote(sib_send.at[i], outs.at[i, core], S_OUT + i, other)
        copy.start()
        return copy

    def add_back(kind):
        mine = own_kv[kind]
        return jnp.concatenate(
            [mine[:STRETCH], mine[STRETCH:] + back_recv[kind].astype(F32)], axis=0
        ).astype(BF16)

    def go_across(unit):
        each(scatter, unit, "wait_recv")
        total = part[unit][position(unit, 0)].astype(F32)
        for step in range(1, side):
            total = total + scattered[unit][step].astype(F32)
        crossed[unit][position(unit, 1)] = total.astype(BF16)
        for step in steps:
            cross(unit, step).start()

    def go_around(unit):
        each(cross, unit, "wait_recv")
        total = crossed[unit][0].astype(F32)
        for step in range(1, side):
            total = total + crossed[unit][step].astype(F32)
        gathered[unit][core, position(unit, 0)] = total.astype(BF16)
        for step in steps:
            gather(unit, step).start()
            gather_other(unit, step).start()
        gather_other(unit, 0).start()

    input_part = input_terms(0, grads[0])
    out_query = hand_out(0, to_slots(grads[0]))
    go_across(0)

    for head in range(2):
        backs[VALUE, head].wait_recv()
    grads[1] = add_back(VALUE)
    input_slots = to_slots(input_part + input_terms(1, grads[1]))
    gi_send[:STRETCH] = input_slots[2]
    gi_send[STRETCH:] = input_slots[3]
    sib_input = remote(gi_send, gi_sib, S_INPUT, other)
    sib_input.start()
    gi_along[tp, :STRETCH] = input_slots[0]
    gi_along[tp, STRETCH:] = input_slots[1]
    out_value = hand_out(2, to_slots(grads[1]))

    go_across(1)
    go_across(2)

    sib_input.wait_recv()
    gi_along[tp] = gi_along[tp] + gi_sib[...]

    def tp_copy(step):
        return remote(
            gi_along.at[tp], gi_along.at[tp], S_ALONG + 12 * side + step, me, lax.rem(tp + step, n_tp)
        )

    def each_tp(method):
        def run(step, carry):
            getattr(tp_copy(step), method)()
            return carry

        lax.fori_loop(1, n_tp, run, 0)

    each_tp("start")
    for head in range(2):
        backs[KEY, head].wait_recv()
    out_key = hand_out(1, to_slots(add_back(KEY)))

    go_around(0)
    go_around(1)
    each_tp("wait_recv")
    total = gi_along[0]
    for x in range(1, n_tp):
        total = total + gi_along[x]
    gi_out[...] = total.astype(BF16)
    stores = [pltpu.make_async_copy(gi_out, gi_hbm, store_sem.at[0])]
    stores[0].start()
    go_around(2)

    for copy in (out_query, out_value, out_key):
        copy.wait_recv()
    stores.append(pltpu.make_async_copy(outs, out_hbm, store_sem.at[1]))
    stores[1].start()

    for copy in (
        sib_key, sib_act, sib_value, sib_query, sib_grad, *next_first, next_act, pass_act,
        *next_kv.values(), *backs.values(), out_query, out_value, out_key, sib_input,
    ):
        copy.wait_send()
    each_tp("wait_send")
    for unit in range(3):
        each(scatter, unit, "wait_send")
        each(cross, unit, "wait_send")
    for unit, hbm in enumerate((ga0_hbm, ga1_hbm, ga2_hbm)):
        each(gather, unit, "wait_recv")
        each(gather_other, unit, "wait_recv", 0)
        stores.append(pltpu.make_async_copy(gathered[unit], hbm, store_sem.at[2 + unit]))
        stores[2 + unit].start()
    for unit in range(3):
        each(gather, unit, "wait_send")
        each(gather_other, unit, "wait_send", 0)
    for store in stores:
        store.wait()


def finish(
    out_hbm, gi_hbm, ga0_hbm, ga1_hbm, ga2_hbm, q_hbm, k_hbm, v_hbm, input_hbm, adapter_hbm,
    outs, head0, value1, query1, wide, adapter, load_sem, store_sem,
):
    loads = [pltpu.make_async_copy(out_hbm.at[i], outs.at[i], load_sem.at[i]) for i in range(3)]
    loads += [
        pltpu.make_async_copy(hbm, block, load_sem.at[3 + i])
        for i, (hbm, block) in enumerate(((ga0_hbm, head0), (ga1_hbm, value1), (ga2_hbm, query1)))
    ]
    for load in loads:
        load.start()
    stores = [
        pltpu.make_async_copy(wide.at[i], hbm, store_sem.at[i])
        for i, hbm in enumerate((q_hbm, k_hbm, v_hbm))
    ]
    stores += [pltpu.make_async_copy(adapter.at[i], adapter_hbm.at[i], store_sem.at[3 + i]) for i in range(2)]
    stores += [pltpu.make_async_copy(gi_hbm, input_hbm, store_sem.at[5])]
    stores[5].start()
    for i in range(3):
        loads[i].wait()
        wide[i] = unpadded([outs[i, 0], outs[i, 1]])
        stores[i].start()
    loads[3].wait()
    for i, head1 in ((1, value1), (0, query1)):
        loads[5 - i].wait()
        heads = []
        for pair in range(2):
            heads += [head0[pair, :, i], head1[pair]]
        heads = [head.reshape(RANK, PAD)[:, :HEAD].astype(F32) for head in heads]
        adapter[i] = jnp.concatenate(heads, axis=1)
        stores[3 + i].start()
    for store in stores:
        store.wait()


def body(
    query_base, key_base, value_base, adapter_activation, adapter_up_weight, output_grad,
    stretch_doc, doc_first, slot_stretch,
):
    n_tp = lax.axis_size("tp")
    side = math.isqrt(lax.axis_size("ctx") // 2)
    rows = RANK // side
    copies = S_ALONG + 12 * side + n_tp
    anywhere = pl.BlockSpec(memory_space=pltpu.HBM)
    smem = pl.BlockSpec(memory_space=pltpu.SMEM)

    def block(*shape, dtype=BF16):
        return pltpu.VMEM(shape, dtype)

    partial_results = pl.pallas_call(
        functools.partial(kernel, side, n_tp),
        out_shape=(
            jax.ShapeDtypeStruct((3, 2, ROWS, PAIR), BF16),
            jax.ShapeDtypeStruct((ROWS, RANK), BF16),
            jax.ShapeDtypeStruct((2, side, 2, rows, PAD), BF16),
            jax.ShapeDtypeStruct((2, side, rows, PAD), BF16),
            jax.ShapeDtypeStruct((2, side, rows, PAD), BF16),
        ),
        in_specs=[smem, smem] + [anywhere] * 6,
        out_specs=(anywhere,) * 5,
        scratch_shapes=[
            block(4, ROWS, COLUMNS),
            block(ROWS, RANK),
            block(2, RANK, COLUMNS),
            block(2, 2, RANK, PAIR),
            block(4, 2, ROWS, PAIR),
            block(4, ROWS, PAIR),
            block(ROWS, RANK),
            block(2, ROWS, RANK),
            block(WINDOW, RANK),
            block(2, ROWS, PAD),
            block(2, WINDOW, PAIR),
            block(2, GROUP_ROWS, PAIR),
            block(2, WINDOW, GROUP_ROWS, dtype=F32),
            block(2, WINDOW, GROUP_ROWS),
            block(2, SENT, PAIR),
            block(2, SENT, PAIR),
            block(2, GROUP_ROWS, PAIR, dtype=F32),
            block(2, GROUP_ROWS, PAIR),
            block(3, ROWS, PAIR),
            block(3, 2, ROWS, PAIR),
            block(ROWS, RANK, dtype=F32),
            block(ROWS, RANK, dtype=F32),
            block(n_tp, ROWS, RANK, dtype=F32),
            *((block(side, 2, rows, PAD), block(side, rows, PAD), block(side, rows, PAD)) * 3),
            block(2, side, 2, rows, PAD),
            block(2, side, rows, PAD),
            block(2, side, rows, PAD),
            block(ROWS, RANK),
            pltpu.SemaphoreType.DMA((6,)),
            pltpu.SemaphoreType.DMA((5,)),
            pltpu.SemaphoreType.DMA((copies,)),
            pltpu.SemaphoreType.DMA((copies,)),
            pltpu.SemaphoreType.REGULAR,
        ],
        compiler_params=pltpu.CompilerParams(
            collective_id=0, has_side_effects=True, vmem_limit_bytes=56 * 2**20
        ),
    )(
        slot_stretch, doc_first, query_base, key_base, value_base, adapter_activation,
        adapter_up_weight, output_grad,
    )
    return pl.pallas_call(
        finish,
        out_shape=(
            jax.ShapeDtypeStruct((ROWS, COLUMNS), BF16),
            jax.ShapeDtypeStruct((ROWS, COLUMNS), BF16),
            jax.ShapeDtypeStruct((ROWS, COLUMNS), BF16),
            jax.ShapeDtypeStruct((ROWS, RANK), BF16),
            jax.ShapeDtypeStruct((2, RANK, COLUMNS), F32),
        ),
        in_specs=[anywhere] * 5,
        out_specs=(anywhere,) * 5,
        scratch_shapes=[
            block(3, 2, ROWS, PAIR),
            block(2, side, 2, rows, PAD),
            block(2, side, rows, PAD),
            block(2, side, rows, PAD),
            block(3, ROWS, COLUMNS),
            block(2, RANK, COLUMNS, dtype=F32),
            pltpu.SemaphoreType.DMA((6,)),
            pltpu.SemaphoreType.DMA((6,)),
        ],
        compiler_params=pltpu.CompilerParams(vmem_limit_bytes=56 * 2**20),
    )(*partial_results)


def solution(mesh):
    return jax.shard_map(
        body,
        mesh=mesh,
        in_specs=(
            P("ctx", "tp"),
            P("ctx", "tp"),
            P("ctx", "tp"),
            P("ctx", None),
            P(None, None, "tp"),
            P("ctx", "tp"),
            P(),
            P(),
            P(),
        ),
        out_specs=(
            P("ctx", "tp"),
            P("ctx", "tp"),
            P("ctx", "tp"),
            P("ctx", None),
            P(None, None, "tp"),
        ),
        check_vma=False,
    )
```

```python
import functools
import math

import jax
import jax.numpy as jnp
from jax import lax
from jax.experimental import pallas as pl
from jax.experimental.pallas import tpu as pltpu
from jax.sharding import PartitionSpec as P

HEAD = 224
PAD = 256
HEADS = 4
PAIR = 2 * PAD
ROWS = 128
STRETCH = 64
GROUP_ROWS = 2 * ROWS
WINDOW = 2 * GROUP_ROWS
SENT = 3 * STRETCH
RANK = 128
COLUMNS = HEADS * HEAD
SCALE = HEAD ** -0.5
FILL = -1e30

KEY, VALUE, QUERY, GRAD = range(4)
S_KEY, S_VALUE, S_QUERY, S_GRAD, S_ACT = range(5)
S_OUT = 5
S_INPUT = 8
S_NEXT = 9
S_BACK = 13
S_PAST = 17
S_FIRST = 19
S_ADAPTER = 20
S_ALONG = 23
S_INPUTS = 32
COPIES = 33
UNIT_AXIS = (0, 0, 1)
MESH = pl.DeviceIdType.MESH
F32 = jnp.float32
BF16 = jnp.bfloat16


def dot(a, b, contract):
    return lax.dot_general(a, b, ((contract[:1], contract[1:]), ((), ())), preferred_element_type=F32)


def padded(values):
    rows = values.shape[0]
    blank = jnp.zeros((rows, PAD - HEAD), values.dtype)
    parts = []
    for head in range(HEADS):
        parts += [values[:, head * HEAD:(head + 1) * HEAD], blank]
    return jnp.concatenate(parts, axis=1)


def unpadded(pairs):
    return jnp.concatenate(
        [pair[:, head * PAD:head * PAD + HEAD] for pair in pairs for head in range(2)], axis=1
    )


def kernel(
    side, n_tp,
    slot_ref, first_ref, q_hbm, k_hbm, v_hbm, a_hbm, w_hbm, g_hbm,
    out_hbm, gi_hbm, ga0_hbm, ga1_hbm, ga2_hbm,
    raw, act, weight, weight_pad, packed, sibling, act_sib, act_past, act_window, key_past,
    window_kv, sorted_qg, probs, probs_low, back_send, back_recv, own_kv,
    grads, sib_send, outs, gi_send, gi_sib, gi_along,
    part0, part1, part2, scattered0, scattered1, scattered2,
    crossed0, crossed1, crossed2, gathered0, gathered1, gathered2, gi_out,
    load_sem, store_sem, send_sem, recv_sem, entered_sem,
):
    part = (part0, part1, part2)
    scattered = (scattered0, scattered1, scattered2)
    crossed = (crossed0, crossed1, crossed2)
    gathered = (gathered0, gathered1, gathered2)
    me = lax.axis_index("ctx")
    tp = lax.axis_index("tp")
    core = lax.rem(me, 2)
    chip = lax.div(me, 2)
    y, z = lax.rem(chip, side), lax.div(chip, side)
    chips = side * side
    other = me + 1 - 2 * core
    after = lax.rem(chip + 1, chips) * 2 + core
    before = lax.rem(chip + chips - 1, chips) * 2 + core
    rows = RANK // side

    def along(axis, step):
        if axis == 0:
            return (z * side + lax.rem(y + step, side)) * 2 + core
        return (lax.rem(z + step, side) * side + y) * 2 + core

    def remote(src, dst, sem, ctx, x=None):
        return pltpu.make_async_remote_copy(
            src_ref=src, dst_ref=dst, send_sem=send_sem.at[sem], recv_sem=recv_sem.at[sem],
            device_id=(ctx, tp if x is None else x), device_id_type=MESH,
        )

    loads = [
        pltpu.make_async_copy(src, dst, load_sem.at[i])
        for i, (src, dst) in enumerate([
            (k_hbm, raw.at[KEY]), (a_hbm, act), (w_hbm, weight), (v_hbm, raw.at[VALUE]),
            (q_hbm, raw.at[QUERY]), (g_hbm, raw.at[GRAD]),
        ])
    ]
    loads[0].start()

    barrier = pltpu.get_barrier_semaphore()

    def greet(ctx, x):
        pl.semaphore_signal(barrier, inc=1, device_id=(ctx, x), device_id_type=MESH)

    steps = [side // 2 + (i // 2) * (1 - 2 * (i % 2)) for i in range(1, side)]
    near = [step for step in steps if min(step, side - step) <= 2]
    for step in near:
        greet(along(0, step), tp)
        greet(along(1, step), tp)
    for step in range(1, n_tp):
        greet(me, lax.rem(tp + step, n_tp))
    after_other = after + 1 - 2 * core
    before_other = before + 1 - 2 * core
    for device in (after, after_other, before, before_other, other):
        greet(device, tp)
    for load in loads[1:]:
        load.start()

    places = [
        slot_ref[2 * me] - 4 * chip, slot_ref[2 * me + 1] - 4 * chip,
        slot_ref[2 * other] - 4 * chip, slot_ref[2 * other + 1] - 4 * chip,
    ]
    past = lax.rem(chip + chips - 1, chips)
    past_places = [slot_ref[4 * past + j] - 4 * past for j in range(4)]

    def in_order(own, sib, places=places):
        slots = [own[:STRETCH], own[STRETCH:], sib[:STRETCH], sib[STRETCH:]]
        result = []
        for i in range(4):
            picked = slots[3]
            for j in (2, 1, 0):
                picked = jnp.where(places[j] == i, slots[j], picked)
            result.append(picked)
        return result

    def to_slots(values):
        result = []
        for j in range(4):
            picked = values[3 * STRETCH:]
            for i in (2, 1, 0):
                picked = jnp.where(places[j] == i, values[i * STRETCH:(i + 1) * STRETCH], picked)
            result.append(picked)
        return result

    def pack(kind, values):
        packed[kind, 0] = values[:, :PAIR]
        packed[kind, 1] = values[:, PAIR:]

    def to_sibling(kind, sem):
        return remote(packed.at[kind, 1 - core], sibling.at[kind], sem, other)

    loads[0].wait()
    pack(KEY, padded(raw[KEY]))
    loads[1].wait()
    pl.semaphore_wait(barrier, 5 + 2 * len(near) + n_tp - 1)
    sib_key = to_sibling(KEY, S_KEY)
    sib_key.start()
    sib_act = remote(act, act_sib, S_ACT, other)
    sib_act.start()
    first = pl.ds(0, PAD)
    next_first = [
        remote(packed.at[KEY, core, :, first], key_past.at[core], S_NEXT, after),
        remote(packed.at[KEY, 1 - core, :, first], key_past.at[core], S_FIRST, after_other),
    ]
    for copy in next_first:
        copy.start()
    next_act = remote(act, act_past.at[core], S_PAST, after)
    next_act.start()
    relays = [(axis, step) for axis in (0, 1) for step in (2, side - 2)] if len(near) < len(steps) else []
    for axis, step in relays:
        pl.semaphore_signal(entered_sem, inc=1, device_id=(along(axis, step), tp), device_id_type=MESH)
    loads[2].wait()
    for i in range(2):
        wide = padded(weight[i])
        weight_pad[i, 0] = wide[:, :PAIR]
        weight_pad[i, 1] = wide[:, PAIR:]

    def adapt(kind, i):
        wide = padded(raw[kind])
        for pair in range(2):
            update = dot(act[...], weight_pad[i, pair], (1, 0))
            base = wide[:, pair * PAIR:(pair + 1) * PAIR].astype(F32)
            packed[kind, pair] = (base + update).astype(BF16)

    loads[3].wait()
    adapt(VALUE, 1)
    sib_value = to_sibling(VALUE, S_VALUE)
    sib_value.start()

    def spread(kind):
        window_kv[kind, :STRETCH] = jnp.zeros((STRETCH, PAIR), BF16)
        for i, values in enumerate(in_order(packed[kind, core], sibling[kind])):
            window_kv[kind, GROUP_ROWS + i * STRETCH:GROUP_ROWS + (i + 1) * STRETCH] = values

    def to_next(kind, head):
        lanes = pl.ds(head * PAD, PAD)
        return remote(
            window_kv.at[kind, pl.ds(GROUP_ROWS + STRETCH, SENT), lanes],
            window_kv.at[kind, pl.ds(STRETCH, SENT), lanes], S_NEXT + 2 * head + kind, after,
        )

    next_kv = {}
    sib_key.wait_recv()
    spread(KEY)
    sib_value.wait_recv()
    spread(VALUE)
    for kind, head in ((VALUE, 0), (KEY, 1), (VALUE, 1)):
        next_kv[kind, head] = to_next(kind, head)
        next_kv[kind, head].start()

    loads[4].wait()
    adapt(QUERY, 0)
    sib_query = to_sibling(QUERY, S_QUERY)
    sib_query.start()
    loads[5].wait()
    pack(GRAD, padded(raw[GRAD]))
    sib_grad = to_sibling(GRAD, S_GRAD)
    sib_grad.start()

    sib_act.wait_recv()
    for i, values in enumerate(in_order(act[...], act_sib[...])):
        act_window[GROUP_ROWS + i * STRETCH:GROUP_ROWS + (i + 1) * STRETCH] = values
    for kind, copy in ((QUERY, sib_query), (GRAD, sib_grad)):
        copy.wait_recv()
        for i, values in enumerate(in_order(packed[kind, core], sibling[kind])):
            sorted_qg[kind - QUERY, i * STRETCH:(i + 1) * STRETCH] = values
    next_act.wait_recv()
    pass_act = remote(act_past.at[core], act_past.at[core], S_PAST + 1, other)
    pass_act.start()

    key_place = lax.broadcasted_iota(jnp.int32, (WINDOW, GROUP_ROWS), 0)
    query_place = lax.broadcasted_iota(jnp.int32, (1, GROUP_ROWS), 1)
    lowest = jnp.zeros((1, GROUP_ROWS), jnp.int32)
    for i in range(4):
        start = STRETCH * (first_ref[4 * chip + i] - 4 * chip + 4)
        lowest = jnp.where(query_place >= i * STRETCH, start, lowest)
    visible = (key_place >= lowest) & (key_place <= query_place + GROUP_ROWS)

    def position(unit, crossing):
        return (y, z)[UNIT_AXIS[unit] ^ crossing]

    def scatter(unit, step):
        target = lax.rem(position(unit, 0) + step, side)
        return remote(
            part[unit].at[target], scattered[unit].at[step], S_ALONG + 3 * unit, along(UNIT_AXIS[unit], step)
        )

    def cross(unit, step):
        block = crossed[unit].at[position(unit, 1)]
        return remote(block, block, S_ALONG + 3 * unit + 1, along(1 - UNIT_AXIS[unit], step))

    def gather(unit, step):
        block = gathered[unit].at[core, position(unit, 0)]
        return remote(block, block, S_ALONG + 3 * unit + 2, along(UNIT_AXIS[unit], step))

    def stage(unit, which):
        block = scattered[unit].at[pl.ds(1, side - 1)]
        return remote(block, block, S_ALONG + 3 * unit + which, other)

    def adapter_terms(block, activations, values):
        terms = dot(activations, values, (0, 0)).astype(BF16)
        for j in range(side):
            block(j)[...] = terms[j * rows:(j + 1) * rows]

    def send_unit(unit):
        for step in steps:
            scatter(unit, step).start()

    def back(kind, head):
        lanes = pl.ds(head * PAD, PAD)
        return remote(
            back_send.at[kind, :, lanes], back_recv.at[kind, :, lanes],
            S_BACK + 2 * head + kind, before,
        )

    backs = {}
    for head in range(2):
        lanes = slice(head * PAD, (head + 1) * PAD)
        if head:
            next_kv[KEY, head].wait_recv()
        else:
            for copy in next_first:
                copy.wait_recv()
            for i, values in enumerate(in_order(key_past[0], key_past[1], past_places)):
                if i:
                    window_kv[KEY, i * STRETCH:(i + 1) * STRETCH, lanes] = values
        scores = dot(window_kv[KEY, :, lanes], sorted_qg[0, :, lanes], (1, 1)) * SCALE
        scores = jnp.where(visible, scores, FILL)
        peak = jnp.max(scores, axis=0, keepdims=True)
        weights = jnp.exp(scores - peak)
        share = weights / jnp.sum(weights, axis=0, keepdims=True)
        probs[head] = share
        low = share.astype(BF16)
        probs_low[head] = low
        terms = dot(low, sorted_qg[1, :, lanes], (1, 0))
        own_kv[VALUE, :, lanes] = terms[GROUP_ROWS:]
        terms = terms.astype(BF16)
        back_send[VALUE, :, lanes] = terms[STRETCH:GROUP_ROWS]
        backs[VALUE, head] = back(VALUE, head)
        backs[VALUE, head].start()
        if not head:
            pass_act.wait_recv()
            act_window[:STRETCH] = jnp.zeros((STRETCH, RANK), BF16)
            for i, values in enumerate(in_order(act_past[0], act_past[1], past_places)):
                if i:
                    act_window[i * STRETCH:(i + 1) * STRETCH] = values
        if head:
            adapter_terms(lambda j: part[1].at[j], act_window[...], terms)
            send_unit(1)
        else:
            adapter_terms(lambda j: part[0].at[j, 1], act_window[...], terms)

        next_kv[VALUE, head].wait_recv()
        grad_probs = dot(window_kv[VALUE, :, lanes], sorted_qg[1, :, lanes], (1, 1))
        row_dot = jnp.sum(probs_low[head].astype(F32) * grad_probs, axis=0, keepdims=True)
        grad_scores = (probs[head] * (grad_probs - row_dot)).astype(BF16)
        summed = (dot(grad_scores, window_kv[KEY, :, lanes], (0, 0)) * SCALE).astype(BF16)
        grads[0, :, lanes] = summed
        if head:
            adapter_terms(lambda j: part[2].at[j], act_window[GROUP_ROWS:], summed)
            send_unit(2)
        else:
            adapter_terms(lambda j: part[0].at[j, 0], act_window[GROUP_ROWS:], summed)
            if relays:
                pl.semaphore_wait(entered_sem, len(relays))
            send_unit(0)
        terms = dot(grad_scores, sorted_qg[0, :, lanes], (1, 0)) * SCALE
        back_send[KEY, :, lanes] = terms[STRETCH:GROUP_ROWS].astype(BF16)
        own_kv[KEY, :, lanes] = terms[GROUP_ROWS:]
        backs[KEY, head] = back(KEY, head)
        backs[KEY, head].start()

    def input_terms(i, values):
        return dot(values, weight_pad[i, core], (1, 1))

    def hand_out(i, slots):
        outs[i, core, :STRETCH] = slots[0]
        outs[i, core, STRETCH:] = slots[1]
        sib_send[i, :STRETCH] = slots[2]
        sib_send[i, STRETCH:] = slots[3]
        copy = remote(sib_send.at[i], outs.at[i, core], S_OUT + i, other)
        copy.start()
        return copy

    def add_back(kind):
        mine = own_kv[kind]
        return jnp.concatenate(
            [mine[:STRETCH], mine[STRETCH:] + back_recv[kind].astype(F32)], axis=0
        ).astype(BF16)

    def go_across(unit):
        stage(unit, 0).wait_recv()
        total = part[unit][position(unit, 0)].astype(F32)
        for step in range(1, side):
            total = total + scattered[unit][step].astype(F32)
        crossed[unit][position(unit, 1)] = total.astype(BF16)
        for step in steps:
            cross(unit, step).start()

    def go_around(unit):
        stage(unit, 1).wait_recv()
        total = crossed[unit][0].astype(F32)
        for step in range(1, side):
            total = total + crossed[unit][step].astype(F32)
        gathered[unit][core, position(unit, 0)] = total.astype(BF16)
        for step in steps:
            gather(unit, step).start()

    input_part = input_terms(0, grads[0])
    out_query = hand_out(0, to_slots(grads[0]))
    go_across(0)

    for head in range(2):
        backs[VALUE, head].wait_recv()
    grads[1] = add_back(VALUE)
    input_slots = to_slots(input_part + input_terms(1, grads[1]))
    gi_send[:STRETCH] = input_slots[2]
    gi_send[STRETCH:] = input_slots[3]
    sib_input = remote(gi_send, gi_sib, S_INPUT, other)
    sib_input.start()
    gi_along[tp, :STRETCH] = input_slots[0]
    gi_along[tp, STRETCH:] = input_slots[1]
    out_value = hand_out(2, to_slots(grads[1]))

    go_across(1)
    go_across(2)

    sib_input.wait_recv()
    gi_along[tp] = gi_along[tp] + gi_sib[...]

    for step in range(1, n_tp):
        block = gi_along.at[tp]
        remote(block, block, S_INPUTS, me, lax.rem(tp + step, n_tp)).start()
    block = gi_along.at[pl.ds(1, n_tp - 1)]
    tp_inputs = remote(block, block, S_INPUTS, other)
    for head in range(2):
        backs[KEY, head].wait_recv()
    out_key = hand_out(1, to_slots(add_back(KEY)))

    go_around(0)
    go_around(1)
    tp_inputs.wait_recv()
    total = gi_along[0]
    for x in range(1, n_tp):
        total = total + gi_along[x]
    gi_out[...] = total.astype(BF16)
    stores = [pltpu.make_async_copy(gi_out, gi_hbm, store_sem.at[0])]
    stores[0].start()
    go_around(2)

    for copy in (out_query, out_value, out_key):
        copy.wait_recv()
    stores.append(pltpu.make_async_copy(outs, out_hbm, store_sem.at[1]))
    stores[1].start()

    for copy in (
        sib_key, sib_act, sib_value, sib_query, sib_grad, *next_first, next_act, pass_act,
        *next_kv.values(), *backs.values(), out_query, out_value, out_key, sib_input,
    ):
        copy.wait_send()
    tp_inputs.wait_send()
    sib_adapter = []
    for unit in range(3):
        stage(unit, 0).wait_send()
        stage(unit, 1).wait_send()
    for unit in range(3):
        stage(unit, 2).wait_recv()
        block = gathered[unit].at[core]
        copy = remote(block, block, S_ADAPTER + unit, other)
        copy.start()
        sib_adapter.append(copy)
        stage(unit, 2).wait_send()
    for unit, hbm in enumerate((ga0_hbm, ga1_hbm, ga2_hbm)):
        sib_adapter[unit].wait_recv()
        stores.append(pltpu.make_async_copy(gathered[unit], hbm, store_sem.at[2 + unit]))
        stores[2 + unit].start()
        sib_adapter[unit].wait_send()
    for store in stores:
        store.wait()


def finish(
    out_hbm, gi_hbm, ga0_hbm, ga1_hbm, ga2_hbm, q_hbm, k_hbm, v_hbm, input_hbm, adapter_hbm,
    outs, head0, value1, query1, wide, adapter, load_sem, store_sem,
):
    loads = [pltpu.make_async_copy(out_hbm.at[i], outs.at[i], load_sem.at[i]) for i in range(3)]
    loads += [
        pltpu.make_async_copy(hbm, block, load_sem.at[3 + i])
        for i, (hbm, block) in enumerate(((ga0_hbm, head0), (ga1_hbm, value1), (ga2_hbm, query1)))
    ]
    for load in loads:
        load.start()
    stores = [
        pltpu.make_async_copy(wide.at[i], hbm, store_sem.at[i])
        for i, hbm in enumerate((q_hbm, k_hbm, v_hbm))
    ]
    stores += [pltpu.make_async_copy(adapter.at[i], adapter_hbm.at[i], store_sem.at[3 + i]) for i in range(2)]
    stores += [pltpu.make_async_copy(gi_hbm, input_hbm, store_sem.at[5])]
    stores[5].start()
    for i in range(3):
        loads[i].wait()
        wide[i] = unpadded([outs[i, 0], outs[i, 1]])
        stores[i].start()
    loads[3].wait()
    for i, head1 in ((1, value1), (0, query1)):
        loads[5 - i].wait()
        heads = []
        for pair in range(2):
            heads += [head0[pair, :, i], head1[pair]]
        heads = [head.reshape(RANK, PAD)[:, :HEAD].astype(F32) for head in heads]
        adapter[i] = jnp.concatenate(heads, axis=1)
        stores[3 + i].start()
    for store in stores:
        store.wait()


def body(
    query_base, key_base, value_base, adapter_activation, adapter_up_weight, output_grad,
    stretch_doc, doc_first, slot_stretch,
):
    n_tp = lax.axis_size("tp")
    side = math.isqrt(lax.axis_size("ctx") // 2)
    rows = RANK // side
    anywhere = pl.BlockSpec(memory_space=pltpu.HBM)
    smem = pl.BlockSpec(memory_space=pltpu.SMEM)

    def block(*shape, dtype=BF16):
        return pltpu.VMEM(shape, dtype)

    partial_results = pl.pallas_call(
        functools.partial(kernel, side, n_tp),
        out_shape=(
            jax.ShapeDtypeStruct((3, 2, ROWS, PAIR), BF16),
            jax.ShapeDtypeStruct((ROWS, RANK), BF16),
            jax.ShapeDtypeStruct((2, side, 2, rows, PAD), BF16),
            jax.ShapeDtypeStruct((2, side, rows, PAD), BF16),
            jax.ShapeDtypeStruct((2, side, rows, PAD), BF16),
        ),
        in_specs=[smem, smem] + [anywhere] * 6,
        out_specs=(anywhere,) * 5,
        scratch_shapes=[
            block(4, ROWS, COLUMNS),
            block(ROWS, RANK),
            block(2, RANK, COLUMNS),
            block(2, 2, RANK, PAIR),
            block(4, 2, ROWS, PAIR),
            block(4, ROWS, PAIR),
            block(ROWS, RANK),
            block(2, ROWS, RANK),
            block(WINDOW, RANK),
            block(2, ROWS, PAD),
            block(2, WINDOW, PAIR),
            block(2, GROUP_ROWS, PAIR),
            block(2, WINDOW, GROUP_ROWS, dtype=F32),
            block(2, WINDOW, GROUP_ROWS),
            block(2, SENT, PAIR),
            block(2, SENT, PAIR),
            block(2, GROUP_ROWS, PAIR, dtype=F32),
            block(2, GROUP_ROWS, PAIR),
            block(3, ROWS, PAIR),
            block(3, 2, ROWS, PAIR),
            block(ROWS, RANK, dtype=F32),
            block(ROWS, RANK, dtype=F32),
            block(n_tp, ROWS, RANK, dtype=F32),
            *((block(side, 2, rows, PAD), block(side, rows, PAD), block(side, rows, PAD)) * 3),
            block(2, side, 2, rows, PAD),
            block(2, side, rows, PAD),
            block(2, side, rows, PAD),
            block(ROWS, RANK),
            pltpu.SemaphoreType.DMA((6,)),
            pltpu.SemaphoreType.DMA((5,)),
            pltpu.SemaphoreType.DMA((COPIES,)),
            pltpu.SemaphoreType.DMA((COPIES,)),
            pltpu.SemaphoreType.REGULAR,
        ],
        compiler_params=pltpu.CompilerParams(
            collective_id=0, has_side_effects=True, vmem_limit_bytes=56 * 2**20
        ),
    )(
        slot_stretch, doc_first, query_base, key_base, value_base, adapter_activation,
        adapter_up_weight, output_grad,
    )
    return pl.pallas_call(
        finish,
        out_shape=(
            jax.ShapeDtypeStruct((ROWS, COLUMNS), BF16),
            jax.ShapeDtypeStruct((ROWS, COLUMNS), BF16),
            jax.ShapeDtypeStruct((ROWS, COLUMNS), BF16),
            jax.ShapeDtypeStruct((ROWS, RANK), BF16),
            jax.ShapeDtypeStruct((2, RANK, COLUMNS), F32),
        ),
        in_specs=[anywhere] * 5,
        out_specs=(anywhere,) * 5,
        scratch_shapes=[
            block(3, 2, ROWS, PAIR),
            block(2, side, 2, rows, PAD),
            block(2, side, rows, PAD),
            block(2, side, rows, PAD),
            block(3, ROWS, COLUMNS),
            block(2, RANK, COLUMNS, dtype=F32),
            pltpu.SemaphoreType.DMA((6,)),
            pltpu.SemaphoreType.DMA((6,)),
        ],
        compiler_params=pltpu.CompilerParams(vmem_limit_bytes=56 * 2**20),
    )(*partial_results)


def solution(mesh):
    return jax.shard_map(
        body,
        mesh=mesh,
        in_specs=(
            P("ctx", "tp"),
            P("ctx", "tp"),
            P("ctx", "tp"),
            P("ctx", None),
            P(None, None, "tp"),
            P("ctx", "tp"),
            P(),
            P(),
            P(),
        ),
        out_specs=(
            P("ctx", "tp"),
            P("ctx", "tp"),
            P("ctx", "tp"),
            P("ctx", None),
            P(None, None, "tp"),
        ),
        check_vma=False,
    )
```

```python
import functools
import math

import jax
import jax.numpy as jnp
from jax import lax
from jax.experimental import pallas as pl
from jax.experimental.pallas import tpu as pltpu
from jax.sharding import PartitionSpec as P

HEAD = 224
PAD = 256
HEADS = 4
PAIR = 2 * PAD
ROWS = 128
STRETCH = 64
GROUP_ROWS = 2 * ROWS
WINDOW = 2 * GROUP_ROWS
SENT = 3 * STRETCH
RANK = 128
COLUMNS = HEADS * HEAD
SCALE = HEAD ** -0.5
FILL = -1e30

KEY, VALUE, QUERY, GRAD = range(4)
S_KEY, S_VALUE, S_QUERY, S_GRAD, S_ACT = range(5)
S_OUT = 5
S_INPUT = 8
S_NEXT = 9
S_BACK = 13
S_PAST = 17
S_FIRST = 19
S_ADAPTER = 20
S_ALONG = 23
S_INPUTS = 32
COPIES = 33
UNIT_AXIS = (1, 1, 0)
MESH = pl.DeviceIdType.MESH
F32 = jnp.float32
BF16 = jnp.bfloat16


def dot(a, b, contract):
    return lax.dot_general(a, b, ((contract[:1], contract[1:]), ((), ())), preferred_element_type=F32)


def padded(values):
    rows = values.shape[0]
    blank = jnp.zeros((rows, PAD - HEAD), values.dtype)
    parts = []
    for head in range(HEADS):
        parts += [values[:, head * HEAD:(head + 1) * HEAD], blank]
    return jnp.concatenate(parts, axis=1)


def unpadded(pairs):
    return jnp.concatenate(
        [pair[:, head * PAD:head * PAD + HEAD] for pair in pairs for head in range(2)], axis=1
    )


def kernel(
    side, n_tp,
    slot_ref, first_ref, q_hbm, k_hbm, v_hbm, a_hbm, w_hbm, g_hbm,
    out_ref, gi_ref, ga0_ref, ga1_ref, ga2_ref,
    raw, act, weight, weight_pad, packed, sibling, act_sib, act_past, act_window, key_past,
    window_kv, sorted_qg, probs, probs_low, back_send, back_recv, own_kv,
    grads, sib_send, outs, gi_send, gi_sib, gi_along,
    part0, part1, part2, scattered0, scattered1, scattered2,
    crossed0, crossed1, crossed2, gathered0, gathered1, gathered2,
    load_sem, send_sem, recv_sem, entered_sem,
):
    part = (part0, part1, part2)
    scattered = (scattered0, scattered1, scattered2)
    crossed = (crossed0, crossed1, crossed2)
    gathered = (gathered0, gathered1, gathered2)
    me = lax.axis_index("ctx")
    tp = lax.axis_index("tp")
    core = lax.rem(me, 2)
    chip = lax.div(me, 2)
    y, z = lax.rem(chip, side), lax.div(chip, side)
    chips = side * side
    other = me + 1 - 2 * core
    after = lax.rem(chip + 1, chips) * 2 + core
    before = lax.rem(chip + chips - 1, chips) * 2 + core
    rows = RANK // side

    def along(axis, step):
        if axis == 0:
            return (z * side + lax.rem(y + step, side)) * 2 + core
        return (lax.rem(z + step, side) * side + y) * 2 + core

    def remote(src, dst, sem, ctx, x=None):
        return pltpu.make_async_remote_copy(
            src_ref=src, dst_ref=dst, send_sem=send_sem.at[sem], recv_sem=recv_sem.at[sem],
            device_id=(ctx, tp if x is None else x), device_id_type=MESH,
        )

    loads = [
        pltpu.make_async_copy(src, dst, load_sem.at[i])
        for i, (src, dst) in enumerate([
            (k_hbm, raw.at[KEY]), (a_hbm, act), (w_hbm, weight), (v_hbm, raw.at[VALUE]),
            (q_hbm, raw.at[QUERY]), (g_hbm, raw.at[GRAD]),
        ])
    ]
    loads[0].start()

    barrier = pltpu.get_barrier_semaphore()

    def greet(ctx, x):
        pl.semaphore_signal(barrier, inc=1, device_id=(ctx, x), device_id_type=MESH)

    steps = [side // 2 + (i // 2) * (1 - 2 * (i % 2)) for i in range(1, side)]
    near = [step for step in steps if min(step, side - step) <= 2]
    for step in near:
        greet(along(0, step), tp)
        greet(along(1, step), tp)
    for step in range(1, n_tp):
        greet(me, lax.rem(tp + step, n_tp))
    after_other = after + 1 - 2 * core
    before_other = before + 1 - 2 * core
    for device in (after, after_other, before, before_other, other):
        greet(device, tp)
    for load in loads[1:]:
        load.start()

    places = [
        slot_ref[2 * me] - 4 * chip, slot_ref[2 * me + 1] - 4 * chip,
        slot_ref[2 * other] - 4 * chip, slot_ref[2 * other + 1] - 4 * chip,
    ]
    past = lax.rem(chip + chips - 1, chips)
    past_places = [slot_ref[4 * past + j] - 4 * past for j in range(4)]

    def in_order(own, sib, places=places):
        slots = [own[:STRETCH], own[STRETCH:], sib[:STRETCH], sib[STRETCH:]]
        result = []
        for i in range(4):
            picked = slots[3]
            for j in (2, 1, 0):
                picked = jnp.where(places[j] == i, slots[j], picked)
            result.append(picked)
        return result

    def to_slots(values):
        result = []
        for j in range(4):
            picked = values[3 * STRETCH:]
            for i in (2, 1, 0):
                picked = jnp.where(places[j] == i, values[i * STRETCH:(i + 1) * STRETCH], picked)
            result.append(picked)
        return result

    def pack(kind, values):
        packed[kind, 0] = values[:, :PAIR]
        packed[kind, 1] = values[:, PAIR:]

    def to_sibling(kind, sem):
        return remote(packed.at[kind, 1 - core], sibling.at[kind], sem, other)

    loads[0].wait()
    pack(KEY, padded(raw[KEY]))
    loads[1].wait()
    pl.semaphore_wait(barrier, 5 + 2 * len(near) + n_tp - 1)
    sib_key = to_sibling(KEY, S_KEY)
    sib_key.start()
    sib_act = remote(act, act_sib, S_ACT, other)
    sib_act.start()
    first = pl.ds(0, PAD)
    next_first = [
        remote(packed.at[KEY, core, :, first], key_past.at[core], S_NEXT, after),
        remote(packed.at[KEY, 1 - core, :, first], key_past.at[core], S_FIRST, after_other),
    ]
    for copy in next_first:
        copy.start()
    next_act = remote(act, act_past.at[core], S_PAST, after)
    next_act.start()
    relays = [(axis, step) for axis in (0, 1) for step in (2, side - 2)] if len(near) < len(steps) else []
    for axis, step in relays:
        pl.semaphore_signal(entered_sem, inc=1, device_id=(along(axis, step), tp), device_id_type=MESH)
    loads[2].wait()
    for i in range(2):
        wide = padded(weight[i])
        weight_pad[i, 0] = wide[:, :PAIR]
        weight_pad[i, 1] = wide[:, PAIR:]

    def adapt(kind, i):
        wide = padded(raw[kind])
        for pair in range(2):
            update = dot(act[...], weight_pad[i, pair], (1, 0))
            base = wide[:, pair * PAIR:(pair + 1) * PAIR].astype(F32)
            packed[kind, pair] = (base + update).astype(BF16)

    loads[3].wait()
    adapt(VALUE, 1)
    sib_value = to_sibling(VALUE, S_VALUE)
    sib_value.start()

    def spread(kind):
        window_kv[kind, :STRETCH] = jnp.zeros((STRETCH, PAIR), BF16)
        for i, values in enumerate(in_order(packed[kind, core], sibling[kind])):
            window_kv[kind, GROUP_ROWS + i * STRETCH:GROUP_ROWS + (i + 1) * STRETCH] = values

    def to_next(kind, head):
        lanes = pl.ds(head * PAD, PAD)
        return remote(
            window_kv.at[kind, pl.ds(GROUP_ROWS + STRETCH, SENT), lanes],
            window_kv.at[kind, pl.ds(STRETCH, SENT), lanes], S_NEXT + 2 * head + kind, after,
        )

    next_kv = {}
    sib_key.wait_recv()
    spread(KEY)
    sib_value.wait_recv()
    spread(VALUE)
    for kind, head in ((VALUE, 0), (KEY, 1), (VALUE, 1)):
        next_kv[kind, head] = to_next(kind, head)
        next_kv[kind, head].start()

    loads[4].wait()
    adapt(QUERY, 0)
    sib_query = to_sibling(QUERY, S_QUERY)
    sib_query.start()
    loads[5].wait()
    pack(GRAD, padded(raw[GRAD]))
    sib_grad = to_sibling(GRAD, S_GRAD)
    sib_grad.start()

    sib_act.wait_recv()
    for i, values in enumerate(in_order(act[...], act_sib[...])):
        act_window[GROUP_ROWS + i * STRETCH:GROUP_ROWS + (i + 1) * STRETCH] = values
    for kind, copy in ((QUERY, sib_query), (GRAD, sib_grad)):
        copy.wait_recv()
        for i, values in enumerate(in_order(packed[kind, core], sibling[kind])):
            sorted_qg[kind - QUERY, i * STRETCH:(i + 1) * STRETCH] = values
    next_act.wait_recv()
    pass_act = remote(act_past.at[core], act_past.at[core], S_PAST + 1, other)
    pass_act.start()

    key_place = lax.broadcasted_iota(jnp.int32, (WINDOW, GROUP_ROWS), 0)
    query_place = lax.broadcasted_iota(jnp.int32, (1, GROUP_ROWS), 1)
    lowest = jnp.zeros((1, GROUP_ROWS), jnp.int32)
    for i in range(4):
        start = STRETCH * (first_ref[4 * chip + i] - 4 * chip + 4)
        lowest = jnp.where(query_place >= i * STRETCH, start, lowest)
    visible = (key_place >= lowest) & (key_place <= query_place + GROUP_ROWS)

    def position(unit, crossing):
        return (y, z)[UNIT_AXIS[unit] ^ crossing]

    def scatter(unit, step):
        target = lax.rem(position(unit, 0) + step, side)
        return remote(
            part[unit].at[target], scattered[unit].at[step], S_ALONG + 3 * unit, along(UNIT_AXIS[unit], step)
        )

    def cross(unit, step):
        block = crossed[unit].at[position(unit, 1)]
        return remote(block, block, S_ALONG + 3 * unit + 1, along(1 - UNIT_AXIS[unit], step))

    def gather(unit, step):
        block = gathered[unit].at[core, position(unit, 0)]
        return remote(block, block, S_ALONG + 3 * unit + 2, along(UNIT_AXIS[unit], step))

    def gather_other(unit, step):
        block = gathered[unit].at[core, position(unit, 0)]
        target = along(UNIT_AXIS[unit], step) + 1 - 2 * core
        return remote(block, block, S_ADAPTER + unit, target)

    def stage(unit, which):
        block = scattered[unit].at[pl.ds(1, side - 1)]
        return remote(block, block, S_ALONG + 3 * unit + which, other)

    def adapter_terms(block, activations, values):
        terms = dot(activations, values, (0, 0)).astype(BF16)
        for j in range(side):
            block(j)[...] = terms[j * rows:(j + 1) * rows]

    def send_unit(unit):
        for step in steps:
            scatter(unit, step).start()

    def back(kind, head):
        lanes = pl.ds(head * PAD, PAD)
        return remote(
            back_send.at[kind, :, lanes], back_recv.at[kind, :, lanes],
            S_BACK + 2 * head + kind, before,
        )

    backs = {}
    for head in range(2):
        lanes = slice(head * PAD, (head + 1) * PAD)
        if head:
            next_kv[KEY, head].wait_recv()
        else:
            for copy in next_first:
                copy.wait_recv()
            for i, values in enumerate(in_order(key_past[0], key_past[1], past_places)):
                if i:
                    window_kv[KEY, i * STRETCH:(i + 1) * STRETCH, lanes] = values
        scores = dot(window_kv[KEY, :, lanes], sorted_qg[0, :, lanes], (1, 1)) * SCALE
        scores = jnp.where(visible, scores, FILL)
        peak = jnp.max(scores, axis=0, keepdims=True)
        weights = jnp.exp(scores - peak)
        share = weights / jnp.sum(weights, axis=0, keepdims=True)
        probs[head] = share
        low = share.astype(BF16)
        probs_low[head] = low
        terms = dot(low, sorted_qg[1, :, lanes], (1, 0))
        own_kv[VALUE, :, lanes] = terms[GROUP_ROWS:]
        terms = terms.astype(BF16)
        back_send[VALUE, :, lanes] = terms[STRETCH:GROUP_ROWS]
        backs[VALUE, head] = back(VALUE, head)
        backs[VALUE, head].start()
        if not head:
            pass_act.wait_recv()
            act_window[:STRETCH] = jnp.zeros((STRETCH, RANK), BF16)
            for i, values in enumerate(in_order(act_past[0], act_past[1], past_places)):
                if i:
                    act_window[i * STRETCH:(i + 1) * STRETCH] = values
        if head:
            adapter_terms(lambda j: part[1].at[j], act_window[...], terms)
            send_unit(1)
        else:
            adapter_terms(lambda j: part[0].at[j, 1], act_window[...], terms)

        next_kv[VALUE, head].wait_recv()
        grad_probs = dot(window_kv[VALUE, :, lanes], sorted_qg[1, :, lanes], (1, 1))
        row_dot = jnp.sum(probs_low[head].astype(F32) * grad_probs, axis=0, keepdims=True)
        grad_scores = (probs[head] * (grad_probs - row_dot)).astype(BF16)
        summed = (dot(grad_scores, window_kv[KEY, :, lanes], (0, 0)) * SCALE).astype(BF16)
        grads[0, :, lanes] = summed
        if head:
            adapter_terms(lambda j: part[2].at[j], act_window[GROUP_ROWS:], summed)
            send_unit(2)
        else:
            adapter_terms(lambda j: part[0].at[j, 0], act_window[GROUP_ROWS:], summed)
            if relays:
                pl.semaphore_wait(entered_sem, len(relays))
            send_unit(0)
        terms = dot(grad_scores, sorted_qg[0, :, lanes], (1, 0)) * SCALE
        back_send[KEY, :, lanes] = terms[STRETCH:GROUP_ROWS].astype(BF16)
        own_kv[KEY, :, lanes] = terms[GROUP_ROWS:]
        backs[KEY, head] = back(KEY, head)
        backs[KEY, head].start()

    def input_terms(i, values):
        return dot(values, weight_pad[i, core], (1, 1))

    def hand_out(i, slots):
        outs[i, core, :STRETCH] = slots[0]
        outs[i, core, STRETCH:] = slots[1]
        sib_send[i, :STRETCH] = slots[2]
        sib_send[i, STRETCH:] = slots[3]
        copy = remote(sib_send.at[i], outs.at[i, core], S_OUT + i, other)
        copy.start()
        return copy

    def add_back(kind):
        mine = own_kv[kind]
        return jnp.concatenate(
            [mine[:STRETCH], mine[STRETCH:] + back_recv[kind].astype(F32)], axis=0
        ).astype(BF16)

    def go_across(unit):
        stage(unit, 0).wait_recv()
        total = part[unit][position(unit, 0)].astype(F32)
        for step in range(1, side):
            total = total + scattered[unit][step].astype(F32)
        crossed[unit][position(unit, 1)] = total.astype(BF16)
        for step in steps:
            cross(unit, step).start()

    def go_around(unit):
        stage(unit, 1).wait_recv()
        total = crossed[unit][0].astype(F32)
        for step in range(1, side):
            total = total + crossed[unit][step].astype(F32)
        gathered[unit][core, position(unit, 0)] = total.astype(BF16)
        for step in steps:
            gather(unit, step).start()
        if unit == 2:
            for step in steps + [0]:
                gather_other(unit, step).start()

    input_part = input_terms(0, grads[0])
    out_query = hand_out(0, to_slots(grads[0]))
    go_across(0)

    for head in range(2):
        backs[VALUE, head].wait_recv()
    grads[1] = add_back(VALUE)
    input_slots = to_slots(input_part + input_terms(1, grads[1]))
    gi_send[:STRETCH] = input_slots[2]
    gi_send[STRETCH:] = input_slots[3]
    sib_input = remote(gi_send, gi_sib, S_INPUT, other)
    sib_input.start()
    gi_along[tp, :STRETCH] = input_slots[0]
    gi_along[tp, STRETCH:] = input_slots[1]
    out_value = hand_out(2, to_slots(grads[1]))

    go_across(1)
    go_across(2)

    sib_input.wait_recv()
    gi_along[tp] = gi_along[tp] + gi_sib[...]

    for step in range(1, n_tp):
        block = gi_along.at[tp]
        remote(block, block, S_INPUTS, me, lax.rem(tp + step, n_tp)).start()
    block = gi_along.at[pl.ds(1, n_tp - 1)]
    tp_inputs = remote(block, block, S_INPUTS, other)
    for head in range(2):
        backs[KEY, head].wait_recv()
    out_key = hand_out(1, to_slots(add_back(KEY)))

    go_around(0)
    go_around(1)
    tp_inputs.wait_recv()
    total = gi_along[0]
    for x in range(1, n_tp):
        total = total + gi_along[x]
    gi_ref[...] = total.astype(BF16)
    go_around(2)

    for copy in (out_query, out_value, out_key):
        copy.wait_recv()
    out_ref[...] = outs[...]

    for copy in (
        sib_key, sib_act, sib_value, sib_query, sib_grad, *next_first, next_act, pass_act,
        *next_kv.values(), *backs.values(), out_query, out_value, out_key, sib_input,
    ):
        copy.wait_send()
    tp_inputs.wait_send()
    sib_adapter = []
    for unit in range(3):
        stage(unit, 0).wait_send()
        stage(unit, 1).wait_send()
    for unit in range(3):
        stage(unit, 2).wait_recv()
        block = gathered[unit].at[core]
        copy = remote(block, block, S_ADAPTER + unit, other)
        if unit < 2:
            copy.start()
        sib_adapter.append(copy)
        stage(unit, 2).wait_send()
    for unit, ref in enumerate((ga0_ref, ga1_ref, ga2_ref)):
        sib_adapter[unit].wait_recv()
        ref[...] = gathered[unit][...]
        sib_adapter[unit].wait_send()


def finish(
    out_ref, gi_ref, head0, value1, query1, q_hbm, k_hbm, v_hbm, input_hbm, adapter_hbm,
    wide, adapter, store_sem,
):
    stores = [
        pltpu.make_async_copy(source, hbm, store_sem.at[i])
        for i, (source, hbm) in enumerate((
            (wide.at[0], q_hbm), (wide.at[1], k_hbm), (wide.at[2], v_hbm),
            (adapter.at[0], adapter_hbm.at[0]), (adapter.at[1], adapter_hbm.at[1]), (gi_ref, input_hbm),
        ))
    ]
    stores[5].start()
    for i, head1 in ((1, value1), (0, query1)):
        heads = []
        for pair in range(2):
            heads += [head0[pair, :, i], head1[pair]]
        heads = [head.reshape(RANK, PAD)[:, :HEAD].astype(F32) for head in heads]
        adapter[i] = jnp.concatenate(heads, axis=1)
        stores[3 + i].start()
    for i in range(3):
        wide[i] = unpadded([out_ref[i, 0], out_ref[i, 1]])
        stores[i].start()
    for store in stores:
        store.wait()


def body(
    query_base, key_base, value_base, adapter_activation, adapter_up_weight, output_grad,
    stretch_doc, doc_first, slot_stretch,
):
    n_tp = lax.axis_size("tp")
    side = math.isqrt(lax.axis_size("ctx") // 2)
    rows = RANK // side
    anywhere = pl.BlockSpec(memory_space=pltpu.HBM)
    vmem = pl.BlockSpec(memory_space=pltpu.VMEM)
    smem = pl.BlockSpec(memory_space=pltpu.SMEM)

    def block(*shape, dtype=BF16):
        return pltpu.VMEM(shape, dtype)

    partial_results = pl.pallas_call(
        functools.partial(kernel, side, n_tp),
        out_shape=(
            pltpu.VMEM((3, 2, ROWS, PAIR), BF16),
            pltpu.VMEM((ROWS, RANK), BF16),
            pltpu.VMEM((2, side, 2, rows, PAD), BF16),
            pltpu.VMEM((2, side, rows, PAD), BF16),
            pltpu.VMEM((2, side, rows, PAD), BF16),
        ),
        in_specs=[smem, smem] + [anywhere] * 6,
        out_specs=(vmem,) * 5,
        scratch_shapes=[
            block(4, ROWS, COLUMNS),
            block(ROWS, RANK),
            block(2, RANK, COLUMNS),
            block(2, 2, RANK, PAIR),
            block(4, 2, ROWS, PAIR),
            block(4, ROWS, PAIR),
            block(ROWS, RANK),
            block(2, ROWS, RANK),
            block(WINDOW, RANK),
            block(2, ROWS, PAD),
            block(2, WINDOW, PAIR),
            block(2, GROUP_ROWS, PAIR),
            block(2, WINDOW, GROUP_ROWS, dtype=F32),
            block(2, WINDOW, GROUP_ROWS),
            block(2, SENT, PAIR),
            block(2, SENT, PAIR),
            block(2, GROUP_ROWS, PAIR, dtype=F32),
            block(2, GROUP_ROWS, PAIR),
            block(3, ROWS, PAIR),
            block(3, 2, ROWS, PAIR),
            block(ROWS, RANK, dtype=F32),
            block(ROWS, RANK, dtype=F32),
            block(n_tp, ROWS, RANK, dtype=F32),
            *((block(side, 2, rows, PAD), block(side, rows, PAD), block(side, rows, PAD)) * 3),
            block(2, side, 2, rows, PAD),
            block(2, side, rows, PAD),
            block(2, side, rows, PAD),
            pltpu.SemaphoreType.DMA((6,)),
            pltpu.SemaphoreType.DMA((COPIES,)),
            pltpu.SemaphoreType.DMA((COPIES,)),
            pltpu.SemaphoreType.REGULAR,
        ],
        compiler_params=pltpu.CompilerParams(
            collective_id=0, has_side_effects=True, vmem_limit_bytes=54 * 2**20
        ),
    )(
        slot_stretch, doc_first, query_base, key_base, value_base, adapter_activation,
        adapter_up_weight, output_grad,
    )
    return pl.pallas_call(
        finish,
        out_shape=(
            jax.ShapeDtypeStruct((ROWS, COLUMNS), BF16),
            jax.ShapeDtypeStruct((ROWS, COLUMNS), BF16),
            jax.ShapeDtypeStruct((ROWS, COLUMNS), BF16),
            jax.ShapeDtypeStruct((ROWS, RANK), BF16),
            jax.ShapeDtypeStruct((2, RANK, COLUMNS), F32),
        ),
        in_specs=[vmem] * 5,
        out_specs=(anywhere,) * 5,
        scratch_shapes=[
            block(3, ROWS, COLUMNS),
            block(2, RANK, COLUMNS, dtype=F32),
            pltpu.SemaphoreType.DMA((6,)),
        ],
        compiler_params=pltpu.CompilerParams(vmem_limit_bytes=32 * 2**20),
    )(*partial_results)


def solution(mesh):
    return jax.shard_map(
        body,
        mesh=mesh,
        in_specs=(
            P("ctx", "tp"),
            P("ctx", "tp"),
            P("ctx", "tp"),
            P("ctx", None),
            P(None, None, "tp"),
            P("ctx", "tp"),
            P(),
            P(),
            P(),
        ),
        out_specs=(
            P("ctx", "tp"),
            P("ctx", "tp"),
            P("ctx", "tp"),
            P("ctx", None),
            P(None, None, "tp"),
        ),
        check_vma=False,
    )
```

```python
import functools
import math

import jax
import jax.numpy as jnp
from jax import lax
from jax.experimental import pallas as pl
from jax.experimental.pallas import tpu as pltpu
from jax.sharding import PartitionSpec as P

HEAD = 224
PAD = 256
HEADS = 4
PAIR = 2 * PAD
ROWS = 128
STRETCH = 64
GROUP_ROWS = 2 * ROWS
WINDOW = 2 * GROUP_ROWS
SENT = 3 * STRETCH
RANK = 128
COLUMNS = HEADS * HEAD
SCALE = HEAD ** -0.5
FILL = -1e30

KEY, VALUE, QUERY, GRAD = range(4)
S_KEY, S_VALUE, S_QUERY, S_GRAD, S_ACT = range(5)
S_OUT = 5
S_INPUT = 8
S_NEXT = 9
S_BACK = 13
S_PAST = 17
S_FIRST = 19
S_ADAPTER = 20
S_ALONG = 23
S_INPUTS = 32
S_PARTS = 33
COPIES = 34
UNIT_AXIS = (1, 1, 0)
MESH = pl.DeviceIdType.MESH
F32 = jnp.float32
BF16 = jnp.bfloat16


def dot(a, b, contract):
    return lax.dot_general(a, b, ((contract[:1], contract[1:]), ((), ())), preferred_element_type=F32)


def padded(values):
    rows = values.shape[0]
    blank = jnp.zeros((rows, PAD - HEAD), values.dtype)
    parts = []
    for head in range(HEADS):
        parts += [values[:, head * HEAD:(head + 1) * HEAD], blank]
    return jnp.concatenate(parts, axis=1)


def unpadded(pairs):
    return jnp.concatenate(
        [pair[:, head * PAD:head * PAD + HEAD] for pair in pairs for head in range(2)], axis=1
    )


def kernel(
    side, n_tp,
    slot_hbm, first_hbm, q_hbm, k_hbm, v_hbm, a_hbm, w_hbm, g_hbm,
    out_ref, gi_ref, ga0_ref, ga1_ref, ga2_ref,
    raw, act, weight, weight_pad, packed, sibling, act_sib, act_past, act_window, key_past,
    window_kv, sorted_qg, probs, probs_low, back_send, back_recv, own_kv,
    grads, sib_send, outs, gi_send, gi_sib, gi_along,
    part0, part1, part2, scattered0, scattered1, scattered2,
    crossed0, crossed1, crossed2, gathered0, gathered1, gathered2,
    slot_ref, first_ref, load_sem, send_sem, recv_sem, entered_sem,
):
    part = (part0, part1, part2)
    scattered = (scattered0, scattered1, scattered2)
    crossed = (crossed0, crossed1, crossed2)
    gathered = (gathered0, gathered1, gathered2)
    me = lax.axis_index("ctx")
    tp = lax.axis_index("tp")
    core = lax.rem(me, 2)
    chip = lax.div(me, 2)
    y, z = lax.rem(chip, side), lax.div(chip, side)
    chips = side * side
    other = me + 1 - 2 * core
    after = lax.rem(chip + 1, chips) * 2 + core
    before = lax.rem(chip + chips - 1, chips) * 2 + core
    rows = RANK // side

    def along(axis, step):
        if axis == 0:
            return (z * side + lax.rem(y + step, side)) * 2 + core
        return (lax.rem(z + step, side) * side + y) * 2 + core

    def remote(src, dst, sem, ctx, x=None):
        return pltpu.make_async_remote_copy(
            src_ref=src, dst_ref=dst, send_sem=send_sem.at[sem], recv_sem=recv_sem.at[sem],
            device_id=(ctx, tp if x is None else x), device_id_type=MESH,
        )

    loads = [
        pltpu.make_async_copy(src, dst, load_sem.at[i])
        for i, (src, dst) in enumerate([
            (k_hbm, raw.at[KEY]), (a_hbm, act), (w_hbm, weight), (v_hbm, raw.at[VALUE]),
            (q_hbm, raw.at[QUERY]), (g_hbm, raw.at[GRAD]), (slot_hbm, slot_ref), (first_hbm, first_ref),
        ])
    ]
    loads[0].start()

    barrier = pltpu.get_barrier_semaphore()

    def greet(ctx, x):
        pl.semaphore_signal(barrier, inc=1, device_id=(ctx, x), device_id_type=MESH)

    steps = [side // 2 + (i // 2) * (1 - 2 * (i % 2)) for i in range(1, side)]
    near = [step for step in steps if min(step, side - step) <= 2]
    for step in near:
        greet(along(0, step), tp)
        greet(along(1, step), tp)
    for step in range(1, n_tp):
        greet(me, lax.rem(tp + step, n_tp))
    after_other = after + 1 - 2 * core
    before_other = before + 1 - 2 * core
    for device in (after, after_other, before, before_other, other):
        greet(device, tp)
    for load in loads[1:]:
        load.start()

    def pack(kind, values):
        packed[kind, 0] = values[:, :PAIR]
        packed[kind, 1] = values[:, PAIR:]

    def to_sibling(kind, sem):
        return remote(packed.at[kind, 1 - core], sibling.at[kind], sem, other)

    loads[0].wait()
    pack(KEY, padded(raw[KEY]))
    loads[1].wait()
    pl.semaphore_wait(barrier, 5 + 2 * len(near) + n_tp - 1)
    sib_key = to_sibling(KEY, S_KEY)
    sib_key.start()
    sib_act = remote(act, act_sib, S_ACT, other)
    sib_act.start()
    share_rows = pl.ds(pl.multiple_of(tp * (ROWS // n_tp), ROWS // n_tp), ROWS // n_tp)
    next_act = remote(act.at[share_rows], act_past.at[core, share_rows], S_PAST, after)
    next_act.start()
    first = pl.ds(0, PAD)
    next_first = [
        remote(packed.at[KEY, core, :, first], key_past.at[core], S_NEXT, after),
        remote(packed.at[KEY, 1 - core, :, first], key_past.at[core], S_FIRST, after_other),
    ]
    for copy in next_first:
        copy.start()
    relays = [(axis, step) for axis in (0, 1) for step in (2, side - 2)] if len(near) < len(steps) else []
    for axis, step in relays:
        pl.semaphore_signal(entered_sem, inc=1, device_id=(along(axis, step), tp), device_id_type=MESH)
    loads[2].wait()

    def adapt(kind, i):
        wide = padded(weight[i])
        weight_pad[i, 0] = wide[:, :PAIR]
        weight_pad[i, 1] = wide[:, PAIR:]
        wide = padded(raw[kind])
        for pair in range(2):
            update = dot(act[...], weight_pad[i, pair], (1, 0))
            base = wide[:, pair * PAIR:(pair + 1) * PAIR].astype(F32)
            packed[kind, pair] = (base + update).astype(BF16)

    loads[3].wait()
    adapt(VALUE, 1)
    sib_value = to_sibling(VALUE, S_VALUE)
    sib_value.start()

    loads[6].wait()
    loads[7].wait()
    places = [
        slot_ref[2 * me] - 4 * chip, slot_ref[2 * me + 1] - 4 * chip,
        slot_ref[2 * other] - 4 * chip, slot_ref[2 * other + 1] - 4 * chip,
    ]
    past = lax.rem(chip + chips - 1, chips)
    past_places = [slot_ref[4 * past + j] - 4 * past for j in range(4)]

    def in_order(own, sib, places=places):
        slots = [own[:STRETCH], own[STRETCH:], sib[:STRETCH], sib[STRETCH:]]
        result = []
        for i in range(4):
            picked = slots[3]
            for j in (2, 1, 0):
                picked = jnp.where(places[j] == i, slots[j], picked)
            result.append(picked)
        return result

    def to_slots(values):
        result = []
        for j in range(4):
            picked = values[3 * STRETCH:]
            for i in (2, 1, 0):
                picked = jnp.where(places[j] == i, values[i * STRETCH:(i + 1) * STRETCH], picked)
            result.append(picked)
        return result

    def spread(kind):
        window_kv[kind, :STRETCH] = jnp.zeros((STRETCH, PAIR), BF16)
        for i, values in enumerate(in_order(packed[kind, core], sibling[kind])):
            window_kv[kind, GROUP_ROWS + i * STRETCH:GROUP_ROWS + (i + 1) * STRETCH] = values

    def to_next(kind, head):
        lanes = pl.ds(head * PAD, PAD)
        return remote(
            window_kv.at[kind, pl.ds(GROUP_ROWS + STRETCH, SENT), lanes],
            window_kv.at[kind, pl.ds(STRETCH, SENT), lanes], S_NEXT + 2 * head + kind, after,
        )

    next_kv = {}
    sib_key.wait_recv()
    spread(KEY)
    sib_value.wait_recv()
    spread(VALUE)
    for kind, head in ((VALUE, 0), (KEY, 1), (VALUE, 1)):
        next_kv[kind, head] = to_next(kind, head)
        next_kv[kind, head].start()

    loads[4].wait()
    adapt(QUERY, 0)
    sib_query = to_sibling(QUERY, S_QUERY)
    sib_query.start()
    loads[5].wait()
    pack(GRAD, padded(raw[GRAD]))
    sib_grad = to_sibling(GRAD, S_GRAD)
    sib_grad.start()

    next_act.wait_recv()
    block = act_past.at[core, share_rows]
    for step in range(1, n_tp):
        remote(block, block, S_PARTS, me, lax.rem(tp + step, n_tp)).start()
    block = act_past.at[core, pl.ds(0, ROWS - ROWS // n_tp)]
    tp_acts = remote(block, block, S_PARTS, other)
    pass_act = remote(act_past.at[core], act_past.at[core], S_PAST + 1, other)
    sib_act.wait_recv()
    for i, values in enumerate(in_order(act[...], act_sib[...])):
        act_window[GROUP_ROWS + i * STRETCH:GROUP_ROWS + (i + 1) * STRETCH] = values
    for kind, copy in ((QUERY, sib_query), (GRAD, sib_grad)):
        copy.wait_recv()
        for i, values in enumerate(in_order(packed[kind, core], sibling[kind])):
            sorted_qg[kind - QUERY, i * STRETCH:(i + 1) * STRETCH] = values

    key_place = lax.broadcasted_iota(jnp.int32, (WINDOW, GROUP_ROWS), 0)
    query_place = lax.broadcasted_iota(jnp.int32, (1, GROUP_ROWS), 1)
    lowest = jnp.zeros((1, GROUP_ROWS), jnp.int32)
    for i in range(4):
        start = STRETCH * (first_ref[4 * chip + i] - 4 * chip + 4)
        lowest = jnp.where(query_place >= i * STRETCH, start, lowest)
    visible = (key_place >= lowest) & (key_place <= query_place + GROUP_ROWS)

    def position(unit, crossing):
        return (y, z)[UNIT_AXIS[unit] ^ crossing]

    def scatter(unit, step):
        target = lax.rem(position(unit, 0) + step, side)
        return remote(
            part[unit].at[target], scattered[unit].at[step], S_ALONG + 3 * unit, along(UNIT_AXIS[unit], step)
        )

    def cross(unit, step):
        block = crossed[unit].at[position(unit, 1)]
        return remote(block, block, S_ALONG + 3 * unit + 1, along(1 - UNIT_AXIS[unit], step))

    def gather(unit, step):
        block = gathered[unit].at[core, position(unit, 0)]
        return remote(block, block, S_ALONG + 3 * unit + 2, along(UNIT_AXIS[unit], step))

    def gather_other(unit, step):
        block = gathered[unit].at[core, position(unit, 0)]
        target = along(UNIT_AXIS[unit], step) + 1 - 2 * core
        return remote(block, block, S_ADAPTER + unit, target)

    def stage(unit, which):
        block = scattered[unit].at[pl.ds(1, side - 1)]
        return remote(block, block, S_ALONG + 3 * unit + which, other)

    def adapter_terms(block, activations, values):
        terms = dot(activations, values, (0, 0)).astype(BF16)
        for j in range(side):
            block(j)[...] = terms[j * rows:(j + 1) * rows]

    def send_unit(unit):
        for step in steps:
            scatter(unit, step).start()

    def back(kind, head):
        lanes = pl.ds(head * PAD, PAD)
        return remote(
            back_send.at[kind, :, lanes], back_recv.at[kind, :, lanes],
            S_BACK + 2 * head + kind, before,
        )

    backs = {}
    for head in range(2):
        lanes = slice(head * PAD, (head + 1) * PAD)
        if head:
            next_kv[KEY, head].wait_recv()
        else:
            for copy in next_first:
                copy.wait_recv()
            for i, values in enumerate(in_order(key_past[0], key_past[1], past_places)):
                if i:
                    window_kv[KEY, i * STRETCH:(i + 1) * STRETCH, lanes] = values
        scores = dot(window_kv[KEY, :, lanes], sorted_qg[0, :, lanes], (1, 1)) * SCALE
        scores = jnp.where(visible, scores, FILL)
        peak = jnp.max(scores, axis=0, keepdims=True)
        weights = jnp.exp(scores - peak)
        share = weights / jnp.sum(weights, axis=0, keepdims=True)
        probs[head] = share
        low = share.astype(BF16)
        probs_low[head] = low
        terms = dot(low, sorted_qg[1, :, lanes], (1, 0))
        own_kv[VALUE, :, lanes] = terms[GROUP_ROWS:]
        terms = terms.astype(BF16)
        back_send[VALUE, :, lanes] = terms[STRETCH:GROUP_ROWS]
        backs[VALUE, head] = back(VALUE, head)
        backs[VALUE, head].start()
        if head:
            adapter_terms(lambda j: part[1].at[j], act_window[...], terms)
            send_unit(1)
        else:
            first_terms = terms
            tp_acts.wait_recv()
            pass_act.start()

        next_kv[VALUE, head].wait_recv()
        grad_probs = dot(window_kv[VALUE, :, lanes], sorted_qg[1, :, lanes], (1, 1))
        row_dot = jnp.sum(probs_low[head].astype(F32) * grad_probs, axis=0, keepdims=True)
        grad_scores = (probs[head] * (grad_probs - row_dot)).astype(BF16)
        summed = (dot(grad_scores, window_kv[KEY, :, lanes], (0, 0)) * SCALE).astype(BF16)
        grads[0, :, lanes] = summed
        if head:
            adapter_terms(lambda j: part[2].at[j], act_window[GROUP_ROWS:], summed)
            send_unit(2)
        else:
            adapter_terms(lambda j: part[0].at[j, 0], act_window[GROUP_ROWS:], summed)
            pass_act.wait_recv()
            act_window[:STRETCH] = jnp.zeros((STRETCH, RANK), BF16)
            for i, values in enumerate(in_order(act_past[0], act_past[1], past_places)):
                if i:
                    act_window[i * STRETCH:(i + 1) * STRETCH] = values
            adapter_terms(lambda j: part[0].at[j, 1], act_window[...], first_terms)
            if relays:
                pl.semaphore_wait(entered_sem, len(relays))
            send_unit(0)
        terms = dot(grad_scores, sorted_qg[0, :, lanes], (1, 0)) * SCALE
        back_send[KEY, :, lanes] = terms[STRETCH:GROUP_ROWS].astype(BF16)
        own_kv[KEY, :, lanes] = terms[GROUP_ROWS:]
        backs[KEY, head] = back(KEY, head)
        backs[KEY, head].start()

    def input_terms(i, values):
        return dot(values, weight_pad[i, core], (1, 1))

    def hand_out(i, slots):
        outs[i, core, :STRETCH] = slots[0]
        outs[i, core, STRETCH:] = slots[1]
        sib_send[i, :STRETCH] = slots[2]
        sib_send[i, STRETCH:] = slots[3]
        copy = remote(sib_send.at[i], outs.at[i, core], S_OUT + i, other)
        copy.start()
        return copy

    def add_back(kind):
        mine = own_kv[kind]
        return jnp.concatenate(
            [mine[:STRETCH], mine[STRETCH:] + back_recv[kind].astype(F32)], axis=0
        ).astype(BF16)

    def go_across(unit):
        stage(unit, 0).wait_recv()
        total = part[unit][position(unit, 0)].astype(F32)
        for step in range(1, side):
            total = total + scattered[unit][step].astype(F32)
        crossed[unit][position(unit, 1)] = total.astype(BF16)
        for step in steps:
            cross(unit, step).start()

    def go_around(unit):
        stage(unit, 1).wait_recv()
        total = crossed[unit][0].astype(F32)
        for step in range(1, side):
            total = total + crossed[unit][step].astype(F32)
        gathered[unit][core, position(unit, 0)] = total.astype(BF16)
        for step in steps:
            gather(unit, step).start()
        if unit == 2:
            for step in steps + [0]:
                gather_other(unit, step).start()

    input_part = input_terms(0, grads[0])
    out_query = hand_out(0, to_slots(grads[0]))
    go_across(0)

    for head in range(2):
        backs[VALUE, head].wait_recv()
    grads[1] = add_back(VALUE)
    input_slots = to_slots(input_part + input_terms(1, grads[1]))
    gi_send[:STRETCH] = input_slots[2]
    gi_send[STRETCH:] = input_slots[3]
    sib_input = remote(gi_send, gi_sib, S_INPUT, other)
    sib_input.start()
    gi_along[tp, :STRETCH] = input_slots[0]
    gi_along[tp, STRETCH:] = input_slots[1]
    out_value = hand_out(2, to_slots(grads[1]))

    go_across(1)
    go_across(2)

    sib_input.wait_recv()
    gi_along[tp] = gi_along[tp] + gi_sib[...]

    for step in range(1, n_tp):
        block = gi_along.at[tp]
        remote(block, block, S_INPUTS, me, lax.rem(tp + step, n_tp)).start()
    block = gi_along.at[pl.ds(1, n_tp - 1)]
    tp_inputs = remote(block, block, S_INPUTS, other)
    for head in range(2):
        backs[KEY, head].wait_recv()
    out_key = hand_out(1, to_slots(add_back(KEY)))

    go_around(0)
    go_around(1)
    tp_inputs.wait_recv()
    total = gi_along[0]
    for x in range(1, n_tp):
        total = total + gi_along[x]
    gi_ref[...] = total.astype(BF16)
    go_around(2)

    for copy in (out_query, out_value, out_key):
        copy.wait_recv()
    out_ref[...] = outs[...]

    for copy in (
        sib_key, sib_act, sib_value, sib_query, sib_grad, *next_first, next_act, tp_acts, pass_act,
        *next_kv.values(), *backs.values(), out_query, out_value, out_key, sib_input,
    ):
        copy.wait_send()
    tp_inputs.wait_send()
    sib_adapter = []
    for unit in range(3):
        stage(unit, 0).wait_send()
        stage(unit, 1).wait_send()
    for unit in range(3):
        stage(unit, 2).wait_recv()
        block = gathered[unit].at[core]
        copy = remote(block, block, S_ADAPTER + unit, other)
        if unit < 2:
            copy.start()
        sib_adapter.append(copy)
        stage(unit, 2).wait_send()
    for unit, ref in enumerate((ga0_ref, ga1_ref, ga2_ref)):
        sib_adapter[unit].wait_recv()
        ref[...] = gathered[unit][...]
        sib_adapter[unit].wait_send()


def finish(
    out_ref, gi_ref, head0, value1, query1, q_hbm, k_hbm, v_hbm, input_hbm, adapter_hbm,
    wide, adapter, store_sem,
):
    stores = [
        pltpu.make_async_copy(source, hbm, store_sem.at[i])
        for i, (source, hbm) in enumerate((
            (wide.at[0], q_hbm), (wide.at[1], k_hbm), (wide.at[2], v_hbm),
            (adapter.at[0], adapter_hbm.at[0]), (adapter.at[1], adapter_hbm.at[1]), (gi_ref, input_hbm),
        ))
    ]
    stores[5].start()
    for i, head1 in ((1, value1), (0, query1)):
        heads = []
        for pair in range(2):
            heads += [head0[pair, :, i], head1[pair]]
        heads = [head.reshape(RANK, PAD)[:, :HEAD].astype(F32) for head in heads]
        adapter[i] = jnp.concatenate(heads, axis=1)
        stores[3 + i].start()
    for i in range(3):
        wide[i] = unpadded([out_ref[i, 0], out_ref[i, 1]])
        stores[i].start()
    for store in stores:
        store.wait()


def body(
    query_base, key_base, value_base, adapter_activation, adapter_up_weight, output_grad,
    stretch_doc, doc_first, slot_stretch,
):
    n_tp = lax.axis_size("tp")
    side = math.isqrt(lax.axis_size("ctx") // 2)
    rows = RANK // side
    stretches = slot_stretch.shape[0]
    anywhere = pl.BlockSpec(memory_space=pltpu.HBM)
    vmem = pl.BlockSpec(memory_space=pltpu.VMEM)

    def block(*shape, dtype=BF16):
        return pltpu.VMEM(shape, dtype)

    partial_results = pl.pallas_call(
        functools.partial(kernel, side, n_tp),
        out_shape=(
            pltpu.VMEM((3, 2, ROWS, PAIR), BF16),
            pltpu.VMEM((ROWS, RANK), BF16),
            pltpu.VMEM((2, side, 2, rows, PAD), BF16),
            pltpu.VMEM((2, side, rows, PAD), BF16),
            pltpu.VMEM((2, side, rows, PAD), BF16),
        ),
        in_specs=[anywhere] * 8,
        out_specs=(vmem,) * 5,
        scratch_shapes=[
            block(4, ROWS, COLUMNS),
            block(ROWS, RANK),
            block(2, RANK, COLUMNS),
            block(2, 2, RANK, PAIR),
            block(4, 2, ROWS, PAIR),
            block(4, ROWS, PAIR),
            block(ROWS, RANK),
            block(2, ROWS, RANK),
            block(WINDOW, RANK),
            block(2, ROWS, PAD),
            block(2, WINDOW, PAIR),
            block(2, GROUP_ROWS, PAIR),
            block(2, WINDOW, GROUP_ROWS, dtype=F32),
            block(2, WINDOW, GROUP_ROWS),
            block(2, SENT, PAIR),
            block(2, SENT, PAIR),
            block(2, GROUP_ROWS, PAIR, dtype=F32),
            block(2, GROUP_ROWS, PAIR),
            block(3, ROWS, PAIR),
            block(3, 2, ROWS, PAIR),
            block(ROWS, RANK, dtype=F32),
            block(ROWS, RANK, dtype=F32),
            block(n_tp, ROWS, RANK, dtype=F32),
            *((block(side, 2, rows, PAD), block(side, rows, PAD), block(side, rows, PAD)) * 3),
            block(2, side, 2, rows, PAD),
            block(2, side, rows, PAD),
            block(2, side, rows, PAD),
            pltpu.SMEM((stretches,), jnp.int32),
            pltpu.SMEM((stretches,), jnp.int32),
            pltpu.SemaphoreType.DMA((8,)),
            pltpu.SemaphoreType.DMA((COPIES,)),
            pltpu.SemaphoreType.DMA((COPIES,)),
            pltpu.SemaphoreType.REGULAR,
        ],
        compiler_params=pltpu.CompilerParams(
            collective_id=0, has_side_effects=True, vmem_limit_bytes=54 * 2**20
        ),
    )(
        slot_stretch, doc_first, query_base, key_base, value_base, adapter_activation,
        adapter_up_weight, output_grad,
    )
    return pl.pallas_call(
        finish,
        out_shape=(
            jax.ShapeDtypeStruct((ROWS, COLUMNS), BF16),
            jax.ShapeDtypeStruct((ROWS, COLUMNS), BF16),
            jax.ShapeDtypeStruct((ROWS, COLUMNS), BF16),
            jax.ShapeDtypeStruct((ROWS, RANK), BF16),
            jax.ShapeDtypeStruct((2, RANK, COLUMNS), F32),
        ),
        in_specs=[vmem] * 5,
        out_specs=(anywhere,) * 5,
        scratch_shapes=[
            block(3, ROWS, COLUMNS),
            block(2, RANK, COLUMNS, dtype=F32),
            pltpu.SemaphoreType.DMA((6,)),
        ],
        compiler_params=pltpu.CompilerParams(vmem_limit_bytes=32 * 2**20),
    )(*partial_results)


def solution(mesh):
    return jax.shard_map(
        body,
        mesh=mesh,
        in_specs=(
            P("ctx", "tp"),
            P("ctx", "tp"),
            P("ctx", "tp"),
            P("ctx", None),
            P(None, None, "tp"),
            P("ctx", "tp"),
            P(),
            P(),
            P(),
        ),
        out_specs=(
            P("ctx", "tp"),
            P("ctx", "tp"),
            P("ctx", "tp"),
            P("ctx", None),
            P(None, None, "tp"),
        ),
        check_vma=False,
    )
```

```python
import functools
import math

import jax
import jax.numpy as jnp
from jax import lax
from jax.experimental import pallas as pl
from jax.experimental.pallas import tpu as pltpu
from jax.sharding import PartitionSpec as P

HEAD = 224
PAD = 256
HEADS = 4
PAIR = 2 * PAD
ROWS = 128
STRETCH = 64
GROUP_ROWS = 2 * ROWS
WINDOW = 2 * GROUP_ROWS
SENT = 3 * STRETCH
RANK = 128
COLUMNS = HEADS * HEAD
SCALE = HEAD ** -0.5
FILL = -1e30

KEY, VALUE, QUERY, GRAD = range(4)
S_KEY, S_VALUE, S_QUERY, S_GRAD, S_ACT = range(5)
S_OUT = 5
S_INPUT = 8
S_NEXT = 9
S_BACK = 13
S_PAST = 17
S_FIRST = 19
S_ADAPTER = 20
S_ALONG = 24
S_INPUTS = 36
S_PARTS = 37
COPIES = 38
UNITS = 4
MESH = pl.DeviceIdType.MESH
F32 = jnp.float32
BF16 = jnp.bfloat16


def dot(a, b, contract):
    return lax.dot_general(a, b, ((contract[:1], contract[1:]), ((), ())), preferred_element_type=F32)


def padded(values):
    rows = values.shape[0]
    blank = jnp.zeros((rows, PAD - HEAD), values.dtype)
    parts = []
    for head in range(HEADS):
        parts += [values[:, head * HEAD:(head + 1) * HEAD], blank]
    return jnp.concatenate(parts, axis=1)


def unpadded(pairs):
    return jnp.concatenate(
        [pair[:, head * PAD:head * PAD + HEAD] for pair in pairs for head in range(2)], axis=1
    )


def kernel(
    side, n_tp,
    slot_hbm, first_hbm, q_hbm, k_hbm, v_hbm, a_hbm, w_hbm, g_hbm,
    out_ref, gi_ref, ga_ref,
    raw, act, weight, weight_pad, packed, sibling, act_sib, act_past, act_window, key_past,
    window_kv, sorted_qg, probs, probs_low, back_send, back_recv, own_kv,
    grads, sib_send, outs, gi_send, gi_sib, gi_along,
    part, scattered, crossed, gathered,
    slot_ref, first_ref, load_sem, send_sem, recv_sem, entered_sem,
):
    me = lax.axis_index("ctx")
    tp = lax.axis_index("tp")
    core = lax.rem(me, 2)
    chip = lax.div(me, 2)
    y, z = lax.rem(chip, side), lax.div(chip, side)
    chips = side * side
    other = me + 1 - 2 * core
    after = lax.rem(chip + 1, chips) * 2 + core
    before = lax.rem(chip + chips - 1, chips) * 2 + core
    rows = RANK // side

    def along(axis, step):
        if axis == 0:
            return (z * side + lax.rem(y + step, side)) * 2 + core
        return (lax.rem(z + step, side) * side + y) * 2 + core

    def remote(src, dst, sem, ctx, x=None):
        return pltpu.make_async_remote_copy(
            src_ref=src, dst_ref=dst, send_sem=send_sem.at[sem], recv_sem=recv_sem.at[sem],
            device_id=(ctx, tp if x is None else x), device_id_type=MESH,
        )

    loads = [
        pltpu.make_async_copy(src, dst, load_sem.at[i])
        for i, (src, dst) in enumerate([
            (k_hbm, raw.at[KEY]), (a_hbm, act), (w_hbm, weight), (v_hbm, raw.at[VALUE]),
            (q_hbm, raw.at[QUERY]), (g_hbm, raw.at[GRAD]), (slot_hbm, slot_ref), (first_hbm, first_ref),
        ])
    ]
    loads[0].start()

    barrier = pltpu.get_barrier_semaphore()

    def greet(ctx, x):
        pl.semaphore_signal(barrier, inc=1, device_id=(ctx, x), device_id_type=MESH)

    steps = [side // 2 + (i // 2) * (1 - 2 * (i % 2)) for i in range(1, side)]
    near = [step for step in steps if min(step, side - step) <= 2]
    for step in near:
        greet(along(0, step), tp)
        greet(along(1, step), tp)
    for step in range(1, n_tp):
        greet(me, lax.rem(tp + step, n_tp))
    after_other = after + 1 - 2 * core
    before_other = before + 1 - 2 * core
    for device in (after, after_other, before, before_other, other):
        greet(device, tp)
    for load in loads[1:]:
        load.start()

    def pack(kind, values):
        packed[kind, 0] = values[:, :PAIR]
        packed[kind, 1] = values[:, PAIR:]

    def to_sibling(kind, sem):
        return remote(packed.at[kind, 1 - core], sibling.at[kind], sem, other)

    loads[0].wait()
    pack(KEY, padded(raw[KEY]))
    loads[1].wait()
    pl.semaphore_wait(barrier, 5 + 2 * len(near) + n_tp - 1)
    sib_key = to_sibling(KEY, S_KEY)
    sib_key.start()
    sib_act = remote(act, act_sib, S_ACT, other)
    sib_act.start()
    share_rows = pl.ds(pl.multiple_of(tp * (ROWS // n_tp), ROWS // n_tp), ROWS // n_tp)
    next_act = remote(act.at[share_rows], act_past.at[core, share_rows], S_PAST, after)
    next_act.start()
    first = pl.ds(0, PAD)
    next_first = [
        remote(packed.at[KEY, core, :, first], key_past.at[core], S_NEXT, after),
        remote(packed.at[KEY, 1 - core, :, first], key_past.at[core], S_FIRST, after_other),
    ]
    for copy in next_first:
        copy.start()
    relays = [(axis, step) for axis in (0, 1) for step in (2, side - 2)] if len(near) < len(steps) else []
    for axis, step in relays:
        pl.semaphore_signal(entered_sem, inc=1, device_id=(along(axis, step), tp), device_id_type=MESH)
    loads[2].wait()

    def adapt(kind, i):
        wide = padded(weight[i])
        weight_pad[i, 0] = wide[:, :PAIR]
        weight_pad[i, 1] = wide[:, PAIR:]
        wide = padded(raw[kind])
        for pair in range(2):
            update = dot(act[...], weight_pad[i, pair], (1, 0))
            base = wide[:, pair * PAIR:(pair + 1) * PAIR].astype(F32)
            packed[kind, pair] = (base + update).astype(BF16)

    loads[3].wait()
    adapt(VALUE, 1)
    sib_value = to_sibling(VALUE, S_VALUE)
    sib_value.start()

    loads[6].wait()
    loads[7].wait()
    places = [
        slot_ref[2 * me] - 4 * chip, slot_ref[2 * me + 1] - 4 * chip,
        slot_ref[2 * other] - 4 * chip, slot_ref[2 * other + 1] - 4 * chip,
    ]
    past = lax.rem(chip + chips - 1, chips)
    past_places = [slot_ref[4 * past + j] - 4 * past for j in range(4)]

    def in_order(own, sib, places=places):
        slots = [own[:STRETCH], own[STRETCH:], sib[:STRETCH], sib[STRETCH:]]
        result = []
        for i in range(4):
            picked = slots[3]
            for j in (2, 1, 0):
                picked = jnp.where(places[j] == i, slots[j], picked)
            result.append(picked)
        return result

    def to_slots(values):
        result = []
        for j in range(4):
            picked = values[3 * STRETCH:]
            for i in (2, 1, 0):
                picked = jnp.where(places[j] == i, values[i * STRETCH:(i + 1) * STRETCH], picked)
            result.append(picked)
        return result

    def spread(kind):
        window_kv[kind, :STRETCH] = jnp.zeros((STRETCH, PAIR), BF16)
        for i, values in enumerate(in_order(packed[kind, core], sibling[kind])):
            window_kv[kind, GROUP_ROWS + i * STRETCH:GROUP_ROWS + (i + 1) * STRETCH] = values

    def to_next(kind, head):
        lanes = pl.ds(head * PAD, PAD)
        return remote(
            window_kv.at[kind, pl.ds(GROUP_ROWS + STRETCH, SENT), lanes],
            window_kv.at[kind, pl.ds(STRETCH, SENT), lanes], S_NEXT + 2 * head + kind, after,
        )

    next_kv = {}
    sib_key.wait_recv()
    spread(KEY)
    sib_value.wait_recv()
    spread(VALUE)
    for kind, head in ((VALUE, 0), (KEY, 1), (VALUE, 1)):
        next_kv[kind, head] = to_next(kind, head)
        next_kv[kind, head].start()

    loads[4].wait()
    adapt(QUERY, 0)
    sib_query = to_sibling(QUERY, S_QUERY)
    sib_query.start()
    loads[5].wait()
    pack(GRAD, padded(raw[GRAD]))
    sib_grad = to_sibling(GRAD, S_GRAD)
    sib_grad.start()

    next_act.wait_recv()
    block = act_past.at[core, share_rows]
    for step in range(1, n_tp):
        remote(block, block, S_PARTS, me, lax.rem(tp + step, n_tp)).start()
    block = act_past.at[core, pl.ds(0, ROWS - ROWS // n_tp)]
    tp_acts = remote(block, block, S_PARTS, other)
    pass_act = remote(act_past.at[core], act_past.at[core], S_PAST + 1, other)
    sib_act.wait_recv()
    for i, values in enumerate(in_order(act[...], act_sib[...])):
        act_window[GROUP_ROWS + i * STRETCH:GROUP_ROWS + (i + 1) * STRETCH] = values
    for kind, copy in ((QUERY, sib_query), (GRAD, sib_grad)):
        copy.wait_recv()
        for i, values in enumerate(in_order(packed[kind, core], sibling[kind])):
            sorted_qg[kind - QUERY, i * STRETCH:(i + 1) * STRETCH] = values

    key_place = lax.broadcasted_iota(jnp.int32, (WINDOW, GROUP_ROWS), 0)
    query_place = lax.broadcasted_iota(jnp.int32, (1, GROUP_ROWS), 1)
    lowest = jnp.zeros((1, GROUP_ROWS), jnp.int32)
    for i in range(4):
        start = STRETCH * (first_ref[4 * chip + i] - 4 * chip + 4)
        lowest = jnp.where(query_place >= i * STRETCH, start, lowest)
    visible = (key_place >= lowest) & (key_place <= query_place + GROUP_ROWS)

    def scatter(unit, step):
        target = lax.rem(z + step, side)
        return remote(
            part.at[unit, target], scattered.at[unit, step], S_ALONG + 3 * unit, along(1, step)
        )

    def cross(unit, step):
        block = crossed.at[unit, y]
        return remote(block, block, S_ALONG + 3 * unit + 1, along(0, step))

    def gather(unit, step):
        block = gathered.at[unit, core, z]
        return remote(block, block, S_ALONG + 3 * unit + 2, along(1, step))

    def gather_other(unit, step):
        block = gathered.at[unit, core, z]
        return remote(block, block, S_ADAPTER + unit, along(1, step) + 1 - 2 * core)

    def stage(unit, which):
        block = scattered.at[unit, pl.ds(1, side - 1)]
        return remote(block, block, S_ALONG + 3 * unit + which, other)

    def send_unit(unit, activations, values):
        terms = dot(activations, values, (0, 0)).astype(BF16)
        for j in range(side):
            part[unit, j] = terms[j * rows:(j + 1) * rows]
        for step in steps:
            scatter(unit, step).start()

    def back(kind, head):
        lanes = pl.ds(head * PAD, PAD)
        return remote(
            back_send.at[kind, :, lanes], back_recv.at[kind, :, lanes],
            S_BACK + 2 * head + kind, before,
        )

    backs = {}
    for head in range(2):
        lanes = slice(head * PAD, (head + 1) * PAD)
        if head:
            next_kv[KEY, head].wait_recv()
        else:
            for copy in next_first:
                copy.wait_recv()
            for i, values in enumerate(in_order(key_past[0], key_past[1], past_places)):
                if i:
                    window_kv[KEY, i * STRETCH:(i + 1) * STRETCH, lanes] = values
        scores = dot(window_kv[KEY, :, lanes], sorted_qg[0, :, lanes], (1, 1)) * SCALE
        scores = jnp.where(visible, scores, FILL)
        peak = jnp.max(scores, axis=0, keepdims=True)
        weights = jnp.exp(scores - peak)
        share = weights / jnp.sum(weights, axis=0, keepdims=True)
        probs[head] = share
        low = share.astype(BF16)
        probs_low[head] = low
        terms = dot(low, sorted_qg[1, :, lanes], (1, 0))
        own_kv[VALUE, :, lanes] = terms[GROUP_ROWS:]
        terms = terms.astype(BF16)
        back_send[VALUE, :, lanes] = terms[STRETCH:GROUP_ROWS]
        backs[VALUE, head] = back(VALUE, head)
        backs[VALUE, head].start()
        if head:
            send_unit(2, act_window[...], terms)
        else:
            first_terms = terms
            tp_acts.wait_recv()
            pass_act.start()

        next_kv[VALUE, head].wait_recv()
        grad_probs = dot(window_kv[VALUE, :, lanes], sorted_qg[1, :, lanes], (1, 1))
        row_dot = jnp.sum(probs_low[head].astype(F32) * grad_probs, axis=0, keepdims=True)
        grad_scores = (probs[head] * (grad_probs - row_dot)).astype(BF16)
        summed = (dot(grad_scores, window_kv[KEY, :, lanes], (0, 0)) * SCALE).astype(BF16)
        grads[0, :, lanes] = summed
        if head:
            send_unit(3, act_window[GROUP_ROWS:], summed)
        else:
            if relays:
                pl.semaphore_wait(entered_sem, len(relays))
            send_unit(1, act_window[GROUP_ROWS:], summed)
            pass_act.wait_recv()
            act_window[:STRETCH] = jnp.zeros((STRETCH, RANK), BF16)
            for i, values in enumerate(in_order(act_past[0], act_past[1], past_places)):
                if i:
                    act_window[i * STRETCH:(i + 1) * STRETCH] = values
            send_unit(0, act_window[...], first_terms)
        terms = dot(grad_scores, sorted_qg[0, :, lanes], (1, 0)) * SCALE
        back_send[KEY, :, lanes] = terms[STRETCH:GROUP_ROWS].astype(BF16)
        own_kv[KEY, :, lanes] = terms[GROUP_ROWS:]
        backs[KEY, head] = back(KEY, head)
        backs[KEY, head].start()

    def input_terms(i, values):
        return dot(values, weight_pad[i, core], (1, 1))

    def hand_out(i, slots):
        outs[i, core, :STRETCH] = slots[0]
        outs[i, core, STRETCH:] = slots[1]
        sib_send[i, :STRETCH] = slots[2]
        sib_send[i, STRETCH:] = slots[3]
        copy = remote(sib_send.at[i], outs.at[i, core], S_OUT + i, other)
        copy.start()
        return copy

    def add_back(kind):
        mine = own_kv[kind]
        return jnp.concatenate(
            [mine[:STRETCH], mine[STRETCH:] + back_recv[kind].astype(F32)], axis=0
        ).astype(BF16)

    def go_across(unit):
        stage(unit, 0).wait_recv()
        total = part[unit, z].astype(F32)
        for step in range(1, side):
            total = total + scattered[unit, step].astype(F32)
        crossed[unit, y] = total.astype(BF16)
        for step in steps:
            cross(unit, step).start()

    def go_around(unit):
        stage(unit, 1).wait_recv()
        total = crossed[unit, 0].astype(F32)
        for step in range(1, side):
            total = total + crossed[unit, step].astype(F32)
        gathered[unit, core, z] = total.astype(BF16)
        for step in steps:
            gather(unit, step).start()
        if unit == UNITS - 1:
            for step in steps + [0]:
                gather_other(unit, step).start()

    input_part = input_terms(0, grads[0])
    out_query = hand_out(0, to_slots(grads[0]))
    go_across(1)
    go_across(0)

    for head in range(2):
        backs[VALUE, head].wait_recv()
    grads[1] = add_back(VALUE)
    input_slots = to_slots(input_part + input_terms(1, grads[1]))
    gi_send[:STRETCH] = input_slots[2]
    gi_send[STRETCH:] = input_slots[3]
    sib_input = remote(gi_send, gi_sib, S_INPUT, other)
    sib_input.start()
    gi_along[tp, :STRETCH] = input_slots[0]
    gi_along[tp, STRETCH:] = input_slots[1]
    out_value = hand_out(2, to_slots(grads[1]))

    go_across(2)
    go_across(3)

    sib_input.wait_recv()
    gi_along[tp] = gi_along[tp] + gi_sib[...]

    for step in range(1, n_tp):
        block = gi_along.at[tp]
        remote(block, block, S_INPUTS, me, lax.rem(tp + step, n_tp)).start()
    block = gi_along.at[pl.ds(1, n_tp - 1)]
    tp_inputs = remote(block, block, S_INPUTS, other)
    go_around(1)
    go_around(0)
    for head in range(2):
        backs[KEY, head].wait_recv()
    out_key = hand_out(1, to_slots(add_back(KEY)))

    go_around(2)
    tp_inputs.wait_recv()
    total = gi_along[0]
    for x in range(1, n_tp):
        total = total + gi_along[x]
    gi_ref[...] = total.astype(BF16)
    go_around(3)

    for copy in (out_query, out_value, out_key):
        copy.wait_recv()
    out_ref[...] = outs[...]

    for copy in (
        sib_key, sib_act, sib_value, sib_query, sib_grad, *next_first, next_act, tp_acts, pass_act,
        *next_kv.values(), *backs.values(), out_query, out_value, out_key, sib_input,
    ):
        copy.wait_send()
    tp_inputs.wait_send()
    sib_adapter = []
    for unit in range(UNITS):
        stage(unit, 0).wait_send()
        stage(unit, 1).wait_send()
    for unit in range(UNITS):
        stage(unit, 2).wait_recv()
        block = gathered.at[unit, core]
        copy = remote(block, block, S_ADAPTER + unit, other)
        if unit < UNITS - 1:
            copy.start()
        sib_adapter.append(copy)
        stage(unit, 2).wait_send()
    for unit in range(UNITS):
        sib_adapter[unit].wait_recv()
        ga_ref[unit] = gathered[unit]
        sib_adapter[unit].wait_send()


def finish(
    out_ref, gi_ref, ga_ref, q_hbm, k_hbm, v_hbm, input_hbm, adapter_hbm,
    wide, adapter, store_sem,
):
    stores = [
        pltpu.make_async_copy(source, hbm, store_sem.at[i])
        for i, (source, hbm) in enumerate((
            (wide.at[0], q_hbm), (wide.at[1], k_hbm), (wide.at[2], v_hbm),
            (adapter.at[0], adapter_hbm.at[0]), (adapter.at[1], adapter_hbm.at[1]), (gi_ref, input_hbm),
        ))
    ]
    stores[5].start()
    for i in range(2):
        heads = [ga_ref[2 * head + 1 - i, pair] for pair in range(2) for head in range(2)]
        heads = [head.reshape(RANK, PAD)[:, :HEAD].astype(F32) for head in heads]
        adapter[i] = jnp.concatenate(heads, axis=1)
        stores[3 + i].start()
    for i in range(3):
        wide[i] = unpadded([out_ref[i, 0], out_ref[i, 1]])
        stores[i].start()
    for store in stores:
        store.wait()


def body(
    query_base, key_base, value_base, adapter_activation, adapter_up_weight, output_grad,
    stretch_doc, doc_first, slot_stretch,
):
    n_tp = lax.axis_size("tp")
    side = math.isqrt(lax.axis_size("ctx") // 2)
    rows = RANK // side
    stretches = slot_stretch.shape[0]
    anywhere = pl.BlockSpec(memory_space=pltpu.HBM)
    vmem = pl.BlockSpec(memory_space=pltpu.VMEM)

    def block(*shape, dtype=BF16):
        return pltpu.VMEM(shape, dtype)

    partial_results = pl.pallas_call(
        functools.partial(kernel, side, n_tp),
        out_shape=(
            pltpu.VMEM((3, 2, ROWS, PAIR), BF16),
            pltpu.VMEM((ROWS, RANK), BF16),
            pltpu.VMEM((UNITS, 2, side, rows, PAD), BF16),
        ),
        in_specs=[anywhere] * 8,
        out_specs=(vmem,) * 3,
        scratch_shapes=[
            block(4, ROWS, COLUMNS),
            block(ROWS, RANK),
            block(2, RANK, COLUMNS),
            block(2, 2, RANK, PAIR),
            block(4, 2, ROWS, PAIR),
            block(4, ROWS, PAIR),
            block(ROWS, RANK),
            block(2, ROWS, RANK),
            block(WINDOW, RANK),
            block(2, ROWS, PAD),
            block(2, WINDOW, PAIR),
            block(2, GROUP_ROWS, PAIR),
            block(2, WINDOW, GROUP_ROWS, dtype=F32),
            block(2, WINDOW, GROUP_ROWS),
            block(2, SENT, PAIR),
            block(2, SENT, PAIR),
            block(2, GROUP_ROWS, PAIR, dtype=F32),
            block(2, GROUP_ROWS, PAIR),
            block(3, ROWS, PAIR),
            block(3, 2, ROWS, PAIR),
            block(ROWS, RANK, dtype=F32),
            block(ROWS, RANK, dtype=F32),
            block(n_tp, ROWS, RANK, dtype=F32),
            block(UNITS, side, rows, PAD),
            block(UNITS, side, rows, PAD),
            block(UNITS, side, rows, PAD),
            block(UNITS, 2, side, rows, PAD),
            pltpu.SMEM((stretches,), jnp.int32),
            pltpu.SMEM((stretches,), jnp.int32),
            pltpu.SemaphoreType.DMA((8,)),
            pltpu.SemaphoreType.DMA((COPIES,)),
            pltpu.SemaphoreType.DMA((COPIES,)),
            pltpu.SemaphoreType.REGULAR,
        ],
        compiler_params=pltpu.CompilerParams(
            collective_id=0, has_side_effects=True, vmem_limit_bytes=54 * 2**20
        ),
    )(
        slot_stretch, doc_first, query_base, key_base, value_base, adapter_activation,
        adapter_up_weight, output_grad,
    )
    return pl.pallas_call(
        finish,
        out_shape=(
            jax.ShapeDtypeStruct((ROWS, COLUMNS), BF16),
            jax.ShapeDtypeStruct((ROWS, COLUMNS), BF16),
            jax.ShapeDtypeStruct((ROWS, COLUMNS), BF16),
            jax.ShapeDtypeStruct((ROWS, RANK), BF16),
            jax.ShapeDtypeStruct((2, RANK, COLUMNS), F32),
        ),
        in_specs=[vmem] * 3,
        out_specs=(anywhere,) * 5,
        scratch_shapes=[
            block(3, ROWS, COLUMNS),
            block(2, RANK, COLUMNS, dtype=F32),
            pltpu.SemaphoreType.DMA((6,)),
        ],
        compiler_params=pltpu.CompilerParams(vmem_limit_bytes=32 * 2**20),
    )(*partial_results)


def solution(mesh):
    return jax.shard_map(
        body,
        mesh=mesh,
        in_specs=(
            P("ctx", "tp"),
            P("ctx", "tp"),
            P("ctx", "tp"),
            P("ctx", None),
            P(None, None, "tp"),
            P("ctx", "tp"),
            P(),
            P(),
            P(),
        ),
        out_specs=(
            P("ctx", "tp"),
            P("ctx", "tp"),
            P("ctx", "tp"),
            P("ctx", None),
            P(None, None, "tp"),
        ),
        check_vma=False,
    )
```

```python
import functools
import math

import jax
import jax.numpy as jnp
from jax import lax
from jax.experimental import pallas as pl
from jax.experimental.pallas import tpu as pltpu
from jax.sharding import PartitionSpec as P

HEAD = 224
PAD = 256
HEADS = 4
PAIR = 2 * PAD
ROWS = 128
STRETCH = 64
GROUP_ROWS = 2 * ROWS
WINDOW = 2 * GROUP_ROWS
SENT = 3 * STRETCH
RANK = 128
COLUMNS = HEADS * HEAD
SCALE = HEAD ** -0.5
FILL = -1e30

KEY, VALUE, QUERY, GRAD = range(4)
S_KEY, S_VALUE, S_QUERY, S_GRAD, S_ACT = range(5)
S_OUT = 5
S_INPUT = 8
S_NEXT = 9
S_BACK = 13
S_PAST = 17
S_FIRST = 19
S_ADAPTER = 20
S_ALONG = 23
S_INPUTS = 32
S_PARTS = 33
COPIES = 34
UNIT_AXIS = (1, 0, 0)
MESH = pl.DeviceIdType.MESH
F32 = jnp.float32
BF16 = jnp.bfloat16


def dot(a, b, contract):
    return lax.dot_general(a, b, ((contract[:1], contract[1:]), ((), ())), preferred_element_type=F32)


def padded(values):
    rows = values.shape[0]
    blank = jnp.zeros((rows, PAD - HEAD), values.dtype)
    parts = []
    for head in range(HEADS):
        parts += [values[:, head * HEAD:(head + 1) * HEAD], blank]
    return jnp.concatenate(parts, axis=1)


def unpadded(pairs):
    return jnp.concatenate(
        [pair[:, head * PAD:head * PAD + HEAD] for pair in pairs for head in range(2)], axis=1
    )


def kernel(
    side, n_tp,
    slot_hbm, first_hbm, q_hbm, k_hbm, v_hbm, a_hbm, w_hbm, g_hbm,
    out_ref, gi_ref, ga0_ref, ga1_ref, ga2_ref,
    raw, act, weight, weight_pad, packed, sibling, act_sib, act_past, act_window, key_past,
    window_kv, sorted_qg, probs, probs_low, back_send, back_recv, own_kv,
    grads, sib_send, outs, gi_send, gi_sib, gi_along,
    part0, part1, part2, scattered0, scattered1, scattered2,
    crossed0, crossed1, crossed2, gathered0, gathered1, gathered2,
    slot_ref, first_ref, load_sem, send_sem, recv_sem, entered_sem,
):
    part = (part0, part1, part2)
    scattered = (scattered0, scattered1, scattered2)
    crossed = (crossed0, crossed1, crossed2)
    gathered = (gathered0, gathered1, gathered2)
    me = lax.axis_index("ctx")
    tp = lax.axis_index("tp")
    core = lax.rem(me, 2)
    chip = lax.div(me, 2)
    y, z = lax.rem(chip, side), lax.div(chip, side)
    chips = side * side
    other = me + 1 - 2 * core
    after = lax.rem(chip + 1, chips) * 2 + core
    before = lax.rem(chip + chips - 1, chips) * 2 + core
    rows = RANK // side

    def along(axis, step):
        if axis == 0:
            return (z * side + lax.rem(y + step, side)) * 2 + core
        return (lax.rem(z + step, side) * side + y) * 2 + core

    def remote(src, dst, sem, ctx, x=None):
        return pltpu.make_async_remote_copy(
            src_ref=src, dst_ref=dst, send_sem=send_sem.at[sem], recv_sem=recv_sem.at[sem],
            device_id=(ctx, tp if x is None else x), device_id_type=MESH,
        )

    loads = [
        pltpu.make_async_copy(src, dst, load_sem.at[i])
        for i, (src, dst) in enumerate([
            (k_hbm, raw.at[KEY]), (a_hbm, act), (w_hbm, weight), (v_hbm, raw.at[VALUE]),
            (q_hbm, raw.at[QUERY]), (g_hbm, raw.at[GRAD]), (slot_hbm, slot_ref), (first_hbm, first_ref),
        ])
    ]
    loads[0].start()

    barrier = pltpu.get_barrier_semaphore()

    def greet(ctx, x):
        pl.semaphore_signal(barrier, inc=1, device_id=(ctx, x), device_id_type=MESH)

    steps = [side // 2 + (i // 2) * (1 - 2 * (i % 2)) for i in range(1, side)]
    near = [step for step in steps if min(step, side - step) <= 2]
    for step in near:
        greet(along(0, step), tp)
        greet(along(1, step), tp)
    for step in range(1, n_tp):
        greet(me, lax.rem(tp + step, n_tp))
    after_other = after + 1 - 2 * core
    before_other = before + 1 - 2 * core
    for device in (after, after_other, before, before_other, other):
        greet(device, tp)
    for load in loads[1:]:
        load.start()

    def pack(kind, values):
        packed[kind, 0] = values[:, :PAIR]
        packed[kind, 1] = values[:, PAIR:]

    def to_sibling(kind, sem):
        return remote(packed.at[kind, 1 - core], sibling.at[kind], sem, other)

    loads[0].wait()
    pack(KEY, padded(raw[KEY]))
    loads[1].wait()
    pl.semaphore_wait(barrier, 5 + 2 * len(near) + n_tp - 1)
    sib_key = to_sibling(KEY, S_KEY)
    sib_key.start()
    sib_act = remote(act, act_sib, S_ACT, other)
    sib_act.start()
    share_rows = pl.ds(pl.multiple_of(tp * (ROWS // n_tp), ROWS // n_tp), ROWS // n_tp)
    next_act = remote(act.at[share_rows], act_past.at[core, share_rows], S_PAST, after)
    next_act.start()
    first = pl.ds(0, PAD)
    next_first = [
        remote(packed.at[KEY, core, :, first], key_past.at[core], S_NEXT, after),
        remote(packed.at[KEY, 1 - core, :, first], key_past.at[core], S_FIRST, after_other),
    ]
    for copy in next_first:
        copy.start()
    relays = [(axis, step) for axis in (0, 1) for step in (2, side - 2)] if len(near) < len(steps) else []
    for axis, step in relays:
        pl.semaphore_signal(entered_sem, inc=1, device_id=(along(axis, step), tp), device_id_type=MESH)
    loads[2].wait()

    def adapt(kind, i):
        wide = padded(weight[i])
        weight_pad[i, 0] = wide[:, :PAIR]
        weight_pad[i, 1] = wide[:, PAIR:]
        wide = padded(raw[kind])
        for pair in range(2):
            update = dot(act[...], weight_pad[i, pair], (1, 0))
            base = wide[:, pair * PAIR:(pair + 1) * PAIR].astype(F32)
            packed[kind, pair] = (base + update).astype(BF16)

    loads[3].wait()
    adapt(VALUE, 1)
    sib_value = to_sibling(VALUE, S_VALUE)
    sib_value.start()

    loads[6].wait()
    loads[7].wait()
    places = [
        slot_ref[2 * me] - 4 * chip, slot_ref[2 * me + 1] - 4 * chip,
        slot_ref[2 * other] - 4 * chip, slot_ref[2 * other + 1] - 4 * chip,
    ]
    past = lax.rem(chip + chips - 1, chips)
    past_places = [slot_ref[4 * past + j] - 4 * past for j in range(4)]

    def in_order(own, sib, places=places):
        slots = [own[:STRETCH], own[STRETCH:], sib[:STRETCH], sib[STRETCH:]]
        result = []
        for i in range(4):
            picked = slots[3]
            for j in (2, 1, 0):
                picked = jnp.where(places[j] == i, slots[j], picked)
            result.append(picked)
        return result

    def to_slots(values):
        result = []
        for j in range(4):
            picked = values[3 * STRETCH:]
            for i in (2, 1, 0):
                picked = jnp.where(places[j] == i, values[i * STRETCH:(i + 1) * STRETCH], picked)
            result.append(picked)
        return result

    def spread(kind):
        window_kv[kind, :STRETCH] = jnp.zeros((STRETCH, PAIR), BF16)
        for i, values in enumerate(in_order(packed[kind, core], sibling[kind])):
            window_kv[kind, GROUP_ROWS + i * STRETCH:GROUP_ROWS + (i + 1) * STRETCH] = values

    def to_next(kind, head):
        lanes = pl.ds(head * PAD, PAD)
        return remote(
            window_kv.at[kind, pl.ds(GROUP_ROWS + STRETCH, SENT), lanes],
            window_kv.at[kind, pl.ds(STRETCH, SENT), lanes], S_NEXT + 2 * head + kind, after,
        )

    next_kv = {}
    sib_key.wait_recv()
    spread(KEY)
    sib_value.wait_recv()
    spread(VALUE)
    for kind, head in ((VALUE, 0), (KEY, 1), (VALUE, 1)):
        next_kv[kind, head] = to_next(kind, head)
        next_kv[kind, head].start()

    loads[4].wait()
    adapt(QUERY, 0)
    sib_query = to_sibling(QUERY, S_QUERY)
    sib_query.start()
    loads[5].wait()
    pack(GRAD, padded(raw[GRAD]))
    sib_grad = to_sibling(GRAD, S_GRAD)
    sib_grad.start()

    next_act.wait_recv()
    block = act_past.at[core, share_rows]
    for step in range(1, n_tp):
        remote(block, block, S_PARTS, me, lax.rem(tp + step, n_tp)).start()
    block = act_past.at[core, pl.ds(0, ROWS - ROWS // n_tp)]
    tp_acts = remote(block, block, S_PARTS, other)
    pass_act = remote(act_past.at[core], act_past.at[core], S_PAST + 1, other)
    sib_act.wait_recv()
    for i, values in enumerate(in_order(act[...], act_sib[...])):
        act_window[GROUP_ROWS + i * STRETCH:GROUP_ROWS + (i + 1) * STRETCH] = values
    for kind, copy in ((QUERY, sib_query), (GRAD, sib_grad)):
        copy.wait_recv()
        for i, values in enumerate(in_order(packed[kind, core], sibling[kind])):
            sorted_qg[kind - QUERY, i * STRETCH:(i + 1) * STRETCH] = values

    key_place = lax.broadcasted_iota(jnp.int32, (WINDOW, GROUP_ROWS), 0)
    query_place = lax.broadcasted_iota(jnp.int32, (1, GROUP_ROWS), 1)
    lowest = jnp.zeros((1, GROUP_ROWS), jnp.int32)
    for i in range(4):
        start = STRETCH * (first_ref[4 * chip + i] - 4 * chip + 4)
        lowest = jnp.where(query_place >= i * STRETCH, start, lowest)
    visible = (key_place >= lowest) & (key_place <= query_place + GROUP_ROWS)

    def position(unit, crossing):
        return (y, z)[UNIT_AXIS[unit] ^ crossing]

    def scatter(unit, step):
        target = lax.rem(position(unit, 0) + step, side)
        return remote(
            part[unit].at[target], scattered[unit].at[step], S_ALONG + 3 * unit, along(UNIT_AXIS[unit], step)
        )

    def cross(unit, step):
        block = crossed[unit].at[position(unit, 1)]
        return remote(block, block, S_ALONG + 3 * unit + 1, along(1 - UNIT_AXIS[unit], step))

    def gather(unit, step):
        block = gathered[unit].at[core, position(unit, 0)]
        return remote(block, block, S_ALONG + 3 * unit + 2, along(UNIT_AXIS[unit], step))

    def gather_other(unit, step):
        block = gathered[unit].at[core, position(unit, 0)]
        target = along(UNIT_AXIS[unit], step) + 1 - 2 * core
        return remote(block, block, S_ADAPTER + unit, target)

    def stage(unit, which):
        block = scattered[unit].at[pl.ds(1, side - 1)]
        return remote(block, block, S_ALONG + 3 * unit + which, other)

    def adapter_terms(block, activations, values):
        terms = dot(activations, values, (0, 0)).astype(BF16)
        for j in range(side):
            block(j)[...] = terms[j * rows:(j + 1) * rows]

    def send_unit(unit):
        for step in steps:
            scatter(unit, step).start()

    def back(kind, head):
        lanes = pl.ds(head * PAD, PAD)
        return remote(
            back_send.at[kind, :, lanes], back_recv.at[kind, :, lanes],
            S_BACK + 2 * head + kind, before,
        )

    backs = {}
    for head in range(2):
        lanes = slice(head * PAD, (head + 1) * PAD)
        if head:
            next_kv[KEY, head].wait_recv()
        else:
            for copy in next_first:
                copy.wait_recv()
            for i, values in enumerate(in_order(key_past[0], key_past[1], past_places)):
                if i:
                    window_kv[KEY, i * STRETCH:(i + 1) * STRETCH, lanes] = values
        scores = dot(window_kv[KEY, :, lanes], sorted_qg[0, :, lanes], (1, 1)) * SCALE
        scores = jnp.where(visible, scores, FILL)
        peak = jnp.max(scores, axis=0, keepdims=True)
        weights = jnp.exp(scores - peak)
        share = weights / jnp.sum(weights, axis=0, keepdims=True)
        probs[head] = share
        low = share.astype(BF16)
        probs_low[head] = low
        terms = dot(low, sorted_qg[1, :, lanes], (1, 0))
        own_kv[VALUE, :, lanes] = terms[GROUP_ROWS:]
        terms = terms.astype(BF16)
        back_send[VALUE, :, lanes] = terms[STRETCH:GROUP_ROWS]
        backs[VALUE, head] = back(VALUE, head)
        backs[VALUE, head].start()
        if head:
            adapter_terms(lambda j: part[1].at[j], act_window[...], terms)
            send_unit(1)
        else:
            first_terms = terms
            tp_acts.wait_recv()
            pass_act.start()

        next_kv[VALUE, head].wait_recv()
        grad_probs = dot(window_kv[VALUE, :, lanes], sorted_qg[1, :, lanes], (1, 1))
        row_dot = jnp.sum(probs_low[head].astype(F32) * grad_probs, axis=0, keepdims=True)
        grad_scores = (probs[head] * (grad_probs - row_dot)).astype(BF16)
        summed = (dot(grad_scores, window_kv[KEY, :, lanes], (0, 0)) * SCALE).astype(BF16)
        grads[0, :, lanes] = summed
        if head:
            adapter_terms(lambda j: part[2].at[j], act_window[GROUP_ROWS:], summed)
            send_unit(2)
        else:
            adapter_terms(lambda j: part[0].at[j, 0], act_window[GROUP_ROWS:], summed)
            pass_act.wait_recv()
            act_window[:STRETCH] = jnp.zeros((STRETCH, RANK), BF16)
            for i, values in enumerate(in_order(act_past[0], act_past[1], past_places)):
                if i:
                    act_window[i * STRETCH:(i + 1) * STRETCH] = values
            adapter_terms(lambda j: part[0].at[j, 1], act_window[...], first_terms)
            if relays:
                pl.semaphore_wait(entered_sem, len(relays))
            send_unit(0)
        terms = dot(grad_scores, sorted_qg[0, :, lanes], (1, 0)) * SCALE
        back_send[KEY, :, lanes] = terms[STRETCH:GROUP_ROWS].astype(BF16)
        own_kv[KEY, :, lanes] = terms[GROUP_ROWS:]
        backs[KEY, head] = back(KEY, head)
        backs[KEY, head].start()

    def input_terms(i, values):
        return dot(values, weight_pad[i, core], (1, 1))

    def hand_out(i, slots):
        outs[i, core, :STRETCH] = slots[0]
        outs[i, core, STRETCH:] = slots[1]
        sib_send[i, :STRETCH] = slots[2]
        sib_send[i, STRETCH:] = slots[3]
        copy = remote(sib_send.at[i], outs.at[i, core], S_OUT + i, other)
        copy.start()
        return copy

    def add_back(kind):
        mine = own_kv[kind]
        return jnp.concatenate(
            [mine[:STRETCH], mine[STRETCH:] + back_recv[kind].astype(F32)], axis=0
        ).astype(BF16)

    def go_across(unit):
        stage(unit, 0).wait_recv()
        total = part[unit][position(unit, 0)].astype(F32)
        for step in range(1, side):
            total = total + scattered[unit][step].astype(F32)
        crossed[unit][position(unit, 1)] = total.astype(BF16)
        for step in steps:
            cross(unit, step).start()

    def go_around(unit):
        stage(unit, 1).wait_recv()
        total = crossed[unit][0].astype(F32)
        for step in range(1, side):
            total = total + crossed[unit][step].astype(F32)
        gathered[unit][core, position(unit, 0)] = total.astype(BF16)
        for step in steps:
            gather(unit, step).start()
        if unit == 2:
            for step in steps + [0]:
                gather_other(unit, step).start()

    input_part = input_terms(0, grads[0])
    out_query = hand_out(0, to_slots(grads[0]))
    go_across(0)

    for head in range(2):
        backs[VALUE, head].wait_recv()
    grads[1] = add_back(VALUE)
    input_slots = to_slots(input_part + input_terms(1, grads[1]))
    gi_send[:STRETCH] = input_slots[2]
    gi_send[STRETCH:] = input_slots[3]
    sib_input = remote(gi_send, gi_sib, S_INPUT, other)
    sib_input.start()
    gi_along[tp, :STRETCH] = input_slots[0]
    gi_along[tp, STRETCH:] = input_slots[1]
    out_value = hand_out(2, to_slots(grads[1]))

    go_across(1)
    go_across(2)

    sib_input.wait_recv()
    gi_along[tp] = gi_along[tp] + gi_sib[...]

    for step in range(1, n_tp):
        block = gi_along.at[tp]
        remote(block, block, S_INPUTS, me, lax.rem(tp + step, n_tp)).start()
    block = gi_along.at[pl.ds(1, n_tp - 1)]
    tp_inputs = remote(block, block, S_INPUTS, other)
    for head in range(2):
        backs[KEY, head].wait_recv()
    out_key = hand_out(1, to_slots(add_back(KEY)))

    go_around(0)
    go_around(1)
    tp_inputs.wait_recv()
    total = gi_along[0]
    for x in range(1, n_tp):
        total = total + gi_along[x]
    gi_ref[...] = total.astype(BF16)
    go_around(2)

    for copy in (out_query, out_value, out_key):
        copy.wait_recv()
    out_ref[...] = outs[...]

    for copy in (
        sib_key, sib_act, sib_value, sib_query, sib_grad, *next_first, next_act, tp_acts, pass_act,
        *next_kv.values(), *backs.values(), out_query, out_value, out_key, sib_input,
    ):
        copy.wait_send()
    tp_inputs.wait_send()
    sib_adapter = []
    for unit in range(3):
        stage(unit, 0).wait_send()
        stage(unit, 1).wait_send()
    for unit in range(3):
        stage(unit, 2).wait_recv()
        block = gathered[unit].at[core]
        copy = remote(block, block, S_ADAPTER + unit, other)
        if unit < 2:
            copy.start()
        sib_adapter.append(copy)
        stage(unit, 2).wait_send()
    for unit, ref in enumerate((ga0_ref, ga1_ref, ga2_ref)):
        sib_adapter[unit].wait_recv()
        ref[...] = gathered[unit][...]
        sib_adapter[unit].wait_send()


def finish(
    out_ref, gi_ref, head0, value1, query1, q_hbm, k_hbm, v_hbm, input_hbm, adapter_hbm,
    wide, adapter, store_sem,
):
    stores = [
        pltpu.make_async_copy(source, hbm, store_sem.at[i])
        for i, (source, hbm) in enumerate((
            (wide.at[0], q_hbm), (wide.at[1], k_hbm), (wide.at[2], v_hbm),
            (adapter.at[0], adapter_hbm.at[0]), (adapter.at[1], adapter_hbm.at[1]), (gi_ref, input_hbm),
        ))
    ]
    stores[5].start()
    for i, head1 in ((1, value1), (0, query1)):
        heads = []
        for pair in range(2):
            heads += [head0[pair, :, i], head1[pair]]
        heads = [head.reshape(RANK, PAD)[:, :HEAD].astype(F32) for head in heads]
        adapter[i] = jnp.concatenate(heads, axis=1)
        stores[3 + i].start()
    for i in range(3):
        wide[i] = unpadded([out_ref[i, 0], out_ref[i, 1]])
        stores[i].start()
    for store in stores:
        store.wait()


def body(
    query_base, key_base, value_base, adapter_activation, adapter_up_weight, output_grad,
    stretch_doc, doc_first, slot_stretch,
):
    n_tp = lax.axis_size("tp")
    side = math.isqrt(lax.axis_size("ctx") // 2)
    rows = RANK // side
    stretches = slot_stretch.shape[0]
    anywhere = pl.BlockSpec(memory_space=pltpu.HBM)
    vmem = pl.BlockSpec(memory_space=pltpu.VMEM)

    def block(*shape, dtype=BF16):
        return pltpu.VMEM(shape, dtype)

    partial_results = pl.pallas_call(
        functools.partial(kernel, side, n_tp),
        out_shape=(
            pltpu.VMEM((3, 2, ROWS, PAIR), BF16),
            pltpu.VMEM((ROWS, RANK), BF16),
            pltpu.VMEM((2, side, 2, rows, PAD), BF16),
            pltpu.VMEM((2, side, rows, PAD), BF16),
            pltpu.VMEM((2, side, rows, PAD), BF16),
        ),
        in_specs=[anywhere] * 8,
        out_specs=(vmem,) * 5,
        scratch_shapes=[
            block(4, ROWS, COLUMNS),
            block(ROWS, RANK),
            block(2, RANK, COLUMNS),
            block(2, 2, RANK, PAIR),
            block(4, 2, ROWS, PAIR),
            block(4, ROWS, PAIR),
            block(ROWS, RANK),
            block(2, ROWS, RANK),
            block(WINDOW, RANK),
            block(2, ROWS, PAD),
            block(2, WINDOW, PAIR),
            block(2, GROUP_ROWS, PAIR),
            block(2, WINDOW, GROUP_ROWS, dtype=F32),
            block(2, WINDOW, GROUP_ROWS),
            block(2, SENT, PAIR),
            block(2, SENT, PAIR),
            block(2, GROUP_ROWS, PAIR, dtype=F32),
            block(2, GROUP_ROWS, PAIR),
            block(3, ROWS, PAIR),
            block(3, 2, ROWS, PAIR),
            block(ROWS, RANK, dtype=F32),
            block(ROWS, RANK, dtype=F32),
            block(n_tp, ROWS, RANK, dtype=F32),
            *((block(side, 2, rows, PAD), block(side, rows, PAD), block(side, rows, PAD)) * 3),
            block(2, side, 2, rows, PAD),
            block(2, side, rows, PAD),
            block(2, side, rows, PAD),
            pltpu.SMEM((stretches,), jnp.int32),
            pltpu.SMEM((stretches,), jnp.int32),
            pltpu.SemaphoreType.DMA((8,)),
            pltpu.SemaphoreType.DMA((COPIES,)),
            pltpu.SemaphoreType.DMA((COPIES,)),
            pltpu.SemaphoreType.REGULAR,
        ],
        compiler_params=pltpu.CompilerParams(
            collective_id=0, has_side_effects=True, vmem_limit_bytes=54 * 2**20
        ),
    )(
        slot_stretch, doc_first, query_base, key_base, value_base, adapter_activation,
        adapter_up_weight, output_grad,
    )
    return pl.pallas_call(
        finish,
        out_shape=(
            jax.ShapeDtypeStruct((ROWS, COLUMNS), BF16),
            jax.ShapeDtypeStruct((ROWS, COLUMNS), BF16),
            jax.ShapeDtypeStruct((ROWS, COLUMNS), BF16),
            jax.ShapeDtypeStruct((ROWS, RANK), BF16),
            jax.ShapeDtypeStruct((2, RANK, COLUMNS), F32),
        ),
        in_specs=[vmem] * 5,
        out_specs=(anywhere,) * 5,
        scratch_shapes=[
            block(3, ROWS, COLUMNS),
            block(2, RANK, COLUMNS, dtype=F32),
            pltpu.SemaphoreType.DMA((6,)),
        ],
        compiler_params=pltpu.CompilerParams(vmem_limit_bytes=32 * 2**20),
    )(*partial_results)


def solution(mesh):
    return jax.shard_map(
        body,
        mesh=mesh,
        in_specs=(
            P("ctx", "tp"),
            P("ctx", "tp"),
            P("ctx", "tp"),
            P("ctx", None),
            P(None, None, "tp"),
            P("ctx", "tp"),
            P(),
            P(),
            P(),
        ),
        out_specs=(
            P("ctx", "tp"),
            P("ctx", "tp"),
            P("ctx", "tp"),
            P("ctx", None),
            P(None, None, "tp"),
        ),
        check_vma=False,
    )
```

```python
import functools
import math

import jax
import jax.numpy as jnp
from jax import lax
from jax.experimental import pallas as pl
from jax.experimental.pallas import tpu as pltpu
from jax.sharding import PartitionSpec as P

HEAD = 224
PAD = 256
HEADS = 4
PAIR = 2 * PAD
ROWS = 128
STRETCH = 64
GROUP_ROWS = 2 * ROWS
WINDOW = 2 * GROUP_ROWS
SENT = 3 * STRETCH
RANK = 128
COLUMNS = HEADS * HEAD
SCALE = HEAD ** -0.5
FILL = -1e30

KEY, VALUE, QUERY, GRAD = range(4)
S_KEY, S_VALUE, S_QUERY, S_GRAD, S_ACT = range(5)
S_OUT = 5
S_INPUT = 8
S_NEXT = 9
S_BACK = 13
S_PAST = 17
S_FIRST = 19
S_ADAPTER = 20
S_ALONG = 23
S_INPUTS = 32
S_PARTS = 33
COPIES = 34
UNIT_AXIS = (1, 0, 0)
MESH = pl.DeviceIdType.MESH
F32 = jnp.float32
BF16 = jnp.bfloat16


def dot(a, b, contract):
    return lax.dot_general(a, b, ((contract[:1], contract[1:]), ((), ())), preferred_element_type=F32)


def padded(values):
    rows = values.shape[0]
    blank = jnp.zeros((rows, PAD - HEAD), values.dtype)
    parts = []
    for head in range(HEADS):
        parts += [values[:, head * HEAD:(head + 1) * HEAD], blank]
    return jnp.concatenate(parts, axis=1)


def unpadded(pairs):
    return jnp.concatenate(
        [pair[:, head * PAD:head * PAD + HEAD] for pair in pairs for head in range(2)], axis=1
    )


def kernel(
    side, n_tp,
    slot_hbm, first_hbm, q_hbm, k_hbm, v_hbm, a_hbm, w_hbm, g_hbm,
    out_ref, gi_ref, ga0_ref, ga1_ref, ga2_ref,
    raw, act, weight, weight_pad, packed, sibling, act_sib, act_past, act_window, key_past,
    window_kv, sorted_qg, probs, probs_low, back_send, back_recv, own_kv,
    grads, sib_send, outs, gi_send, gi_sib, gi_along,
    part0, part1, part2, scattered0, scattered1, scattered2,
    crossed0, crossed1, crossed2, gathered0, gathered1, gathered2,
    slot_ref, first_ref, load_sem, send_sem, recv_sem, entered_sem,
):
    part = (part0, part1, part2)
    scattered = (scattered0, scattered1, scattered2)
    crossed = (crossed0, crossed1, crossed2)
    gathered = (gathered0, gathered1, gathered2)
    me = lax.axis_index("ctx")
    tp = lax.axis_index("tp")
    core = lax.rem(me, 2)
    chip = lax.div(me, 2)
    y, z = lax.rem(chip, side), lax.div(chip, side)
    chips = side * side
    other = me + 1 - 2 * core
    after = lax.rem(chip + 1, chips) * 2 + core
    before = lax.rem(chip + chips - 1, chips) * 2 + core
    rows = RANK // side

    def along(axis, step):
        if axis == 0:
            return (z * side + lax.rem(y + step, side)) * 2 + core
        return (lax.rem(z + step, side) * side + y) * 2 + core

    def remote(src, dst, sem, ctx, x=None):
        return pltpu.make_async_remote_copy(
            src_ref=src, dst_ref=dst, send_sem=send_sem.at[sem], recv_sem=recv_sem.at[sem],
            device_id=(ctx, tp if x is None else x), device_id_type=MESH,
        )

    loads = [
        pltpu.make_async_copy(src, dst, load_sem.at[i])
        for i, (src, dst) in enumerate([
            (k_hbm, raw.at[KEY]), (a_hbm, act), (w_hbm, weight), (v_hbm, raw.at[VALUE]),
            (q_hbm, raw.at[QUERY]), (g_hbm, raw.at[GRAD]), (slot_hbm, slot_ref), (first_hbm, first_ref),
        ])
    ]
    loads[0].start()

    barrier = pltpu.get_barrier_semaphore()

    def greet(ctx, x):
        pl.semaphore_signal(barrier, inc=1, device_id=(ctx, x), device_id_type=MESH)

    steps = [side // 2 + (i // 2) * (1 - 2 * (i % 2)) for i in range(1, side)]
    near = [step for step in steps if min(step, side - step) <= 2]
    for step in near:
        greet(along(0, step), tp)
        greet(along(1, step), tp)
    for step in range(1, n_tp):
        greet(me, lax.rem(tp + step, n_tp))
    after_other = after + 1 - 2 * core
    before_other = before + 1 - 2 * core
    for device in (after, after_other, before, before_other, other):
        greet(device, tp)
    for load in loads[1:]:
        load.start()

    def pack(kind, values):
        packed[kind, 0] = values[:, :PAIR]
        packed[kind, 1] = values[:, PAIR:]

    def to_sibling(kind, sem):
        return remote(packed.at[kind, 1 - core], sibling.at[kind], sem, other)

    loads[0].wait()
    pack(KEY, padded(raw[KEY]))
    loads[1].wait()
    pl.semaphore_wait(barrier, 5 + 2 * len(near) + n_tp - 1)
    sib_key = to_sibling(KEY, S_KEY)
    sib_key.start()
    sib_act = remote(act, act_sib, S_ACT, other)
    sib_act.start()
    share_rows = pl.ds(pl.multiple_of(tp * (ROWS // n_tp), ROWS // n_tp), ROWS // n_tp)
    next_act = remote(act.at[share_rows], act_past.at[core, share_rows], S_PAST, after)
    next_act.start()
    first = pl.ds(0, PAD)
    next_first = [
        remote(packed.at[KEY, core, :, first], key_past.at[core], S_NEXT, after),
        remote(packed.at[KEY, 1 - core, :, first], key_past.at[core], S_FIRST, after_other),
    ]
    for copy in next_first:
        copy.start()
    relays = [(axis, step) for axis in (0, 1) for step in (2, side - 2)] if len(near) < len(steps) else []
    for axis, step in relays:
        pl.semaphore_signal(entered_sem, inc=1, device_id=(along(axis, step), tp), device_id_type=MESH)
    loads[2].wait()

    def adapt(kind, i):
        wide = padded(weight[i])
        weight_pad[i, 0] = wide[:, :PAIR]
        weight_pad[i, 1] = wide[:, PAIR:]
        wide = padded(raw[kind])
        for pair in range(2):
            update = dot(act[...], weight_pad[i, pair], (1, 0))
            base = wide[:, pair * PAIR:(pair + 1) * PAIR].astype(F32)
            packed[kind, pair] = (base + update).astype(BF16)

    loads[3].wait()
    adapt(VALUE, 1)
    sib_value = to_sibling(VALUE, S_VALUE)
    sib_value.start()

    loads[6].wait()
    loads[7].wait()
    places = [
        slot_ref[2 * me] - 4 * chip, slot_ref[2 * me + 1] - 4 * chip,
        slot_ref[2 * other] - 4 * chip, slot_ref[2 * other + 1] - 4 * chip,
    ]
    past = lax.rem(chip + chips - 1, chips)
    past_places = [slot_ref[4 * past + j] - 4 * past for j in range(4)]

    def in_order(own, sib, places=places):
        slots = [own[:STRETCH], own[STRETCH:], sib[:STRETCH], sib[STRETCH:]]
        result = []
        for i in range(4):
            picked = slots[3]
            for j in (2, 1, 0):
                picked = jnp.where(places[j] == i, slots[j], picked)
            result.append(picked)
        return result

    def to_slots(values):
        result = []
        for j in range(4):
            picked = values[3 * STRETCH:]
            for i in (2, 1, 0):
                picked = jnp.where(places[j] == i, values[i * STRETCH:(i + 1) * STRETCH], picked)
            result.append(picked)
        return result

    def spread(kind):
        window_kv[kind, :STRETCH] = jnp.zeros((STRETCH, PAIR), BF16)
        for i, values in enumerate(in_order(packed[kind, core], sibling[kind])):
            window_kv[kind, GROUP_ROWS + i * STRETCH:GROUP_ROWS + (i + 1) * STRETCH] = values

    def to_next(kind, head):
        lanes = pl.ds(head * PAD, PAD)
        return remote(
            window_kv.at[kind, pl.ds(GROUP_ROWS + STRETCH, SENT), lanes],
            window_kv.at[kind, pl.ds(STRETCH, SENT), lanes], S_NEXT + 2 * head + kind, after,
        )

    next_kv = {}
    sib_key.wait_recv()
    spread(KEY)
    sib_value.wait_recv()
    spread(VALUE)
    for kind, head in ((VALUE, 0), (KEY, 1), (VALUE, 1)):
        next_kv[kind, head] = to_next(kind, head)
        next_kv[kind, head].start()

    loads[4].wait()
    adapt(QUERY, 0)
    sib_query = to_sibling(QUERY, S_QUERY)
    sib_query.start()
    loads[5].wait()
    pack(GRAD, padded(raw[GRAD]))
    sib_grad = to_sibling(GRAD, S_GRAD)
    sib_grad.start()

    next_act.wait_recv()
    block = act_past.at[core, share_rows]
    for step in range(1, n_tp):
        remote(block, block, S_PARTS, me, lax.rem(tp + step, n_tp)).start()
    block = act_past.at[core, pl.ds(0, ROWS - ROWS // n_tp)]
    tp_acts = remote(block, block, S_PARTS, other)
    pass_act = remote(act_past.at[core], act_past.at[core], S_PAST + 1, other)
    sib_act.wait_recv()
    for i, values in enumerate(in_order(act[...], act_sib[...])):
        act_window[GROUP_ROWS + i * STRETCH:GROUP_ROWS + (i + 1) * STRETCH] = values
    for kind, copy in ((QUERY, sib_query), (GRAD, sib_grad)):
        copy.wait_recv()
        for i, values in enumerate(in_order(packed[kind, core], sibling[kind])):
            sorted_qg[kind - QUERY, i * STRETCH:(i + 1) * STRETCH] = values

    key_place = lax.broadcasted_iota(jnp.int32, (WINDOW, GROUP_ROWS), 0)
    query_place = lax.broadcasted_iota(jnp.int32, (1, GROUP_ROWS), 1)
    lowest = jnp.zeros((1, GROUP_ROWS), jnp.int32)
    for i in range(4):
        start = STRETCH * (first_ref[4 * chip + i] - 4 * chip + 4)
        lowest = jnp.where(query_place >= i * STRETCH, start, lowest)
    visible = (key_place >= lowest) & (key_place <= query_place + GROUP_ROWS)

    def position(unit, crossing):
        return (y, z)[UNIT_AXIS[unit] ^ crossing]

    def scatter(unit, step):
        target = lax.rem(position(unit, 0) + step, side)
        return remote(
            part[unit].at[target], scattered[unit].at[step], S_ALONG + 3 * unit, along(UNIT_AXIS[unit], step)
        )

    def cross(unit, step):
        block = crossed[unit].at[position(unit, 1)]
        return remote(block, block, S_ALONG + 3 * unit + 1, along(1 - UNIT_AXIS[unit], step))

    def gather(unit, step):
        block = gathered[unit].at[core, position(unit, 0)]
        return remote(block, block, S_ALONG + 3 * unit + 2, along(UNIT_AXIS[unit], step))

    def gather_other(unit, step):
        block = gathered[unit].at[core, position(unit, 0)]
        target = along(UNIT_AXIS[unit], step) + 1 - 2 * core
        return remote(block, block, S_ADAPTER + unit, target)

    def stage(unit, which):
        block = scattered[unit].at[pl.ds(1, side - 1)]
        return remote(block, block, S_ALONG + 3 * unit + which, other)

    def adapter_terms(block, activations, values):
        terms = dot(activations, values, (0, 0)).astype(BF16)
        for j in range(side):
            block(j)[...] = terms[j * rows:(j + 1) * rows]

    def send_unit(unit):
        for step in steps:
            scatter(unit, step).start()

    def back(kind, head):
        lanes = pl.ds(head * PAD, PAD)
        return remote(
            back_send.at[kind, :, lanes], back_recv.at[kind, :, lanes],
            S_BACK + 2 * head + kind, before,
        )

    backs = {}
    for head in range(2):
        lanes = slice(head * PAD, (head + 1) * PAD)
        if head:
            next_kv[KEY, head].wait_recv()
        else:
            for copy in next_first:
                copy.wait_recv()
            for i, values in enumerate(in_order(key_past[0], key_past[1], past_places)):
                if i:
                    window_kv[KEY, i * STRETCH:(i + 1) * STRETCH, lanes] = values
        scores = dot(window_kv[KEY, :, lanes], sorted_qg[0, :, lanes], (1, 1)) * SCALE
        scores = jnp.where(visible, scores, FILL)
        peak = jnp.max(scores, axis=0, keepdims=True)
        weights = jnp.exp(scores - peak)
        share = weights / jnp.sum(weights, axis=0, keepdims=True)
        probs[head] = share
        low = share.astype(BF16)
        probs_low[head] = low
        terms = dot(low, sorted_qg[1, :, lanes], (1, 0))
        own_kv[VALUE, :, lanes] = terms[GROUP_ROWS:]
        terms = terms.astype(BF16)
        back_send[VALUE, :, lanes] = terms[STRETCH:GROUP_ROWS]
        backs[VALUE, head] = back(VALUE, head)
        backs[VALUE, head].start()
        if head:
            adapter_terms(lambda j: part[1].at[j], act_window[...], terms)
        else:
            first_terms = terms
            tp_acts.wait_recv()
            pass_act.start()

        next_kv[VALUE, head].wait_recv()
        if head:
            send_unit(1)
        grad_probs = dot(window_kv[VALUE, :, lanes], sorted_qg[1, :, lanes], (1, 1))
        row_dot = jnp.sum(probs_low[head].astype(F32) * grad_probs, axis=0, keepdims=True)
        grad_scores = (probs[head] * (grad_probs - row_dot)).astype(BF16)
        summed = (dot(grad_scores, window_kv[KEY, :, lanes], (0, 0)) * SCALE).astype(BF16)
        grads[0, :, lanes] = summed
        if head:
            adapter_terms(lambda j: part[2].at[j], act_window[GROUP_ROWS:], summed)
            send_unit(2)
        else:
            adapter_terms(lambda j: part[0].at[j, 0], act_window[GROUP_ROWS:], summed)
            pass_act.wait_recv()
            act_window[:STRETCH] = jnp.zeros((STRETCH, RANK), BF16)
            for i, values in enumerate(in_order(act_past[0], act_past[1], past_places)):
                if i:
                    act_window[i * STRETCH:(i + 1) * STRETCH] = values
            adapter_terms(lambda j: part[0].at[j, 1], act_window[...], first_terms)
            if relays:
                pl.semaphore_wait(entered_sem, len(relays))
            send_unit(0)
        terms = dot(grad_scores, sorted_qg[0, :, lanes], (1, 0)) * SCALE
        back_send[KEY, :, lanes] = terms[STRETCH:GROUP_ROWS].astype(BF16)
        own_kv[KEY, :, lanes] = terms[GROUP_ROWS:]
        backs[KEY, head] = back(KEY, head)
        backs[KEY, head].start()

    def input_terms(i, values):
        return dot(values, weight_pad[i, core], (1, 1))

    def hand_out(i, slots):
        outs[i, core, :STRETCH] = slots[0]
        outs[i, core, STRETCH:] = slots[1]
        sib_send[i, :STRETCH] = slots[2]
        sib_send[i, STRETCH:] = slots[3]
        copy = remote(sib_send.at[i], outs.at[i, core], S_OUT + i, other)
        copy.start()
        return copy

    def add_back(kind):
        mine = own_kv[kind]
        return jnp.concatenate(
            [mine[:STRETCH], mine[STRETCH:] + back_recv[kind].astype(F32)], axis=0
        ).astype(BF16)

    def go_across(unit):
        stage(unit, 0).wait_recv()
        total = part[unit][position(unit, 0)].astype(F32)
        for step in range(1, side):
            total = total + scattered[unit][step].astype(F32)
        crossed[unit][position(unit, 1)] = total.astype(BF16)
        for step in steps:
            cross(unit, step).start()

    def go_around(unit):
        stage(unit, 1).wait_recv()
        total = crossed[unit][0].astype(F32)
        for step in range(1, side):
            total = total + crossed[unit][step].astype(F32)
        gathered[unit][core, position(unit, 0)] = total.astype(BF16)
        for step in steps:
            gather(unit, step).start()
        if unit == 2:
            for step in steps + [0]:
                gather_other(unit, step).start()

    input_part = input_terms(0, grads[0])
    out_query = hand_out(0, to_slots(grads[0]))
    go_across(0)

    for head in range(2):
        backs[VALUE, head].wait_recv()
    grads[1] = add_back(VALUE)
    input_slots = to_slots(input_part + input_terms(1, grads[1]))
    gi_send[:STRETCH] = input_slots[2]
    gi_send[STRETCH:] = input_slots[3]
    sib_input = remote(gi_send, gi_sib, S_INPUT, other)
    sib_input.start()
    gi_along[tp, :STRETCH] = input_slots[0]
    gi_along[tp, STRETCH:] = input_slots[1]
    out_value = hand_out(2, to_slots(grads[1]))

    go_across(1)
    go_across(2)

    sib_input.wait_recv()
    gi_along[tp] = gi_along[tp] + gi_sib[...]

    for step in range(1, n_tp):
        block = gi_along.at[tp]
        remote(block, block, S_INPUTS, me, lax.rem(tp + step, n_tp)).start()
    block = gi_along.at[pl.ds(1, n_tp - 1)]
    tp_inputs = remote(block, block, S_INPUTS, other)
    for head in range(2):
        backs[KEY, head].wait_recv()
    out_key = hand_out(1, to_slots(add_back(KEY)))

    go_around(0)
    go_around(1)
    tp_inputs.wait_recv()
    total = gi_along[0]
    for x in range(1, n_tp):
        total = total + gi_along[x]
    gi_ref[...] = total.astype(BF16)
    go_around(2)

    for copy in (out_query, out_value, out_key):
        copy.wait_recv()
    out_ref[...] = outs[...]

    for copy in (
        sib_key, sib_act, sib_value, sib_query, sib_grad, *next_first, next_act, tp_acts, pass_act,
        *next_kv.values(), *backs.values(), out_query, out_value, out_key, sib_input,
    ):
        copy.wait_send()
    tp_inputs.wait_send()
    sib_adapter = []
    for unit in range(3):
        stage(unit, 0).wait_send()
        stage(unit, 1).wait_send()
    for unit in range(3):
        stage(unit, 2).wait_recv()
        block = gathered[unit].at[core]
        copy = remote(block, block, S_ADAPTER + unit, other)
        if unit < 2:
            copy.start()
        sib_adapter.append(copy)
        stage(unit, 2).wait_send()
    for unit, ref in enumerate((ga0_ref, ga1_ref, ga2_ref)):
        sib_adapter[unit].wait_recv()
        ref[...] = gathered[unit][...]
        sib_adapter[unit].wait_send()


def finish(
    out_ref, gi_ref, head0, value1, query1, q_hbm, k_hbm, v_hbm, input_hbm, adapter_hbm,
    wide, adapter, store_sem,
):
    stores = [
        pltpu.make_async_copy(source, hbm, store_sem.at[i])
        for i, (source, hbm) in enumerate((
            (wide.at[0], q_hbm), (wide.at[1], k_hbm), (wide.at[2], v_hbm),
            (adapter.at[0], adapter_hbm.at[0]), (adapter.at[1], adapter_hbm.at[1]), (gi_ref, input_hbm),
        ))
    ]
    stores[5].start()
    for i, head1 in ((1, value1), (0, query1)):
        heads = []
        for pair in range(2):
            heads += [head0[pair, :, i], head1[pair]]
        heads = [head.reshape(RANK, PAD)[:, :HEAD].astype(F32) for head in heads]
        adapter[i] = jnp.concatenate(heads, axis=1)
        stores[3 + i].start()
    for i in range(3):
        wide[i] = unpadded([out_ref[i, 0], out_ref[i, 1]])
        stores[i].start()
    for store in stores:
        store.wait()


def body(
    query_base, key_base, value_base, adapter_activation, adapter_up_weight, output_grad,
    stretch_doc, doc_first, slot_stretch,
):
    n_tp = lax.axis_size("tp")
    side = math.isqrt(lax.axis_size("ctx") // 2)
    rows = RANK // side
    stretches = slot_stretch.shape[0]
    anywhere = pl.BlockSpec(memory_space=pltpu.HBM)
    vmem = pl.BlockSpec(memory_space=pltpu.VMEM)

    def block(*shape, dtype=BF16):
        return pltpu.VMEM(shape, dtype)

    partial_results = pl.pallas_call(
        functools.partial(kernel, side, n_tp),
        out_shape=(
            pltpu.VMEM((3, 2, ROWS, PAIR), BF16),
            pltpu.VMEM((ROWS, RANK), BF16),
            pltpu.VMEM((2, side, 2, rows, PAD), BF16),
            pltpu.VMEM((2, side, rows, PAD), BF16),
            pltpu.VMEM((2, side, rows, PAD), BF16),
        ),
        in_specs=[anywhere] * 8,
        out_specs=(vmem,) * 5,
        scratch_shapes=[
            block(4, ROWS, COLUMNS),
            block(ROWS, RANK),
            block(2, RANK, COLUMNS),
            block(2, 2, RANK, PAIR),
            block(4, 2, ROWS, PAIR),
            block(4, ROWS, PAIR),
            block(ROWS, RANK),
            block(2, ROWS, RANK),
            block(WINDOW, RANK),
            block(2, ROWS, PAD),
            block(2, WINDOW, PAIR),
            block(2, GROUP_ROWS, PAIR),
            block(2, WINDOW, GROUP_ROWS, dtype=F32),
            block(2, WINDOW, GROUP_ROWS),
            block(2, SENT, PAIR),
            block(2, SENT, PAIR),
            block(2, GROUP_ROWS, PAIR, dtype=F32),
            block(2, GROUP_ROWS, PAIR),
            block(3, ROWS, PAIR),
            block(3, 2, ROWS, PAIR),
            block(ROWS, RANK, dtype=F32),
            block(ROWS, RANK, dtype=F32),
            block(n_tp, ROWS, RANK, dtype=F32),
            *((block(side, 2, rows, PAD), block(side, rows, PAD), block(side, rows, PAD)) * 3),
            block(2, side, 2, rows, PAD),
            block(2, side, rows, PAD),
            block(2, side, rows, PAD),
            pltpu.SMEM((stretches,), jnp.int32),
            pltpu.SMEM((stretches,), jnp.int32),
            pltpu.SemaphoreType.DMA((8,)),
            pltpu.SemaphoreType.DMA((COPIES,)),
            pltpu.SemaphoreType.DMA((COPIES,)),
            pltpu.SemaphoreType.REGULAR,
        ],
        compiler_params=pltpu.CompilerParams(
            collective_id=0, has_side_effects=True, vmem_limit_bytes=54 * 2**20
        ),
    )(
        slot_stretch, doc_first, query_base, key_base, value_base, adapter_activation,
        adapter_up_weight, output_grad,
    )
    return pl.pallas_call(
        finish,
        out_shape=(
            jax.ShapeDtypeStruct((ROWS, COLUMNS), BF16),
            jax.ShapeDtypeStruct((ROWS, COLUMNS), BF16),
            jax.ShapeDtypeStruct((ROWS, COLUMNS), BF16),
            jax.ShapeDtypeStruct((ROWS, RANK), BF16),
            jax.ShapeDtypeStruct((2, RANK, COLUMNS), F32),
        ),
        in_specs=[vmem] * 5,
        out_specs=(anywhere,) * 5,
        scratch_shapes=[
            block(3, ROWS, COLUMNS),
            block(2, RANK, COLUMNS, dtype=F32),
            pltpu.SemaphoreType.DMA((6,)),
        ],
        compiler_params=pltpu.CompilerParams(vmem_limit_bytes=32 * 2**20),
    )(*partial_results)


def solution(mesh):
    return jax.shard_map(
        body,
        mesh=mesh,
        in_specs=(
            P("ctx", "tp"),
            P("ctx", "tp"),
            P("ctx", "tp"),
            P("ctx", None),
            P(None, None, "tp"),
            P("ctx", "tp"),
            P(),
            P(),
            P(),
        ),
        out_specs=(
            P("ctx", "tp"),
            P("ctx", "tp"),
            P("ctx", "tp"),
            P("ctx", None),
            P(None, None, "tp"),
        ),
        check_vma=False,
    )
```
